32 devices in a mesh: dp: 4 (over y, x), expert: 8 (over z, core).
Axes of the slice: x: 2, y: 2, z: 4, core: 2. Of those that a mesh axis runs over, the one named last changes fastest.
Arguments:
- tokens: bfloat16 [4096, 2048], P(('dp', 'expert')), may hold values from -6 to 6
- target: bfloat16 [4096, 2048], P(('dp', 'expert')), may hold values from -6 to 6
- valid: int32 [4096], P(('dp', 'expert')), may hold values from 0 to 1, as said below
- routes: int32 [4096, 6], P('dp'), may hold values from 0 to 15, all different within a row; in each aligned block of 128 rows (0 to 127, 128 to 255, ...) at most 64 rows name the same one
- lengths: int32 [1, 4], replicated, may hold values from 1 to 2048, 4096 in all within a row
- first_gain_vector: float32 [2048], replicated, may hold values from 0.5 to 1.5
- second_gain_vector: float32 [2048], replicated, may hold values from 0.5 to 1.5
- latent_gain_vector: float32 [512], replicated, may hold values from 0.5 to 1.5
- latent_compress_weight: bfloat16 [2048, 576], replicated, may hold values from -0.125 to 0.125
- query_weight: bfloat16 [2048, 3072], P(None, 'expert'), may hold values from -0.125 to 0.125
- latent_expand_weight: bfloat16 [512, 4096], P(None, 'expert'), may hold values from -0.25 to 0.25
- output_weight: bfloat16 [2048, 2048], P('expert'), may hold values from -1.5 to 1.5
- router_weight: bfloat16 [2048, 16], replicated, may hold values from -0.0625 to 0.0625
- shared_gate_weight: bfloat16 [2048, 2816], P(None, 'expert'), may hold values from -0.125 to 0.125
- shared_up_weight: bfloat16 [2048, 2816], P(None, 'expert'), may hold values from -0.125 to 0.125
- shared_down_weight: bfloat16 [2816, 2048], P('expert'), may hold values from -0.109375 to 0.109375
- expert_gate_weight: bfloat16 [16, 2048, 1408], P('expert', 'dp'), may hold values from -0.125 to 0.125
- expert_up_weight: bfloat16 [16, 2048, 1408], P('expert', 'dp'), may hold values from -0.125 to 0.125
- expert_down_weight: bfloat16 [16, 1408, 2048], P('expert', None, 'dp'), may hold values from -0.3125 to 0.3125
Outputs:
- output: bfloat16 [4096, 2048], P(('dp', 'expert'))
- loss: float32 [], replicated
- grad_tokens: float32 [4096, 2048], P(('dp', 'expert'))
- grad_norm1: float32 [2048], replicated
- grad_norm2: float32 [2048], replicated
- grad_latent_gain: float32 [512], replicated
- grad_kva: float32 [2048, 576], replicated
- query_weight_gradient: float32 [2048, 3072], P('dp', 'expert')
- latent_expand_gradient: float32 [512, 4096], P('dp', 'expert')
- output_weight_gradient: float32 [2048, 2048], P('expert', 'dp')
- grad_router: float32 [2048, 16], replicated
- shared_gate_gradient: float32 [2048, 2816], P('dp', 'expert')
- shared_up_gradient: float32 [2048, 2816], P('dp', 'expert')
- shared_down_gradient: float32 [2816, 2048], P('expert', 'dp')
- expert_gate_gradient: float32 [16, 2048, 1408], P('expert', 'dp')
- expert_up_gradient: float32 [16, 2048, 1408], P('expert', 'dp')
- expert_down_gradient: float32 [16, 1408, 2048], P('expert', None, 'dp')
The draws below stay inside these ranges and needn't reach their ends.
Inputs may be any that keep to these rules, and one draw needn't show every extreme that they name: `routes`: each row names 6 different experts. In each aligned block of 128 rows (the tokens of one device) no expert is named by more than 64 rows, a bound that some block reaches. Each row holds the lengths of the documents of one sequence in order; they sum to 4096, and the longest is exactly half of 4096. `valid`: the first token always counts.
All inputs are finite; a program needn't handle non-finite values.
Results may differ from the reference program's by a relative error of at most 0.025.
Values may be sent and summed in bfloat16 or wider, within the bound.
No kernel may reach another device: no remote copies, remote signals or barrier semaphores. Data moves between devices by JAX's collectives and lax.ppermute only.
A program may use at most 320 MiB of HBM per device.

```python
import math
import jax
import jax.numpy as jnp
import numpy as np
from jax import lax

MODEL_WIDTH = 2048
HEADS = 16
NOPE = 128
ROPE = 64
VDIM = 128
LATENT = 512
EXPERT_HIDDEN = 1408
SHARED = 2816
TOPK = 6
TOK_DEV = 128
SEQ = 4096
WINDOW = 1024
DOCS = 4
ROUTED_EXPERTS = 16
TOKENS = 4096
SEQS = 1
CAP = 64


def draw_valid(key, part):
    key = jax.random.fold_in(key, 7)
    index = jnp.arange(TOKENS, dtype=jnp.int32)
    level = 30 + 65 * index // TOKENS
    drawn = jax.random.randint(key, (TOKENS,), 0, 100, dtype=jnp.int32)
    return jnp.where((drawn < level) | (index == 0), 1, 0).astype(jnp.int32)


def shard_levels(key, extent, split, low, top_value):
    loudness = 1.0
    for position, parts in split:
        steps = jax.random.uniform(jax.random.fold_in(jax.random.fold_in(key, 6), position), (parts,), jnp.float32, low / len(split), top_value / len(split))
        loudness = loudness * jnp.repeat(jnp.exp(steps), extent[position] // parts).reshape((-1,) + (1,) * (len(extent) - 1 - position))
    return loudness


def length_profile(number_of, total, limit, lean):
    loads = [(1 << 20) // math.isqrt(standing ** lean) + 1 for standing in range(2, number_of + 1)]
    surplus, counts = total - limit - (number_of - 1), [1] * (number_of - 1)
    while surplus > 0:
        movable = [i for i in range(number_of - 1) if counts[i] < limit]
        pool, budget = sum([loads[i] for i in movable]), surplus
        for i in movable:
            more = min(limit - counts[i], max(1, budget * loads[i] // pool), surplus)
            counts[i] = counts[i] + more
            surplus = surplus - more
    return np.array([limit] + counts)


def ragged_sizes(stream_key, amount, total, bound, slope):
    if amount == 2:
        one = jax.random.randint(stream_key, (), max(1, total - bound), min(bound, total - 1) + 1)
        return jnp.stack([one, total - one])
    sizes = jnp.asarray(length_profile(amount, total, bound, slope), jnp.int32)
    pairs = (amount - 1) // 2
    giver, sink = sizes[1:1 + 2 * pairs:2], sizes[2:2 + 2 * pairs:2]
    margin = jnp.minimum(giver - 1, bound - sink)
    moved = jax.random.randint(jax.random.fold_in(stream_key, 1), (pairs,), 0, 1 << 20) % (margin + 1)
    sizes = sizes.at[1:1 + 2 * pairs:2].set(giver - moved).at[2:2 + 2 * pairs:2].set(sink + moved)
    return sizes[jax.random.permutation(jax.random.fold_in(stream_key, 2), amount)]


def deal_out(own_key, own, number, rows, number_of, top, limit, lean):
    ranking = jax.random.permutation(own_key, number_of)
    crowded, common = load_shares(number_of, rows * top, limit, lean, True), load_shares(number_of, rows * top, limit, lean, False)
    places = jnp.arange(number_of)

    def named(sizes, offset_by):
        used = int((sizes > 0).sum())
        fixed = max(1, used // 4)
        passed = fixed + (places - fixed + offset_by * (used - fixed)) % max(1, number_of - fixed)
        return jnp.zeros((number_of,), jnp.int32).at[ranking[jnp.where(places < fixed, places, passed)]].set(jnp.asarray(sizes, jnp.int32))

    sizes = jnp.where(number % 4 == 0, named(crowded, number // 4), named(common, number - number // 4 - 1))
    mixed = jax.random.permutation(jax.random.fold_in(own, 3), number_of)
    donor, taker = mixed[0:number_of // 2 * 2:2], mixed[1:number_of // 2 * 2:2]
    slack = jnp.minimum(sizes[donor] - 1, limit - sizes[taker]) // 2
    slack = jnp.where((donor == ranking[0]) | (taker == ranking[0]) | (sizes[taker] == 0), 0, jnp.maximum(slack, 0))
    passed = jax.random.randint(jax.random.fold_in(own, 4), (number_of // 2,), 0, 1 << 20) % (slack + 1)
    sizes = sizes.at[donor].add(-passed).at[taker].add(passed)
    items = jnp.searchsorted(jnp.cumsum(sizes), jnp.arange(rows * top), side="right").astype(jnp.int32)
    listing = items.reshape(top, rows).T
    listing = listing[jax.random.permutation(jax.random.fold_in(own, 1), rows)]
    offset_by = jax.random.randint(jax.random.fold_in(own, 2), (rows, 1), 0, top)
    return jnp.take_along_axis(listing, (jnp.arange(top)[None, :] + offset_by) % top, axis=1)


def load_shares(amount, total, limit, slope, full):
    portions = [(1 << 20) // math.isqrt(rank ** slope) + 1 for rank in range(1, amount + 1)]
    largest = limit if full else min(limit, max(-(-total // amount), total * portions[0] // sum(portions)))
    least = 1 if total - largest >= amount - 1 else 0
    holding, spare = [largest] + [least] * (amount - 1), total - largest - least * (amount - 1)
    while spare > 0:
        free = [i for i in range(1, amount) if holding[i] < largest] or [i for i in range(1, amount) if holding[i] < limit]
        whole, remaining = sum([portions[i] for i in free]), spare
        for i in free:
            addition = min(limit - holding[i], max(1, remaining * portions[i] // whole), spare)
            holding[i] = holding[i] + addition
            spare = spare - addition
    return np.array(holding)


def centred(stream_key, dims, width, most, split=(), kind=jnp.bfloat16):
    values = jax.random.normal(stream_key, dims, jnp.float32) * width
    if len(split) > 0:
        values = shard_levels(stream_key, dims, split, -0.22, 0.18) * values
    return jnp.clip(values, min=-most, max=most).astype(kind)


def setup_inputs(seed: int = 0) -> dict:
    splits = jax.random.split(jax.random.key(seed), 20)
    tokens = centred(splits[0], (TOKENS, MODEL_WIDTH), 1.0, 6.0, ((0, 32),))
    target = centred(splits[1], (TOKENS, MODEL_WIDTH), 1.0, 6.0, ((0, 32),))
    valid = draw_valid(jax.random.fold_in(splits[19], 71), 0)
    routes_keys = jax.random.split(jax.random.fold_in(splits[3], 1), TOKENS // TOK_DEV)
    routes_turns = jax.random.permutation(jax.random.fold_in(splits[3], 3), TOKENS // TOK_DEV)
    routes = jax.vmap(lambda own, number: deal_out(jax.random.fold_in(splits[3], 2), own, number, TOK_DEV, ROUTED_EXPERTS, TOPK, CAP, 1))(routes_keys, routes_turns).reshape((TOKENS, TOPK))
    lengths = jax.vmap(lambda own: ragged_sizes(own, DOCS, SEQ, SEQ // 2, 2))(jax.random.split(splits[4], SEQS)).reshape((SEQS, DOCS)).astype(jnp.int32)
    first_gain_vector = jnp.clip(1.0 + 0.1 * jax.random.normal(splits[5], (MODEL_WIDTH,), jnp.float32), 0.5, 1.5)
    second_gain_vector = jnp.clip(1.0 + 0.1 * jax.random.normal(splits[6], (MODEL_WIDTH,), jnp.float32), 0.5, 1.5)
    latent_gain_vector = jnp.clip(1.0 + 0.1 * jax.random.normal(splits[7], (LATENT,), jnp.float32), 0.5, 1.5)
    latent_compress_weight = centred(splits[8], (MODEL_WIDTH, LATENT + ROPE), MODEL_WIDTH ** -0.5, 0.125)
    query_weight = centred(splits[9], (MODEL_WIDTH, HEADS * (NOPE + ROPE)), MODEL_WIDTH ** -0.5, 0.125, ((1, 8),))
    latent_expand_weight = centred(splits[10], (LATENT, HEADS * (NOPE + VDIM)), LATENT ** -0.5, 0.25, ((1, 8),))
    output_weight = centred(splits[11], (HEADS * VDIM, MODEL_WIDTH), (max(4, MODEL_WIDTH // 128)) ** -0.5, 1.5, ((0, 8),))
    router_weight = centred(splits[12], (MODEL_WIDTH, ROUTED_EXPERTS), (4 * MODEL_WIDTH) ** -0.5, 0.0625)
    shared_gate_weight = centred(splits[13], (MODEL_WIDTH, SHARED), MODEL_WIDTH ** -0.5, 0.125, ((1, 8),))
    shared_up_weight = centred(splits[14], (MODEL_WIDTH, SHARED), MODEL_WIDTH ** -0.5, 0.125, ((1, 8),))
    shared_down_weight = centred(splits[15], (SHARED, MODEL_WIDTH), SHARED ** -0.5, 0.109375, ((0, 8),))
    expert_gate_weight = centred(splits[16], (ROUTED_EXPERTS, MODEL_WIDTH, EXPERT_HIDDEN), MODEL_WIDTH ** -0.5, 0.125, ((0, 8), (1, 4)))
    expert_up_weight = centred(splits[17], (ROUTED_EXPERTS, MODEL_WIDTH, EXPERT_HIDDEN), MODEL_WIDTH ** -0.5, 0.125, ((0, 8), (1, 4)))
    expert_down_weight = centred(splits[18], (ROUTED_EXPERTS, EXPERT_HIDDEN, MODEL_WIDTH), (EXPERT_HIDDEN // 4) ** -0.5, 0.3125, ((0, 8), (2, 4)))
    return {"tokens": tokens, "target": target, "valid": valid, "routes": routes, "lengths": lengths, "first_gain_vector": first_gain_vector, "second_gain_vector": second_gain_vector, "latent_gain_vector": latent_gain_vector, "latent_compress_weight": latent_compress_weight, "query_weight": query_weight, "latent_expand_weight": latent_expand_weight, "output_weight": output_weight, "router_weight": router_weight, "shared_gate_weight": shared_gate_weight, "shared_up_weight": shared_up_weight, "shared_down_weight": shared_down_weight, "expert_gate_weight": expert_gate_weight, "expert_up_weight": expert_up_weight, "expert_down_weight": expert_down_weight}


highest = lax.Precision.HIGHEST
epsilon = 1e-06

@jax.custom_vjp
def low(v):
    return lax.optimization_barrier(v.astype(jnp.bfloat16)).astype(jnp.float32)

@jax.custom_vjp
def low_back(v):
    return v

def low_keep(v):
    return (low(v), None)

def low_pass(kept, grad):
    return (grad,)

def back_keep(v):
    return (v, None)

def back_low(kept, grad):
    return (low(grad),)
low.defvjp(low_keep, low_pass)
low_back.defvjp(back_keep, back_low)

def matmul(left, right):
    return jnp.dot(left, right, precision=highest)

def rms(values, gain):
    return values * lax.rsqrt(lax.optimization_barrier(jnp.mean(values * values, axis=-1, keepdims=True)) + epsilon) * gain

def rotate(values, cosine, sine):
    half = values.shape[-1] // 2
    first, second = (values[..., :half], values[..., half:])
    return jnp.concatenate([first * cosine - second * sine, first * sine + second * cosine], axis=-1)

def reference(tokens, target, valid, routes, lengths, first_gain_vector, second_gain_vector, latent_gain_vector, latent_compress_weight, query_weight, latent_expand_weight, output_weight, router_weight, shared_gate_weight, shared_up_weight, shared_down_weight, expert_gate_weight, expert_up_weight, expert_down_weight):
    total_count = tokens.shape[0]
    index = jnp.arange(total_count, dtype=jnp.int32)
    seq_id = (index // SEQ).astype(jnp.int32)
    place = (index - seq_id * SEQ).astype(jnp.int32)
    bounds = jnp.cumsum(lengths, axis=1).astype(jnp.int32)
    labels = jnp.arange(lengths.shape[0], dtype=jnp.int32)
    hits = (seq_id[:, None, None] == labels[None, :, None]) & (bounds[None, :, :] <= place[:, None, None])
    docs = lax.optimization_barrier(jnp.sum(hits.astype(jnp.int32), axis=(1, 2))).astype(jnp.int32)
    pad_seq = jnp.concatenate([jnp.full((WINDOW,), -1, jnp.int32), seq_id])
    pad_docs = jnp.concatenate([jnp.full((WINDOW,), -1, jnp.int32), docs])
    pad_index = jnp.concatenate([jnp.arange(-WINDOW, 0, dtype=jnp.int32), index])
    half = ROPE // 2
    freq = jnp.exp(-jnp.log(10000.0) * jnp.arange(half, dtype=jnp.float32) / half)
    angle = place.astype(jnp.float32)[:, None] * freq[None, :]
    cosine, sine = (jnp.cos(angle), jnp.sin(angle))
    block = min(512, total_count)
    starts = jnp.arange(total_count // block, dtype=jnp.int32) * block
    score_scale = (NOPE + ROPE) ** (-0.5)
    owners = total_count // TOK_DEV
    flat_routes = routes.reshape(owners, TOK_DEV * TOPK)
    hot = (flat_routes[:, :, None] == jnp.arange(ROUTED_EXPERTS, dtype=jnp.int32)[None, None, :]).astype(jnp.int32)
    ranks = lax.optimization_barrier(jnp.sum((jnp.cumsum(hot, axis=1) - 1) * hot, axis=2)).astype(jnp.int32)
    owner_ids = jnp.broadcast_to(jnp.arange(owners, dtype=jnp.int32)[:, None], flat_routes.shape)
    entries = jnp.arange(total_count * TOPK, dtype=jnp.int32).reshape(owners, TOK_DEV * TOPK)
    lookup_table = jnp.full((ROUTED_EXPERTS, owners, CAP), total_count * TOPK, jnp.int32)
    lookup_table = lookup_table.at[flat_routes, owner_ids, ranks].set(entries).reshape(ROUTED_EXPERTS, owners * CAP)
    counted = valid.astype(jnp.float32)
    count = jnp.sum(counted)
    target_f = target.astype(jnp.float32)

    def forward_pass(tokens_float, first_norm_gain, second_norm_gain, latent_norm_gain, latent_compress, query_matrix, latent_expand, output_matrix, router_matrix, shared_gate_matrix, shared_up_matrix, shared_down_matrix, expert_gate_matrix, expert_up_matrix, expert_down):
        normed = low(rms(tokens_float, first_norm_gain))
        projected = low_back(matmul(normed, latent_compress))
        latent = low(jnp.concatenate([rms(projected[:, :LATENT], latent_norm_gain), rotate(projected[:, LATENT:], cosine, sine)], axis=1))
        query_proj = low_back(matmul(normed, query_matrix)).reshape(total_count, HEADS, NOPE + ROPE)
        queries = low(jnp.concatenate([query_proj[..., :NOPE], rotate(query_proj[..., NOPE:], cosine[:, None, :], sine[:, None, :])], axis=-1))
        key_value = low_back(matmul(latent[:, :LATENT], latent_expand)).reshape(total_count, HEADS, NOPE + VDIM)
        keys = jnp.concatenate([low(key_value[..., :NOPE]), jnp.broadcast_to(latent[:, None, LATENT:], (total_count, HEADS, ROPE))], axis=-1)
        values = low(key_value[..., NOPE:])
        pad_keys = jnp.concatenate([jnp.zeros((WINDOW, HEADS, NOPE + ROPE), jnp.float32), keys], axis=0)
        pad_values = jnp.concatenate([jnp.zeros((WINDOW, HEADS, VDIM), jnp.float32), values], axis=0)

        def attend(start):
            query_block = lax.dynamic_slice_in_dim(queries, start, block, 0)
            key_block = lax.dynamic_slice_in_dim(pad_keys, start, WINDOW + block, 0)
            value_block = lax.dynamic_slice_in_dim(pad_values, start, WINDOW + block, 0)
            query_index = start + jnp.arange(block, dtype=jnp.int32)
            query_seq = lax.dynamic_slice_in_dim(seq_id, start, block, 0)
            query_doc = lax.dynamic_slice_in_dim(docs, start, block, 0)
            key_index = lax.dynamic_slice_in_dim(pad_index, start, WINDOW + block, 0)
            key_seq = lax.dynamic_slice_in_dim(pad_seq, start, WINDOW + block, 0)
            key_doc = lax.dynamic_slice_in_dim(pad_docs, start, WINDOW + block, 0)
            allowed = (key_index[None, :] >= 0) & (query_seq[:, None] == key_seq[None, :]) & (query_doc[:, None] == key_doc[None, :])
            allowed = allowed & (query_index[:, None] >= key_index[None, :]) & (query_index[:, None] - key_index[None, :] < WINDOW)
            scores = low_back(jnp.einsum('qhd,khd->hqk', query_block, key_block, precision=highest) * score_scale)
            scores = jnp.where(allowed[None], scores, -1e+30)
            top = lax.optimization_barrier(jnp.max(scores, axis=-1, keepdims=True))
            raised = jnp.exp(scores - top)
            probs = raised / lax.optimization_barrier(jnp.sum(raised, axis=-1, keepdims=True))
            return jnp.einsum('hqk,khd->qhd', low(probs), value_block, precision=highest)
        mixed = lax.map(jax.checkpoint(attend), starts).reshape(total_count, HEADS * VDIM)
        heads_out = low(low_back(mixed))
        attention = low_back(matmul(heads_out, output_matrix))
        hidden = tokens_float + attention
        branch_in = low(rms(hidden, second_norm_gain))
        logits = matmul(branch_in, router_matrix)
        chosen = jnp.take_along_axis(logits, routes, axis=1)
        weights = jnp.exp(chosen - lax.optimization_barrier(jnp.max(chosen, axis=1, keepdims=True)))
        gates = weights / lax.optimization_barrier(jnp.sum(weights, axis=1, keepdims=True))
        shared_gate = low_back(matmul(branch_in, shared_gate_matrix))
        shared_up = low_back(matmul(branch_in, shared_up_matrix))
        shared_hidden = low(jax.nn.silu(shared_gate) * shared_up)
        shared = low_back(matmul(shared_hidden, shared_down_matrix))
        padded_in = jnp.concatenate([branch_in, jnp.zeros((1, MODEL_WIDTH), jnp.float32)], axis=0)
        gate_pad = jnp.concatenate([gates.reshape(-1), jnp.zeros((1,), jnp.float32)])

        def expert_update(total, items):
            gate_w, up_w, down_w, slots = items
            slot_rows = low_back(padded_in[slots // TOPK])
            expert_gate = low_back(matmul(slot_rows, gate_w))
            expert_up = low_back(matmul(slot_rows, up_w))
            expert_hidden = low(jax.nn.silu(expert_gate) * expert_up)
            expert_out = low(low_back(matmul(expert_hidden, down_w)))
            total = total.at[slots // TOPK].add(gate_pad[slots][:, None] * expert_out)
            return (total, None)
        routed_result, ignored_value = lax.scan(jax.checkpoint(expert_update), jnp.zeros((total_count + 1, MODEL_WIDTH), jnp.float32), (expert_gate_matrix, expert_up_matrix, expert_down, lookup_table))
        result = hidden + shared + routed_result[:total_count]
        difference = result - target_f
        squares = jnp.sum(counted[:, None] * difference * difference)
        objective = total_count * 0.5 * squares / count
        return (objective, (result, squares / (count * MODEL_WIDTH)))
    parameters = (tokens.astype(jnp.float32), first_gain_vector, second_gain_vector, latent_gain_vector, latent_compress_weight.astype(jnp.float32), query_weight.astype(jnp.float32), latent_expand_weight.astype(jnp.float32), output_weight.astype(jnp.float32), router_weight.astype(jnp.float32), shared_gate_weight.astype(jnp.float32), shared_up_weight.astype(jnp.float32), shared_down_weight.astype(jnp.float32), expert_gate_weight.astype(jnp.float32), expert_up_weight.astype(jnp.float32), expert_down_weight.astype(jnp.float32))
    objective, backward, aux = jax.vjp(forward_pass, *parameters, has_aux=True)
    result, loss = aux
    grads = backward(jnp.ones((), jnp.float32))
    return (result.astype(jnp.bfloat16), loss, grads[0], grads[1], grads[2], grads[3], grads[4], grads[5], grads[6], grads[7], grads[8], grads[9], grads[10], grads[11], grads[12], grads[13], grads[14])
```

```python
import functools

import jax
import jax.numpy as jnp
from jax import lax
from jax.experimental import pallas as pl
from jax.experimental.pallas import tpu as pltpu
from jax.sharding import PartitionSpec as P

NOPE = 128
ROPE = 64
VDIM = 128
LATENT = 512
SEQ = 4096
WINDOW = 1024
QUERY_BLOCK = 256

epsilon = 1e-06
masked_value = -1e30
score_scale = (NOPE + ROPE) ** (-0.5)
bf16 = jnp.bfloat16
f32 = jnp.float32


def dot_plain(left, right):
    return lax.dot_general(left, right, (((1,), (0,)), ((), ())), preferred_element_type=f32)


def dot_right_t(left, right):
    return lax.dot_general(left, right, (((1,), (1,)), ((), ())), preferred_element_type=f32)


def dot_left_t(left, right):
    return lax.dot_general(left, right, (((0,), (0,)), ((), ())), preferred_element_type=f32)


def normalize(values):
    factor = lax.rsqrt(jnp.mean(values * values, axis=-1, keepdims=True) + epsilon)
    return (values * factor, factor)


def norm_back(grad_out, unit, factor, gain):
    grad_unit = grad_out * gain
    return factor * (grad_unit - unit * jnp.mean(grad_unit * unit, axis=-1, keepdims=True))


def angles(place, half):
    freq = jnp.exp(-jnp.log(10000.0) * jnp.arange(half, dtype=f32) / half)
    angle = place.astype(f32)[:, None] * freq[None, :]
    return (jnp.cos(angle), jnp.sin(angle))


def rotate(values, cosine, sine):
    half = values.shape[-1] // 2
    first, second = (values[..., :half], values[..., half:])
    return jnp.concatenate(
        [first * cosine - second * sine, first * sine + second * cosine], axis=-1
    )


def unrotate(grads, cosine, sine):
    half = grads.shape[-1] // 2
    first, second = (grads[..., :half], grads[..., half:])
    return jnp.concatenate(
        [first * cosine + second * sine, second * cosine - first * sine], axis=-1
    )


def silu_parts(values):
    sigma = jax.nn.sigmoid(values)
    return (values * sigma, sigma * (1.0 + values * (1.0 - sigma)))


def head_lanes(block, head):
    lane = lax.broadcasted_iota(jnp.int32, (block, 2 * ROPE), 1)
    return (lane // (ROPE // 2)) % 2 == head


def allowed_keys(low, block, span):
    row = lax.broadcasted_iota(jnp.int32, (block, span), 0)
    col = lax.broadcasted_iota(jnp.int32, (block, span), 1)
    return (col <= row + WINDOW) & (col >= low)


def read_chunks(refs, first, last):
    return jnp.concatenate([ref[:, first:last] for ref in refs], axis=0)


def head_parts(query, lanes, kv, rope, head):
    turned = jnp.where(lanes, query[:, 2 * NOPE :], 0)
    query_head = jnp.concatenate([query[:, head * NOPE : (head + 1) * NOPE], turned], axis=1)
    base = head * (NOPE + VDIM)
    key_head = jnp.concatenate([read_chunks(kv, base, base + NOPE), rope], axis=1)
    return (query_head, key_head, read_chunks(kv, base + NOPE, base + NOPE + VDIM))


def attend_kernel(chunks, normed, cosine, sine, low, query_w, out_w, *refs):
    kv, key_rope = refs[:chunks], refs[chunks : 2 * chunks]
    query_out, mixed_out, log_out, part_out = refs[2 * chunks :]
    block = normed.shape[0]
    proj = dot_plain(normed[...], query_w[...])
    turned = proj[:, 2 * NOPE :]
    turned = turned * cosine[...] + pltpu.roll(turned, ROPE, 1) * sine[...]
    query = jnp.concatenate([proj[:, : 2 * NOPE], turned], axis=1).astype(bf16)
    query_out[...] = query
    mask = allowed_keys(low[...], block, WINDOW + block)
    rope = read_chunks(key_rope, 0, 2 * ROPE)
    mixed, logs = [], []
    for head in range(2):
        query_head, key_head, value_head = head_parts(query, head_lanes(block, head), kv, rope, head)
        scores = jnp.where(mask, dot_right_t(query_head, key_head) * score_scale, masked_value)
        top = jnp.max(scores, axis=1, keepdims=True)
        raised = jnp.exp(scores - top)
        total = jnp.sum(raised, axis=1, keepdims=True)
        probs = (raised * (1.0 / total)).astype(bf16)
        mixed.append(dot_plain(probs, value_head))
        logs.append(top + jnp.log(total))
    lane = lax.broadcasted_iota(jnp.int32, (block, 128), 1)
    log_out[...] = jnp.where(lane == 0, logs[0], logs[1])
    mixed = jnp.concatenate(mixed, axis=1).astype(bf16)
    mixed_out[...] = mixed
    part_out[...] = dot_plain(mixed, out_w[...]).astype(bf16)


def by_rows(block, cols, offset=0):
    return pl.BlockSpec((block, cols), lambda i: (i + offset, 0))


def whole(shape):
    return pl.BlockSpec(shape, lambda i: (0, 0))


def attend(normed, cosine, sine, low, query_w, kv, key_rope, out_w):
    rows, width = normed.shape
    block = QUERY_BLOCK
    chunks = 1 + WINDOW // block
    query_cols = query_w.shape[1]
    rows_of = functools.partial(by_rows, block)
    return pl.pallas_call(
        functools.partial(attend_kernel, chunks),
        grid=(rows // block,),
        in_specs=[
            rows_of(width),
            rows_of(2 * ROPE),
            rows_of(2 * ROPE),
            rows_of(1),
            whole(query_w.shape),
            whole(out_w.shape),
        ]
        + [rows_of(kv.shape[1], chunk) for chunk in range(chunks)]
        + [rows_of(key_rope.shape[1], chunk) for chunk in range(chunks)],
        out_specs=[rows_of(query_cols), rows_of(2 * VDIM), rows_of(128), rows_of(width)],
        out_shape=[
            jax.ShapeDtypeStruct((rows, query_cols), bf16),
            jax.ShapeDtypeStruct((rows, 2 * VDIM), bf16),
            jax.ShapeDtypeStruct((rows, 128), f32),
            jax.ShapeDtypeStruct((rows, width), bf16),
        ],
        compiler_params=pltpu.CompilerParams(vmem_limit_bytes=50 * 1024 * 1024),
        cost_estimate=pl.CostEstimate(
            flops=2 * rows * (width * (query_cols + 2 * VDIM) + 2 * (WINDOW + block) * 384),
            bytes_accessed=20 * 1024 * 1024,
            transcendentals=2 * rows * (WINDOW + block),
        ),
        name="attend",
    )(normed, cosine, sine, low, query_w, out_w, *([kv] * chunks), *([key_rope] * chunks))


def attend_back_kernel(
    chunks, grad, query_in, logs, cosine, sine, low, query_w, out_w, *refs
):
    kv, key_rope = refs[:chunks], refs[chunks : 2 * chunks]
    query_grad_out, part_out = refs[2 * chunks : 2 * chunks + 2]
    kv_past, rope_past, kv_own, rope_own, kv_sum, rope_sum = refs[2 * chunks + 2 :]
    block = grad.shape[0]

    @pl.when(pl.program_id(0) == 0)
    def clear():
        kv_sum[...] = jnp.zeros_like(kv_sum)
        rope_sum[...] = jnp.zeros_like(rope_sum)

    def add(total, past, cols, piece):
        for chunk in range(chunks):
            part = piece[chunk * block : (chunk + 1) * block]
            if chunk < chunks - 1:
                part = part + total[chunk * block : (chunk + 1) * block, cols]
            if chunk == 0:
                past[:, cols] = part.astype(past.dtype)
            else:
                total[(chunk - 1) * block : chunk * block, cols] = part

    mixed_grad = dot_right_t(grad[...], out_w[...]).astype(bf16)
    mask = allowed_keys(low[...], block, WINDOW + block)
    rope = read_chunks(key_rope, 0, 2 * ROPE)
    query = query_in[...]
    plain, turned, rope_piece = [], 0.0, 0.0
    for head in range(2):
        lanes = head_lanes(block, head)
        query_head, key_head, value_head = head_parts(query, lanes, kv, rope, head)
        base = head * (NOPE + VDIM)
        grad_head = mixed_grad[:, head * VDIM : (head + 1) * VDIM]
        scores = jnp.where(mask, dot_right_t(query_head, key_head) * score_scale, masked_value)
        probs = jnp.exp(scores - logs[:, head : head + 1])
        prob_grad = dot_right_t(grad_head, value_head)
        shift = jnp.sum(probs * prob_grad, axis=1, keepdims=True)
        score_grad = (probs * (prob_grad - shift)).astype(bf16)
        key_piece = dot_left_t(score_grad, query_head) * score_scale
        add(kv_sum, kv_past, slice(base, base + NOPE), key_piece[:, :NOPE])
        value_piece = dot_left_t(probs.astype(bf16), grad_head)
        add(kv_sum, kv_past, slice(base + NOPE, base + NOPE + VDIM), value_piece)
        rope_piece = rope_piece + key_piece[:, NOPE:]
        query_piece = dot_plain(score_grad, key_head) * score_scale
        plain.append(query_piece[:, :NOPE])
        turned = turned + jnp.where(lanes, query_piece[:, NOPE:], 0.0)
    add(rope_sum, rope_past, slice(0, 2 * ROPE), rope_piece)
    turned = turned * cosine[...] - pltpu.roll(turned, ROPE, 1) * sine[...]
    query_grad = jnp.concatenate(plain + [turned], axis=1).astype(bf16)
    query_grad_out[...] = query_grad
    part_out[...] = dot_right_t(query_grad, query_w[...]).astype(bf16)

    @pl.when(pl.program_id(0) == pl.num_programs(0) - 1)
    def finish():
        kv_own[...] = kv_sum[...].astype(bf16)
        rope_own[...] = rope_sum[...]


def attend_back(grad, query, logs, cosine, sine, low, query_w, kv, key_rope, out_w):
    rows, width = grad.shape
    block = QUERY_BLOCK
    chunks = 1 + WINDOW // block
    query_cols = query_w.shape[1]
    rows_of = functools.partial(by_rows, block)
    kv_cols, rope_cols = kv.shape[1], key_rope.shape[1]
    return pl.pallas_call(
        functools.partial(attend_back_kernel, chunks),
        grid=(rows // block,),
        in_specs=[
            rows_of(width),
            rows_of(query_cols),
            rows_of(128),
            rows_of(2 * ROPE),
            rows_of(2 * ROPE),
            rows_of(1),
            whole(query_w.shape),
            whole(out_w.shape),
        ]
        + [rows_of(kv_cols, chunk) for chunk in range(chunks)]
        + [rows_of(rope_cols, chunk) for chunk in range(chunks)],
        out_specs=[
            rows_of(query_cols),
            rows_of(width),
            rows_of(kv_cols),
            rows_of(rope_cols),
            whole((WINDOW, kv_cols)),
            whole((WINDOW, rope_cols)),
        ],
        out_shape=[
            jax.ShapeDtypeStruct((rows, query_cols), bf16),
            jax.ShapeDtypeStruct((rows, width), bf16),
            jax.ShapeDtypeStruct((rows, kv_cols), bf16),
            jax.ShapeDtypeStruct((rows, rope_cols), f32),
            jax.ShapeDtypeStruct((WINDOW, kv_cols), bf16),
            jax.ShapeDtypeStruct((WINDOW, rope_cols), f32),
        ],
        scratch_shapes=[pltpu.VMEM((WINDOW, kv_cols), f32), pltpu.VMEM((WINDOW, rope_cols), f32)],
        compiler_params=pltpu.CompilerParams(vmem_limit_bytes=50 * 1024 * 1024),
        cost_estimate=pl.CostEstimate(
            flops=2 * rows * (width * (query_cols + 2 * VDIM) + 2 * (WINDOW + block) * 1024),
            bytes_accessed=30 * 1024 * 1024,
            transcendentals=2 * rows * (WINDOW + block),
        ),
        name="attend_back",
    )(
        grad, query, logs, cosine, sine, low, query_w, out_w, *([kv] * chunks), *([key_rope] * chunks)
    )


def split_query_columns(weight):
    head = NOPE + ROPE
    half = ROPE // 2
    pieces = [weight[:, :NOPE], weight[:, head : head + NOPE]]
    for part in range(2):
        for index in range(2):
            first = index * head + NOPE + part * half
            pieces.append(weight[:, first : first + half])
    return jnp.concatenate(pieces, axis=1)


def join_query_columns(grad):
    half = ROPE // 2
    base = 2 * NOPE
    pieces = []
    for index in range(2):
        pieces.append(grad[:, index * NOPE : (index + 1) * NOPE])
        for part in range(2):
            first = base + part * ROPE + index * half
            pieces.append(grad[:, first : first + half])
    return jnp.concatenate(pieces, axis=1)


class Pairing:
    def __init__(self, groups, members):
        self.groups = groups
        self.members = members
        self.bits = groups.bit_length() - 1
        top = self.bits - 1
        self.partner = (1 << top, 1)
        self.others = (
            [1 << bit for bit in range(top)],
            [1 << (bit + 1) for bit in range(top)],
        )
        self.group = lax.axis_index("dp")
        self.odd = lax.axis_index("expert") % 2

    def chosen(self, masks):
        return jnp.where(self.odd == 1, masks[1], masks[0])

    def place(self, masks):
        return self.group ^ self.chosen(masks)

    def bit(self):
        return jnp.where(self.group & self.chosen(self.partner), 1, 0)

    def swap(self, value, masks):
        pairs = []
        for group in range(self.groups):
            for member in range(self.members):
                other = group ^ masks[member % 2]
                pairs.append((group * self.members + member, other * self.members + member))
        return lax.ppermute(value, ("dp", "expert"), pairs)

    def swap_partner(self, value):
        return self.swap(value, self.partner)

    def gather(self, kept, given):
        masks = [(0, 0), self.partner]
        held = jnp.stack([kept, self.swap_partner(given)])
        for step in zip(*self.others):
            held = jnp.concatenate([held, self.swap(held, step)])
            masks = masks + [(even ^ step[0], odd ^ step[1]) for even, odd in masks]
        out = jnp.zeros((self.groups,) + kept.shape, kept.dtype)
        for index, mask in enumerate(masks):
            out = lax.dynamic_update_slice_in_dim(
                out, held[index : index + 1], self.place(mask), 0
            )
        return out

    def scatter(self, grad):
        masks = [(0, 0), self.partner]
        for step in zip(*self.others):
            masks = masks + [(even ^ step[0], odd ^ step[1]) for even, odd in masks]
        held = [lax.dynamic_index_in_dim(grad, self.place(mask), 0, False) for mask in masks]
        for step in reversed(list(zip(*self.others))):
            half = len(held) // 2
            arrived = self.swap(jnp.stack(held[half:]), step)
            held = [
                (held[index].astype(f32) + arrived[index].astype(f32)).astype(bf16)
                for index in range(half)
            ]
        return (held[0], self.swap_partner(held[1]))

    def total(self, value):
        for bit in range(self.bits):
            value = value + self.swap(value, (1 << bit, 1 << bit))
        return value


def body(
    tokens,
    target,
    valid,
    routes,
    lengths,
    first_gain_vector,
    second_gain_vector,
    latent_gain_vector,
    latent_compress_weight,
    query_weight,
    latent_expand_weight,
    output_weight,
    router_weight,
    shared_gate_weight,
    shared_up_weight,
    shared_down_weight,
    expert_gate_weight,
    expert_up_weight,
    expert_down_weight,
):
    rows, width = tokens.shape
    members = lax.axis_size("expert")
    groups = lax.axis_size("dp")
    member = lax.axis_index("expert")
    group = lax.axis_index("dp")
    group_size = rows * members
    local_experts = expert_gate_weight.shape[0]
    route_count = routes.shape[1]
    expert_count = router_weight.shape[1]
    hidden_width = expert_gate_weight.shape[2]
    capacity = rows * route_count * 4 // (3 * local_experts * members)
    pairing = Pairing(groups, members)
    bit = pairing.bit()

    def pick(weight, index):
        return lax.dynamic_index_in_dim(weight, index, 0, False)

    down_t = jnp.swapaxes(expert_down_weight, 1, 2)
    gate_w, up_w, down_w = [
        pairing.gather(pick(weight, bit), pick(weight, 1 - bit)).reshape(width, hidden_width)
        for weight in (expert_gate_weight, expert_up_weight, down_t)
    ]

    counted = valid.astype(f32)
    count = lax.psum(jnp.sum(counted), ("dp", "expert"))

    tokens_float = tokens.astype(f32)
    own_unit, own_factor = normalize(tokens_float)
    own_normed = (own_unit * first_gain_vector).astype(bf16)
    projected = dot_plain(own_normed, latent_compress_weight)
    own_first = (group * members + member) * rows
    own_place = (own_first + jnp.arange(rows, dtype=jnp.int32)) % SEQ
    own_cos, own_sin = angles(own_place, ROPE // 2)
    latent_unit, latent_factor = normalize(projected[:, :LATENT])
    latent = jnp.concatenate(
        [latent_unit * latent_gain_vector, rotate(projected[:, LATENT:], own_cos, own_sin)], axis=1
    ).astype(bf16)
    group_latent = lax.all_gather(latent, "expert", axis=0, tiled=True)
    normed = lax.all_gather(own_normed, "expert", axis=0, tiled=True)
    previous = lax.ppermute(group_latent, "dp", [(i, i + 1) for i in range(groups - 1)])
    key_latent = jnp.concatenate([previous, group_latent], axis=0)

    index = group * group_size + jnp.arange(group_size, dtype=jnp.int32)
    seq_id = jnp.floor_divide(index, SEQ)
    place = index - seq_id * SEQ
    bounds = lax.dynamic_slice_in_dim(
        jnp.cumsum(lengths, axis=1), group * group_size // SEQ, 1, 0
    )
    doc_start = jnp.max(jnp.where(bounds <= place[:, None], bounds, 0), axis=1)
    in_block = jnp.arange(group_size, dtype=jnp.int32) % QUERY_BLOCK
    low = jnp.maximum(doc_start - place + WINDOW + in_block, in_block + 1)[:, None]
    cosine, sine = angles(place, ROPE // 2)
    cosine = jnp.concatenate([cosine] * 4, axis=1)
    sine = jnp.concatenate([-sine, -sine, sine, sine], axis=1)

    hot = jnp.any(routes[:, :, None] == jnp.arange(expert_count, dtype=jnp.int32), axis=1)
    routes_t = routes.T.reshape(route_count, members, rows)
    order = jnp.arange(rows, dtype=jnp.int32)
    earlier = (order[:, None] < order[None, :]).astype(bf16)
    mine = member * local_experts + bit
    other = member * local_experts + 1 - bit

    def slots_of(expert):
        hit = jnp.any(routes_t == expert, axis=0)
        rank = dot_plain(hit.astype(bf16), earlier).astype(jnp.int32)
        slot = jnp.arange(capacity, dtype=jnp.int32)[None, :, None]
        return (hit[:, None, :] & (rank[:, None, :] == slot)).astype(bf16)

    slots_mine, slots_other = slots_of(mine), slots_of(other)

    def to_slots(slots, values):
        return jnp.einsum(
            "bst,btd->bsd", slots, values.reshape(members, rows, -1), preferred_element_type=f32
        )

    def from_slots(slots, values):
        return jnp.einsum(
            "bst,bsd->btd", slots, values, preferred_element_type=f32
        ).reshape(group_size, -1)

    query_w = split_query_columns(query_weight)
    kv = dot_plain(key_latent[:, :LATENT], latent_expand_weight).astype(bf16)
    half = LATENT + ROPE // 2
    key_rope = jnp.concatenate(
        [key_latent[:, LATENT:half]] * 2 + [key_latent[:, half:]] * 2, axis=1
    )
    query, mixed, logs, attention_part = attend(
        normed, cosine, sine, low, query_w, kv, key_rope, output_weight
    )
    attention = lax.psum_scatter(attention_part, "expert", scatter_dimension=0, tiled=True)
    hidden = tokens_float + attention.astype(f32)
    hidden_unit, hidden_factor = normalize(hidden)
    own_branch = (hidden_unit * second_gain_vector).astype(bf16)
    branch = lax.all_gather(own_branch, "expert", axis=0, tiled=True)

    logits = jnp.where(hot, dot_plain(branch, router_weight), masked_value)
    top = jnp.max(logits, axis=1, keepdims=True)
    raised = jnp.where(hot, jnp.exp(logits - top), 0.0)
    gates = raised / jnp.sum(raised, axis=1, keepdims=True)
    experts = jnp.arange(expert_count, dtype=jnp.int32)[None, :]
    gate_mine = jnp.sum(jnp.where(experts == mine, gates, 0.0), axis=1, keepdims=True)
    gate_other = jnp.sum(jnp.where(experts == other, gates, 0.0), axis=1, keepdims=True)

    in_other = to_slots(slots_other, branch).astype(bf16)
    in_arrived = pairing.swap_partner(in_other)
    in_mine = to_slots(slots_mine, branch).astype(bf16)

    def expert_forward(slot_in):
        flat = slot_in.reshape(-1, width)
        gate = dot_plain(flat, gate_w)
        up = dot_plain(flat, up_w)
        act, slope = silu_parts(gate)
        inner = (act * up).astype(bf16)
        out = dot_right_t(inner, down_w).astype(bf16).reshape(slot_in.shape)
        return (flat, act.astype(bf16), (up * slope).astype(bf16), inner, out)

    flat_m, act_m, slope_m, inner_m, out_mine = expert_forward(in_mine)
    shared_gate = dot_plain(branch, shared_gate_weight)
    shared_up = dot_plain(branch, shared_up_weight)
    shared_act, shared_slope = silu_parts(shared_gate)
    shared_hidden = (shared_act * shared_up).astype(bf16)
    flat_a, act_a, slope_a, inner_a, out_arrived = expert_forward(in_arrived)
    out_other = pairing.swap_partner(out_arrived)
    branch_part = (
        dot_plain(shared_hidden, shared_down_weight)
        + gate_mine * from_slots(slots_mine, out_mine)
        + gate_other * from_slots(slots_other, out_other)
    ).astype(bf16)
    branch_sum = lax.psum_scatter(branch_part, "expert", scatter_dimension=0, tiled=True)
    result = hidden + branch_sum.astype(f32)
    difference = result - target.astype(f32)
    squares = jnp.sum(counted[:, None] * difference * difference)
    total_tokens = rows * members * groups
    grad_out = total_tokens / count * counted[:, None] * difference

    grad_low = lax.all_gather(grad_out.astype(bf16), "expert", axis=0, tiled=True)

    def slot_gates(slots, gate):
        return jnp.sum(slots.astype(f32) * gate.reshape(members, 1, rows), axis=2)

    def out_grads(slots, gate, out):
        grads = to_slots(slots, grad_low)
        gate_grad = jnp.sum(grads * out.astype(f32), axis=2)
        gate_grad = jnp.sum(slots.astype(f32) * gate_grad[:, :, None], axis=1).reshape(group_size, 1)
        return ((slot_gates(slots, gate)[:, :, None] * grads).astype(bf16), gate_grad)

    out_grad_other, gate_grad_other = out_grads(slots_other, gate_other, out_other)
    out_grad_arrived = pairing.swap_partner(out_grad_other)
    out_grad_mine, gate_grad_mine = out_grads(slots_mine, gate_mine, out_mine)

    def expert_backward(out_grad, act, slope):
        flat = out_grad.reshape(-1, width)
        inner_grad = dot_plain(flat, down_w)
        gate_grad = (inner_grad * slope.astype(f32)).astype(bf16)
        up_grad = (inner_grad * act.astype(f32)).astype(bf16)
        in_grad = (dot_right_t(gate_grad, gate_w) + dot_right_t(up_grad, up_w)).astype(bf16)
        return (flat, gate_grad, up_grad, in_grad.reshape(out_grad.shape))

    flat_gm, gate_gm, up_gm, in_grad_mine = expert_backward(out_grad_mine, act_m, slope_m)
    grad_hidden = dot_right_t(grad_low, shared_down_weight)
    grad_shared_gate = (grad_hidden * shared_up * shared_slope).astype(bf16)
    grad_shared_up = (grad_hidden * shared_act).astype(bf16)
    flat_ga, gate_ga, up_ga, in_grad_arrived = expert_backward(out_grad_arrived, act_a, slope_a)
    in_grad_other = pairing.swap_partner(in_grad_arrived)

    gate_grads = jnp.where(experts == mine, gate_grad_mine, 0.0) + jnp.where(
        experts == other, gate_grad_other, 0.0
    )
    logit_grad = gates * (gate_grads - jnp.sum(gates * gate_grads, axis=1, keepdims=True))
    grad_router = dot_left_t(branch, logit_grad.astype(bf16))
    branch_grad_part = (
        dot_right_t(grad_shared_gate, shared_gate_weight)
        + dot_right_t(grad_shared_up, shared_up_weight)
        + dot_right_t(logit_grad.astype(bf16), router_weight)
        + from_slots(slots_mine, in_grad_mine)
        + from_slots(slots_other, in_grad_other)
    ).astype(bf16)
    branch_grad = lax.psum_scatter(
        branch_grad_part, "expert", scatter_dimension=0, tiled=True
    ).astype(f32)

    def weight_grad(left_m, left_a, right_m, right_a):
        left = jnp.concatenate([left_m, left_a])
        right = jnp.concatenate([right_m, right_a])
        grad = dot_left_t(left, right).astype(bf16).reshape(groups, -1, hidden_width)
        own, others = pairing.scatter(grad)
        own, others = own.astype(f32), others.astype(f32)
        return jnp.where(bit == 0, jnp.stack([own, others]), jnp.stack([others, own]))

    expert_down_gradient = jnp.swapaxes(weight_grad(flat_gm, flat_ga, inner_m, inner_a), 1, 2)
    expert_gate_gradient = weight_grad(flat_m, flat_a, gate_gm, gate_ga)
    expert_up_gradient = weight_grad(flat_m, flat_a, up_gm, up_ga)

    def sum_groups(grad):
        return lax.psum_scatter(grad, "dp", scatter_dimension=0, tiled=True).astype(f32)

    shared_cols = shared_gate.shape[1]
    shared_grads = sum_groups(
        jnp.concatenate(
            [
                dot_left_t(branch, grad_shared_gate).astype(bf16),
                dot_left_t(branch, grad_shared_up).astype(bf16),
                dot_left_t(grad_low, shared_hidden).astype(bf16),
            ],
            axis=1,
        )
    )
    shared_gate_gradient = shared_grads[:, :shared_cols]
    shared_up_gradient = shared_grads[:, shared_cols : 2 * shared_cols]
    shared_down_gradient = shared_grads[:, 2 * shared_cols :].T

    grad_norm2 = jnp.sum(branch_grad * hidden_unit, axis=0)
    grad_hidden_own = grad_out + norm_back(
        branch_grad, hidden_unit, hidden_factor, second_gain_vector
    )
    grad_attention = lax.all_gather(grad_hidden_own.astype(bf16), "expert", axis=0, tiled=True)
    query_grad, normed_grad_part, kv_past, rope_past, kv_own, rope_own = attend_back(
        grad_attention, query, logs, cosine, sine, low, query_w, kv, key_rope, output_weight
    )

    def latent_back(kv_grad, rope_grad):
        half = ROPE // 2
        first = rope_grad[:, :half] + rope_grad[:, half:ROPE]
        second = rope_grad[:, ROPE : ROPE + half] + rope_grad[:, ROPE + half :]
        return jnp.concatenate(
            [dot_right_t(kv_grad, latent_expand_weight), first, second], axis=1
        )

    back = lax.ppermute(
        latent_back(kv_past, rope_past).astype(bf16),
        "dp",
        [(i + 1, i) for i in range(groups - 1)],
    )
    latent_grad = lax.psum_scatter(
        (latent_back(kv_own, rope_own) + back.astype(f32)).astype(bf16),
        "expert",
        scatter_dimension=0,
        tiled=True,
    ).astype(f32)
    normed_grad = lax.psum_scatter(
        normed_grad_part, "expert", scatter_dimension=0, tiled=True
    ).astype(f32)

    expand_grad = (
        dot_left_t(previous[:, :LATENT], kv_past) + dot_left_t(group_latent[:, :LATENT], kv_own)
    ).astype(bf16)
    expand_shape = expand_grad.shape
    query_cols = query_w.shape[1]
    attention_grads = sum_groups(
        jnp.concatenate(
            [
                dot_left_t(normed, query_grad).astype(bf16),
                dot_left_t(grad_attention, mixed).astype(bf16),
                expand_grad.reshape(width, -1),
            ],
            axis=1,
        )
    )
    query_weight_gradient = join_query_columns(attention_grads[:, :query_cols])
    output_weight_gradient = attention_grads[:, query_cols : query_cols + 2 * VDIM].T
    latent_expand_gradient = attention_grads[:, query_cols + 2 * VDIM :].reshape(
        expand_shape[0] // groups, expand_shape[1]
    )

    grad_latent_gain = jnp.sum(latent_grad[:, :LATENT] * latent_unit, axis=0)
    grad_projected = jnp.concatenate(
        [
            norm_back(latent_grad[:, :LATENT], latent_unit, latent_factor, latent_gain_vector),
            unrotate(latent_grad[:, LATENT:], own_cos, own_sin),
        ],
        axis=1,
    ).astype(bf16)
    group_projected = lax.all_gather(grad_projected, "expert", axis=0, tiled=True)
    slice_cols = width // members
    normed_slice = lax.dynamic_slice_in_dim(normed, member * slice_cols, slice_cols, 1)
    compress_slice = pairing.total(dot_left_t(normed_slice, group_projected))
    grad_kva = lax.all_gather(
        compress_slice.astype(bf16), "expert", axis=0, tiled=True
    ).astype(f32)
    normed_grad = normed_grad + dot_right_t(grad_projected, latent_compress_weight)
    grad_norm1 = jnp.sum(normed_grad * own_unit, axis=0)
    grad_tokens = grad_hidden_own + norm_back(
        normed_grad, own_unit, own_factor, first_gain_vector
    )
    squares, grad_norm1, grad_norm2, grad_latent_gain, grad_router = lax.psum(
        (squares, grad_norm1, grad_norm2, grad_latent_gain, grad_router), ("dp", "expert")
    )
    return (
        result.astype(bf16),
        squares / (count * width),
        grad_tokens,
        grad_norm1,
        grad_norm2,
        grad_latent_gain,
        grad_kva,
        query_weight_gradient,
        latent_expand_gradient,
        output_weight_gradient,
        grad_router,
        shared_gate_gradient,
        shared_up_gradient,
        shared_down_gradient,
        expert_gate_gradient,
        expert_up_gradient,
        expert_down_gradient,
    )


def solution(mesh):
    placed = (
        P(("dp", "expert"), None),
        P(("dp", "expert"), None),
        P(("dp", "expert")),
        P("dp", None),
        P(),
        P(),
        P(),
        P(),
        P(),
        P(None, "expert"),
        P(None, "expert"),
        P("expert", None),
        P(),
        P(None, "expert"),
        P(None, "expert"),
        P("expert", None),
        P("expert", "dp", None),
        P("expert", "dp", None),
        P("expert", None, "dp"),
    )
    return jax.shard_map(
        body,
        mesh=mesh,
        in_specs=placed,
        out_specs=(
            P(("dp", "expert"), None),
            P(),
            P(("dp", "expert"), None),
            P(),
            P(),
            P(),
            P(),
            P("dp", "expert"),
            P("dp", "expert"),
            P("expert", "dp"),
            P(),
            P("dp", "expert"),
            P("dp", "expert"),
            P("expert", "dp"),
            P("expert", "dp", None),
            P("expert", "dp", None),
            P("expert", None, "dp"),
        ),
        check_vma=False,
    )
```

```python
import functools

import jax
import jax.numpy as jnp
from jax import lax
from jax.experimental import pallas as pl
from jax.experimental.pallas import tpu as pltpu
from jax.sharding import PartitionSpec as P

NOPE = 128
ROPE = 64
VDIM = 128
LATENT = 512
SEQ = 4096
WINDOW = 1024
QUERY_BLOCK = 256

epsilon = 1e-06
masked_value = -1e30
score_scale = (NOPE + ROPE) ** (-0.5)
bf16 = jnp.bfloat16
f32 = jnp.float32
small_cost = pl.CostEstimate(flops=1, bytes_accessed=1, transcendentals=0)


def dot_plain(left, right):
    return lax.dot_general(left, right, (((1,), (0,)), ((), ())), preferred_element_type=f32)


def dot_right_t(left, right):
    return lax.dot_general(left, right, (((1,), (1,)), ((), ())), preferred_element_type=f32)


def dot_left_t(left, right):
    return lax.dot_general(left, right, (((0,), (0,)), ((), ())), preferred_element_type=f32)


def normalize(values):
    factor = lax.rsqrt(jnp.mean(values * values, axis=-1, keepdims=True) + epsilon)
    return (values * factor, factor)


def norm_back(grad_out, unit, factor, gain):
    grad_unit = grad_out * gain
    return factor * (grad_unit - unit * jnp.mean(grad_unit * unit, axis=-1, keepdims=True))


def angles(place, half):
    freq = jnp.exp(-jnp.log(10000.0) * jnp.arange(half, dtype=f32) / half)
    angle = place.astype(f32)[:, None] * freq[None, :]
    return (jnp.cos(angle), jnp.sin(angle))


def silu_parts(values):
    sigma = jax.nn.sigmoid(values)
    return (values * sigma, sigma * (1.0 + values * (1.0 - sigma)))


def head_lanes(block, head):
    lane = lax.broadcasted_iota(jnp.int32, (block, 2 * ROPE), 1)
    return (lane // (ROPE // 2)) % 2 == head


def allowed_keys(low, block, span):
    row = lax.broadcasted_iota(jnp.int32, (block, span), 0)
    col = lax.broadcasted_iota(jnp.int32, (block, span), 1)
    return (col <= row + WINDOW) & (col >= low)


def read_chunks(refs, first, last):
    return jnp.concatenate([ref[:, first:last] for ref in refs], axis=0)


def head_parts(query, lanes, kv, rope, head):
    turned = jnp.where(lanes, query[:, 2 * NOPE :], 0)
    query_head = jnp.concatenate([query[:, head * NOPE : (head + 1) * NOPE], turned], axis=1)
    base = head * (NOPE + VDIM)
    key_head = jnp.concatenate([read_chunks(kv, base, base + NOPE), rope], axis=1)
    return (query_head, key_head, read_chunks(kv, base + NOPE, base + NOPE + VDIM))


def attend_kernel(chunks, normed, cosine, sine, low, query_w, out_w, *refs):
    kv, key_rope = refs[:chunks], refs[chunks : 2 * chunks]
    query_out, mixed_out, log_out, part_out = refs[-4:]
    block = normed.shape[0]
    proj = dot_plain(normed[...], query_w[...])
    turned = proj[:, 2 * NOPE :]
    turned = turn(turned, cosine[...], sine[...])
    query = jnp.concatenate([proj[:, : 2 * NOPE], turned], axis=1).astype(bf16)
    query_out[...] = query
    mask = allowed_keys(low[...], block, WINDOW + block)
    rope = read_chunks(key_rope, 0, 2 * ROPE)
    mixed, logs = [], []
    for head in range(2):
        query_head, key_head, value_head = head_parts(query, head_lanes(block, head), kv, rope, head)
        scores = jnp.where(mask, dot_right_t(query_head, key_head) * score_scale, masked_value)
        top = jnp.max(scores, axis=1, keepdims=True)
        raised = jnp.exp(scores - top)
        total = jnp.sum(raised, axis=1, keepdims=True)
        probs = (raised * (1.0 / total)).astype(bf16)
        mixed.append(dot_plain(probs, value_head))
        logs.append(top + jnp.log(total))
    lane = lax.broadcasted_iota(jnp.int32, (block, 128), 1)
    log_out[...] = jnp.where(lane == 0, logs[0], logs[1])
    mixed = jnp.concatenate(mixed, axis=1).astype(bf16)
    mixed_out[...] = mixed
    part_out[...] = dot_plain(mixed, out_w[...]).astype(bf16)


def by_rows(block, cols, offset=0):
    return pl.BlockSpec((block, cols), lambda i: (i + offset, 0))


def whole(shape):
    return pl.BlockSpec(shape, lambda i: (0, 0))


def unread(arrays):
    return [pl.BlockSpec(memory_space=pl.ANY) for _ in arrays]


def turn(values, cosine, sine):
    return values * cosine + pltpu.roll(values, ROPE, 1) * sine


def turn_back(values, cosine, sine):
    return values * cosine - pltpu.roll(values, ROPE, 1) * sine


def own_keys_kernel(normed, cosine, sine, gain, compress, expand, *refs):
    kv, key_rope, latent = refs[-3:]
    projected = dot_right_t(normed[...], compress[...])
    unit, _ = normalize(projected[:, :LATENT])
    low = (unit * gain[...]).astype(bf16)
    latent[...] = low
    kv[...] = dot_plain(low, expand[...]).astype(bf16)
    key_rope[...] = turn(projected[:, LATENT:], cosine[...], sine[...]).astype(bf16)


def own_keys(normed, cosine, sine, gain, compress, expand, after):
    rows, width = normed.shape
    block = QUERY_BLOCK
    blocks = rows // block
    kv_cols, rope_cols = expand.shape[1], 2 * ROPE
    return pl.pallas_call(
        own_keys_kernel,
        grid=(blocks,),
        in_specs=[
            by_rows(block, width),
            by_rows(block, rope_cols),
            by_rows(block, rope_cols),
            whole((1, LATENT)),
            whole(compress.shape),
            whole(expand.shape),
        ]
        + unread(after),
        out_specs=[
            by_rows(block, kv_cols, blocks),
            by_rows(block, rope_cols, blocks),
            by_rows(block, LATENT),
        ],
        out_shape=[
            jax.ShapeDtypeStruct((2 * rows, kv_cols), bf16),
            jax.ShapeDtypeStruct((2 * rows, rope_cols), bf16),
            jax.ShapeDtypeStruct((rows, LATENT), bf16),
        ],
        compiler_params=pltpu.CompilerParams(vmem_limit_bytes=40 * 1024 * 1024),
        cost_estimate=small_cost,
        name="own_keys",
    )(normed, cosine, sine, gain[None], compress, expand, *after)


def past_keys_kernel(previous, expand, kv_in, rope_in, kv, key_rope):
    kv[...] = dot_plain(previous[:, :LATENT], expand[...]).astype(bf16)
    key_rope[...] = previous[:, LATENT:]


def past_keys(previous, expand, kv, key_rope):
    block = QUERY_BLOCK
    return pl.pallas_call(
        past_keys_kernel,
        grid=(previous.shape[0] // block,),
        in_specs=[by_rows(block, previous.shape[1]), whole(expand.shape)] + unread([kv, key_rope]),
        out_specs=[by_rows(block, kv.shape[1]), by_rows(block, key_rope.shape[1])],
        out_shape=[
            jax.ShapeDtypeStruct(kv.shape, bf16),
            jax.ShapeDtypeStruct(key_rope.shape, bf16),
        ],
        input_output_aliases={2: 0, 3: 1},
        cost_estimate=small_cost,
        name="past_keys",
    )(previous, expand, kv, key_rope)


def attend(normed, cosine, sine, low, query_w, kv, key_rope, out_w, after):
    rows, width = normed.shape
    block = QUERY_BLOCK
    chunks = 1 + WINDOW // block
    query_cols = query_w.shape[1]
    rows_of = functools.partial(by_rows, block)
    return pl.pallas_call(
        functools.partial(attend_kernel, chunks),
        grid=(rows // block,),
        in_specs=[
            rows_of(width),
            rows_of(2 * ROPE),
            rows_of(2 * ROPE),
            rows_of(1),
            whole(query_w.shape),
            whole(out_w.shape),
        ]
        + [rows_of(kv.shape[1], chunk) for chunk in range(chunks)]
        + [rows_of(key_rope.shape[1], chunk) for chunk in range(chunks)]
        + unread(after),
        out_specs=[rows_of(query_cols), rows_of(2 * VDIM), rows_of(128), rows_of(width)],
        out_shape=[
            jax.ShapeDtypeStruct((rows, query_cols), bf16),
            jax.ShapeDtypeStruct((rows, 2 * VDIM), bf16),
            jax.ShapeDtypeStruct((rows, 128), f32),
            jax.ShapeDtypeStruct((rows, width), bf16),
        ],
        compiler_params=pltpu.CompilerParams(vmem_limit_bytes=50 * 1024 * 1024),
        cost_estimate=small_cost,
        name="attend",
    )(normed, cosine, sine, low, query_w, out_w, *([kv] * chunks), *([key_rope] * chunks), *after)


def attend_back_kernel(
    chunks, grad, query_in, logs, cosine, sine, low, query_w, out_w, *refs
):
    kv, key_rope = refs[:chunks], refs[chunks : 2 * chunks]
    query_grad_out, part_out, kv_past, rope_past, kv_own, rope_own, kv_sum, rope_sum = refs[-8:]
    block = grad.shape[0]

    @pl.when(pl.program_id(0) == 0)
    def clear():
        kv_sum[...] = jnp.zeros_like(kv_sum)
        rope_sum[...] = jnp.zeros_like(rope_sum)

    def add(total, past, cols, piece):
        for chunk in range(chunks):
            part = piece[chunk * block : (chunk + 1) * block]
            if chunk < chunks - 1:
                part = part + total[chunk * block : (chunk + 1) * block, cols]
            if chunk == 0:
                past[:, cols] = part.astype(past.dtype)
            else:
                total[(chunk - 1) * block : chunk * block, cols] = part

    mixed_grad = dot_right_t(grad[...], out_w[...]).astype(bf16)
    mask = allowed_keys(low[...], block, WINDOW + block)
    rope = read_chunks(key_rope, 0, 2 * ROPE)
    query = query_in[...]
    plain, turned, rope_piece = [], 0.0, 0.0
    for head in range(2):
        lanes = head_lanes(block, head)
        query_head, key_head, value_head = head_parts(query, lanes, kv, rope, head)
        base = head * (NOPE + VDIM)
        grad_head = mixed_grad[:, head * VDIM : (head + 1) * VDIM]
        scores = jnp.where(mask, dot_right_t(query_head, key_head) * score_scale, masked_value)
        probs = jnp.exp(scores - logs[:, head : head + 1])
        prob_grad = dot_right_t(grad_head, value_head)
        shift = jnp.sum(probs * prob_grad, axis=1, keepdims=True)
        score_grad = (probs * (prob_grad - shift)).astype(bf16)
        key_piece = dot_left_t(score_grad, query_head) * score_scale
        add(kv_sum, kv_past, slice(base, base + NOPE), key_piece[:, :NOPE])
        value_piece = dot_left_t(probs.astype(bf16), grad_head)
        add(kv_sum, kv_past, slice(base + NOPE, base + NOPE + VDIM), value_piece)
        rope_piece = rope_piece + key_piece[:, NOPE:]
        query_piece = dot_plain(score_grad, key_head) * score_scale
        plain.append(query_piece[:, :NOPE])
        turned = turned + jnp.where(lanes, query_piece[:, NOPE:], 0.0)
    add(rope_sum, rope_past, slice(0, 2 * ROPE), rope_piece)
    turned = turn_back(turned, cosine[...], sine[...])
    query_grad = jnp.concatenate(plain + [turned], axis=1).astype(bf16)
    query_grad_out[...] = query_grad
    part_out[...] = dot_right_t(query_grad, query_w[...]).astype(bf16)

    @pl.when(pl.program_id(0) == pl.num_programs(0) - 1)
    def finish():
        kv_own[...] = kv_sum[...].astype(bf16)
        rope_own[...] = rope_sum[...].astype(bf16)


def attend_back(grad, query, logs, cosine, sine, low, query_w, kv, key_rope, out_w, after):
    rows, width = grad.shape
    block = QUERY_BLOCK
    chunks = 1 + WINDOW // block
    query_cols = query_w.shape[1]
    rows_of = functools.partial(by_rows, block)
    kv_cols, rope_cols = kv.shape[1], key_rope.shape[1]
    return pl.pallas_call(
        functools.partial(attend_back_kernel, chunks),
        grid=(rows // block,),
        in_specs=[
            rows_of(width),
            rows_of(query_cols),
            rows_of(128),
            rows_of(2 * ROPE),
            rows_of(2 * ROPE),
            rows_of(1),
            whole(query_w.shape),
            whole(out_w.shape),
        ]
        + [rows_of(kv_cols, chunk) for chunk in range(chunks)]
        + [rows_of(rope_cols, chunk) for chunk in range(chunks)]
        + unread(after),
        out_specs=[
            rows_of(query_cols),
            rows_of(width),
            rows_of(kv_cols),
            rows_of(rope_cols),
            whole((WINDOW, kv_cols)),
            whole((WINDOW, rope_cols)),
        ],
        out_shape=[
            jax.ShapeDtypeStruct((rows, query_cols), bf16),
            jax.ShapeDtypeStruct((rows, width), bf16),
            jax.ShapeDtypeStruct((rows, kv_cols), bf16),
            jax.ShapeDtypeStruct((rows, rope_cols), bf16),
            jax.ShapeDtypeStruct((WINDOW, kv_cols), bf16),
            jax.ShapeDtypeStruct((WINDOW, rope_cols), bf16),
        ],
        scratch_shapes=[pltpu.VMEM((WINDOW, kv_cols), f32), pltpu.VMEM((WINDOW, rope_cols), f32)],
        compiler_params=pltpu.CompilerParams(vmem_limit_bytes=50 * 1024 * 1024),
        cost_estimate=small_cost,
        name="attend_back",
    )(
        grad,
        query,
        logs,
        cosine,
        sine,
        low,
        query_w,
        out_w,
        *([kv] * chunks),
        *([key_rope] * chunks),
        *after,
    )


def norm_kernel(tokens, attention, gain, *refs):
    hidden_out, unit_out, factor_out, branch_out = refs[-4:]
    hidden = tokens[...].astype(f32) + attention[...].astype(f32)
    unit, factor = normalize(hidden)
    hidden_out[...] = hidden
    unit_out[...] = unit
    factor_out[...] = factor
    branch_out[...] = (unit * gain[...]).astype(bf16)


def norm(tokens, attention, gain, after):
    rows, width = tokens.shape
    full = whole((rows, width))
    return pl.pallas_call(
        norm_kernel,
        grid=(1,),
        in_specs=[full, full, whole((1, width))] + unread(after),
        out_specs=[full, full, whole((rows, 1)), full],
        out_shape=[
            jax.ShapeDtypeStruct((rows, width), f32),
            jax.ShapeDtypeStruct((rows, width), f32),
            jax.ShapeDtypeStruct((rows, 1), f32),
            jax.ShapeDtypeStruct((rows, width), bf16),
        ],
        cost_estimate=small_cost,
        name="norm",
    )(tokens, attention, gain[None], *after)


def norm_back_kernel(branch_grad, grad_out, unit, factor, gain, *refs):
    hidden_grad_out, low_out, gain_grad_out = refs[-3:]
    grad = branch_grad[...].astype(f32)
    hidden_grad = grad_out[...] + norm_back(grad, unit[...], factor[...], gain[...])
    hidden_grad_out[...] = hidden_grad
    low_out[...] = hidden_grad.astype(bf16)
    gain_grad_out[...] = jnp.sum(grad * unit[...], axis=0, keepdims=True)


def norm_back_rows(branch_grad, grad_out, unit, factor, gain, after):
    rows, width = unit.shape
    full, line = whole((rows, width)), whole((1, width))
    return pl.pallas_call(
        norm_back_kernel,
        grid=(1,),
        in_specs=[full, full, full, whole((rows, 1)), line] + unread(after),
        out_specs=[full, full, line],
        out_shape=[
            jax.ShapeDtypeStruct((rows, width), f32),
            jax.ShapeDtypeStruct((rows, width), bf16),
            jax.ShapeDtypeStruct((1, width), f32),
        ],
        cost_estimate=small_cost,
        name="norm_back",
    )(branch_grad, grad_out, unit, factor, gain[None], *after)


def load_all(step, pairs):
    @pl.when(step == 0)
    def start():
        for source, target, semaphore in pairs:
            pltpu.make_async_copy(source, target, semaphore).start()


def wait_for(pairs):
    for source, target, semaphore in pairs:
        pltpu.make_async_copy(source, target, semaphore).wait()


def expert_kernel(count, extra, places, slot_in, *refs):
    act_out, slope_out, inner_out, out, held, gate_sum, up_sum, semaphores = refs[count + extra :]
    step = pl.program_id(0)
    order = [(ref, item) for ref in refs[:count] for item in (0, 1)]
    order += [(ref, 2) for ref in refs[:count]]
    pairs = [
        (ref.at[item], held.at[index], semaphores.at[index])
        for index, (ref, item) in enumerate(order)
    ]
    load_all(step, pairs)
    for index in range(count):

        @pl.when(step == index)
        def add(index=index):
            wait_for(pairs[2 * index : 2 * index + 2])
            gate = dot_plain(slot_in[...], held[2 * index])
            up = dot_plain(slot_in[...], held[2 * index + 1])
            if index > 0:
                gate = gate + gate_sum[...]
                up = up + up_sum[...]
            if index < count - 1:
                gate_sum[...] = gate
                up_sum[...] = up
            else:
                act, slope = silu_parts(gate)
                act_out[...] = act.astype(bf16)
                slope_out[...] = (up * slope).astype(bf16)
                inner_out[...] = (act * up).astype(bf16)

        @pl.when(step == count + index)
        def down(index=index):
            wait_for(pairs[2 * count + index : 2 * count + index + 1])
            out[...] = dot_right_t(inner_out[...], held[2 * count + index]).astype(bf16)


def expert_back_kernel(count, extra, places, out_grad, act, slope, *refs):
    gate_out, up_out, in_grad, held, inner_sum, semaphores = refs[count + extra :]
    step = pl.program_id(0)
    order = [(ref, 2) for ref in refs[:count]]
    order += [(ref, item) for ref in refs[:count] for item in (0, 1)]
    pairs = [
        (ref.at[item], held.at[index], semaphores.at[index])
        for index, (ref, item) in enumerate(order)
    ]
    load_all(step, pairs)
    for index in range(count):

        @pl.when(step == index)
        def add(index=index):
            wait_for(pairs[index : index + 1])
            inner = dot_plain(out_grad[...], held[index])
            if index > 0:
                inner = inner + inner_sum[...]
            if index < count - 1:
                inner_sum[...] = inner
            else:
                gate_out[...] = (inner * slope[...].astype(f32)).astype(bf16)
                up_out[...] = (inner * act[...].astype(f32)).astype(bf16)

        @pl.when(step == count + index)
        def back(index=index):
            first = count + 2 * index
            wait_for(pairs[first : first + 2])
            in_grad[...] = (
                dot_right_t(gate_out[...], held[first]) + dot_right_t(up_out[...], held[first + 1])
            ).astype(bf16)


def expert_call(kernel, name, places, slots, fixed, weights, outputs, sums, after):
    count = len(weights)
    rows, width = slots.shape
    _, depth, hidden = weights[0].shape
    inner = pl.BlockSpec((rows, hidden), lambda i, places: (0, 0))
    return pl.pallas_call(
        functools.partial(kernel, count, len(after)),
        grid_spec=pltpu.PrefetchScalarGridSpec(
            num_scalar_prefetch=1,
            grid=(2 * count,),
            in_specs=[
                pl.BlockSpec((rows, depth), lambda i, places: (0, places[jnp.minimum(i, count - 1)]))
            ]
            + [inner] * len(fixed)
            + unread(weights)
            + unread(after),
            out_specs=[inner] * outputs
            + [pl.BlockSpec((rows, depth), lambda i, places: (0, places[jnp.maximum(i - count, 0)]))],
            scratch_shapes=[pltpu.VMEM((3 * count, depth, hidden), bf16)]
            + [pltpu.VMEM((rows, hidden), f32)] * sums
            + [pltpu.SemaphoreType.DMA((3 * count,))],
        ),
        out_shape=[jax.ShapeDtypeStruct((rows, hidden), bf16)] * outputs
        + [jax.ShapeDtypeStruct((rows, width), bf16)],
        compiler_params=pltpu.CompilerParams(vmem_limit_bytes=56 * 1024 * 1024),
        cost_estimate=small_cost,
        name=name,
    )(places, slots, *fixed, *weights, *after)


def weight_grad_kernel(count, plan, places, *refs):
    half = count // 2
    outs = refs[-1 - half * len(plan) :]
    step = pl.program_id(0)
    for number, segments in enumerate(plan):
        first = 0
        for terms in segments:
            grad = 0.0
            for left, right in terms:
                grad = grad + dot_left_t(refs[left][...], refs[right][...])
            last = first + grad.shape[1]
            for index in range(count):

                @pl.when(step == index)
                def store(index=index, number=number, cols=slice(first, last), grad=grad):
                    if index < half:
                        outs[0][index, number, :, cols] = grad.astype(bf16)
                    else:
                        out = outs[1 + (index - half) * len(plan) + number]
                        out[:, cols] = grad.astype(bf16)

            first = last


def weight_grads(name, places, outputs, after=()):
    count = places.shape[0]
    lefts, rights = [], []
    for segments in outputs:
        for terms in segments:
            for left, right in terms:
                if not any(left is other for other in lefts):
                    lefts.append(left)
                rights.append(right)
    plan, position, flops = [], len(lefts), 0
    for segments in outputs:
        planned, columns = [], 0
        for terms in segments:
            numbers = []
            for left, right in terms:
                numbers.append(([left is other for other in lefts].index(True), position))
                position += 1
                flops += 2 * left.shape[0] * left.shape[1] * right.shape[1]
            planned.append(numbers)
            columns += terms[0][1].shape[1]
        plan.append(planned)
    piece = (lefts[0].shape[1] // count, columns)
    shapes = [(count // 2, len(outputs)) + piece] + [piece] * (count // 2 * len(outputs))
    kept, *given = pl.pallas_call(
        functools.partial(weight_grad_kernel, count, plan),
        grid_spec=pltpu.PrefetchScalarGridSpec(
            num_scalar_prefetch=1,
            grid=(count,),
            in_specs=[
                pl.BlockSpec((left.shape[0], left.shape[1] // count), lambda i, places: (0, places[i]))
                for left in lefts
            ]
            + [pl.BlockSpec(right.shape, lambda i, places: (0, 0)) for right in rights]
            + unread(after),
            out_specs=[pl.BlockSpec(shapes[0], lambda i, places: (0, 0, 0, 0))]
            + [pl.BlockSpec(shape, lambda i, places: (0, 0)) for shape in shapes[1:]],
        ),
        out_shape=[jax.ShapeDtypeStruct(shape, bf16) for shape in shapes],
        compiler_params=pltpu.CompilerParams(vmem_limit_bytes=56 * 1024 * 1024),
        cost_estimate=small_cost,
        name=name,
    )(places, *lefts, *rights, *after)
    return kept, given


def lead(array, *indices):
    shape = (1,) * len(indices) + array.shape[-2:]
    return pl.BlockSpec(shape, lambda i, *prefetched: indices + (0, 0))


def flat(ref):
    for _ in ref.shape[2:]:
        ref = ref.at[0]
    return ref[...].astype(f32)


def finish_kernel(cuts, own, arrived, other, *refs):
    total = flat(own) + flat(arrived) + flat(other)
    outs = refs[-len(cuts) :]
    for (first, last, turned), out in zip(cuts, outs):
        part = total[:, first:last]
        out[...] = part.T[: out.shape[0]] if turned else part


def finish(name, parts, cuts, sizes, after):
    own, arrived, other = parts
    arrived, other = arrived[0], other[0]
    rows = own.shape[-2]
    shapes = [
        (size, rows) if turned else (rows, last - first)
        for (first, last, turned), size in zip(cuts, sizes)
    ]
    return pl.pallas_call(
        functools.partial(finish_kernel, cuts),
        grid=(1,),
        in_specs=[lead(own, 0, 0), lead(arrived), lead(other)] + unread(after),
        out_specs=[whole(shape) for shape in shapes],
        out_shape=[jax.ShapeDtypeStruct(shape, f32) for shape in shapes],
        compiler_params=pltpu.CompilerParams(vmem_limit_bytes=40 * 1024 * 1024),
        cost_estimate=small_cost,
        name=name,
    )(own, arrived, other, *after)


def prepare_kernel(bits, gate, up, down, *outs):
    for step in range(2):

        @pl.when(pl.program_id(0) == step)
        def copy(step=step):
            outs[step][0] = gate[0]
            outs[step][1] = up[0]
            outs[step][2] = down[0].T


def prepare(bit, gate, up, down):
    _, depth, hidden = gate.shape
    shape = (3, depth, hidden)

    def chosen(array):
        return pl.BlockSpec(
            (1,) + array.shape[1:], lambda i, bits: (jnp.where(i == 0, 1 - bits[0], bits[0]), 0, 0)
        )

    return pl.pallas_call(
        prepare_kernel,
        grid_spec=pltpu.PrefetchScalarGridSpec(
            num_scalar_prefetch=1,
            grid=(2,),
            in_specs=[chosen(gate), chosen(up), chosen(down)],
            out_specs=[pl.BlockSpec(shape, lambda i, bits: (0, 0, 0))] * 2,
        ),
        out_shape=[jax.ShapeDtypeStruct(shape, bf16)] * 2,
        compiler_params=pltpu.CompilerParams(vmem_limit_bytes=56 * 1024 * 1024),
        cost_estimate=small_cost,
        name="prepare",
    )(bit.reshape(1), gate, up, down)


def dispatch_kernel(branch, slots, *refs):
    mine_out, other_out = refs[-2:]
    capacity = slots.shape[1] // 2
    for owner in range(slots.shape[0]):
        rows = slots.shape[2]
        rows_in = dot_plain(slots[owner], branch[owner * rows : (owner + 1) * rows]).astype(bf16)
        mine_out[owner * capacity : (owner + 1) * capacity] = rows_in[:capacity]
        other_out[owner * capacity : (owner + 1) * capacity] = rows_in[capacity:]


def slot_specs(slots, step):
    members, both, rows = slots.shape
    return (
        pl.BlockSpec((step, both, rows), lambda i: (i, 0, 0)),
        functools.partial(by_rows, step * both // 2),
        functools.partial(by_rows, step * rows),
        (members // step,),
    )


def dispatch(branch, slots, after):
    members, both, _ = slots.shape
    width = branch.shape[1]
    slot_spec, slot_rows, token_rows, grid = slot_specs(slots, 2)
    shape = jax.ShapeDtypeStruct((members * both // 2, width), bf16)
    return pl.pallas_call(
        dispatch_kernel,
        grid=grid,
        in_specs=[token_rows(width), slot_spec] + unread(after),
        out_specs=[slot_rows(width)] * 2,
        out_shape=[shape, shape],
        cost_estimate=small_cost,
        name="dispatch",
    )(branch, slots, *after)


def shared_kernel(branch, weights, act_out, slope_out, inner_out):
    hidden = act_out.shape[1]
    both = dot_right_t(branch[...], weights[...])
    gate, up = both[:, :hidden], both[:, hidden:]
    act, slope = silu_parts(gate)
    act_out[...] = act.astype(bf16)
    slope_out[...] = (up * slope).astype(bf16)
    inner_out[...] = (act * up).astype(bf16)


def shared_forward(branch, weights):
    rows, width = branch.shape
    hidden = weights.shape[0] // 3
    block = 512
    shape = jax.ShapeDtypeStruct((rows, hidden), bf16)
    return pl.pallas_call(
        shared_kernel,
        grid=(rows // block,),
        in_specs=[by_rows(block, width), whole((2 * hidden, width))],
        out_specs=[by_rows(block, hidden)] * 3,
        out_shape=[shape] * 3,
        compiler_params=pltpu.CompilerParams(vmem_limit_bytes=40 * 1024 * 1024),
        cost_estimate=small_cost,
        name="shared_forward",
    )(branch, weights)


def shared_back_kernel(grad, down, act, slope, *refs):
    out = refs[-1]
    hidden = act.shape[1]
    inner = dot_right_t(grad[...], down[...])
    out[:, :hidden] = (inner * slope[...].astype(f32)).astype(bf16)
    out[:, hidden:] = (inner * act[...].astype(f32)).astype(bf16)


def shared_back(grad, weights, act, slope, after):
    rows, width = grad.shape
    hidden = act.shape[1]
    block = 512
    return pl.pallas_call(
        shared_back_kernel,
        grid=(rows // block,),
        in_specs=[
            by_rows(block, width),
            pl.BlockSpec((hidden, width), lambda i: (2, 0)),
            by_rows(block, hidden),
            by_rows(block, hidden),
        ]
        + unread(after),
        out_specs=by_rows(block, 2 * hidden),
        out_shape=jax.ShapeDtypeStruct((rows, 2 * hidden), bf16),
        compiler_params=pltpu.CompilerParams(vmem_limit_bytes=40 * 1024 * 1024),
        cost_estimate=small_cost,
        name="shared_back",
    )(grad, weights, act, slope, *after)


def combine_kernel(inner, down, slots, out_mine, out_other, gate_mine, gate_other, out):
    rows = slots.shape[2]
    capacity = slots.shape[1] // 2
    total = dot_plain(inner[...], down[...])
    for owner in range(slots.shape[0]):
        tokens = slice(owner * rows, (owner + 1) * rows)
        places = slice(owner * capacity, (owner + 1) * capacity)
        mine = dot_left_t(slots[owner, :capacity], out_mine[places])
        other = dot_left_t(slots[owner, capacity:], out_other[places])
        part = total[tokens] + gate_mine[tokens] * mine + gate_other[tokens] * other
        out[tokens] = part.astype(bf16)


def combine(inner, weights, slots, out_mine, out_other, gate_mine, gate_other):
    hidden, width = inner.shape[1], weights.shape[1]
    slot_spec, slot_rows, token_rows, grid = slot_specs(slots, 4)
    return pl.pallas_call(
        combine_kernel,
        grid=grid,
        in_specs=[
            token_rows(hidden),
            pl.BlockSpec((hidden, width), lambda i: (2, 0)),
            slot_spec,
            slot_rows(width),
            slot_rows(width),
            token_rows(1),
            token_rows(1),
        ],
        out_specs=token_rows(width),
        out_shape=jax.ShapeDtypeStruct((inner.shape[0], width), bf16),
        compiler_params=pltpu.CompilerParams(vmem_limit_bytes=50 * 1024 * 1024),
        cost_estimate=small_cost,
        name="combine",
    )(inner, weights, slots, out_mine, out_other, gate_mine, gate_other)


def out_grad_kernel(grad, slots, out_mine, out_other, gate_mine, gate_other, *refs):
    grad_mine, grad_other, gate_grad_mine, gate_grad_other = refs
    rows = slots.shape[2]
    capacity = slots.shape[1] // 2
    for owner in range(slots.shape[0]):
        places = slice(owner * capacity, (owner + 1) * capacity)
        hot = slots[owner].astype(f32)
        both = dot_plain(slots[owner], grad[owner * rows : (owner + 1) * rows])
        halves = (
            (hot[:capacity], both[:capacity], out_mine, gate_mine, grad_mine, gate_grad_mine),
            (hot[capacity:], both[capacity:], out_other, gate_other, grad_other, gate_grad_other),
        )
        for hot_half, slot_grad, out, gate, grad_out, gate_out in halves:
            slot_gate = jnp.sum(hot_half * gate[owner], axis=1, keepdims=True)
            grad_out[places] = (slot_gate * slot_grad).astype(bf16)
            gate_grad = jnp.sum(slot_grad * out[places].astype(f32), axis=1, keepdims=True)
            gate_out[owner] = jnp.sum(hot_half * gate_grad, axis=0, keepdims=True)


def out_grads(grad, slots, out_mine, out_other, gate_mine, gate_other):
    members, both, rows = slots.shape
    width = grad.shape[1]
    slot_spec, slot_rows, token_rows, grid = slot_specs(slots, 2)
    line = pl.BlockSpec((2, 1, rows), lambda i: (i, 0, 0))
    grads = jax.ShapeDtypeStruct((members * both // 2, width), bf16)
    gates = jax.ShapeDtypeStruct((members, 1, rows), f32)
    return pl.pallas_call(
        out_grad_kernel,
        grid=grid,
        in_specs=[token_rows(width), slot_spec, slot_rows(width), slot_rows(width), line, line],
        out_specs=[slot_rows(width), slot_rows(width), line, line],
        out_shape=[grads, grads, gates, gates],
        compiler_params=pltpu.CompilerParams(vmem_limit_bytes=40 * 1024 * 1024),
        cost_estimate=small_cost,
        name="out_grads",
    )(
        grad,
        slots,
        out_mine,
        out_other,
        gate_mine.reshape(members, 1, rows),
        gate_other.reshape(members, 1, rows),
    )


def combine_back_kernel(grads, logit_grad, weights, router, slots, in_mine, in_other, *refs):
    out = refs[-1]
    rows = slots.shape[2]
    capacity = slots.shape[1] // 2
    total = dot_plain(grads[...], weights[...]) + dot_right_t(logit_grad[...], router[...])
    for owner in range(slots.shape[0]):
        tokens = slice(owner * rows, (owner + 1) * rows)
        places = slice(owner * capacity, (owner + 1) * capacity)
        arrived = jnp.concatenate([in_mine[places], in_other[places]], axis=0)
        out[tokens] = (total[tokens] + dot_left_t(slots[owner], arrived)).astype(bf16)


def combine_back(grads, logit_grad, weights, router, slots, in_mine, in_other, after):
    width = weights.shape[1]
    slot_spec, slot_rows, token_rows, grid = slot_specs(slots, 4)
    return pl.pallas_call(
        combine_back_kernel,
        grid=grid,
        in_specs=[
            token_rows(grads.shape[1]),
            token_rows(logit_grad.shape[1]),
            whole((grads.shape[1], width)),
            whole(router.shape),
            slot_spec,
            slot_rows(width),
            slot_rows(width),
        ]
        + unread(after),
        out_specs=token_rows(width),
        out_shape=jax.ShapeDtypeStruct((grads.shape[0], width), bf16),
        compiler_params=pltpu.CompilerParams(vmem_limit_bytes=50 * 1024 * 1024),
        cost_estimate=small_cost,
        name="combine_back",
    )(grads, logit_grad, weights, router, slots, in_mine, in_other, *after)


def latent_grad_kernel(kv_past, rope_past, kv_own, rope_own, expand, *refs):
    out = refs[-1]
    for index, (kv, rope) in enumerate(((kv_past, rope_past), (kv_own, rope_own))):
        out[index, :, :LATENT] = dot_right_t(kv[...], expand[...]).astype(bf16)
        out[index, :, LATENT:] = rope[...]


def latent_grads(kv_past, rope_past, kv_own, rope_own, expand, after):
    rows, cols = kv_past.shape
    rope_cols = rope_past.shape[1]
    block = QUERY_BLOCK
    kv_spec, rope_spec = by_rows(block, cols), by_rows(block, rope_cols)
    return pl.pallas_call(
        latent_grad_kernel,
        grid=(rows // block,),
        in_specs=[kv_spec, rope_spec, kv_spec, rope_spec, whole(expand.shape)] + unread(after),
        out_specs=pl.BlockSpec((2, block, LATENT + rope_cols), lambda i: (0, i, 0)),
        out_shape=jax.ShapeDtypeStruct((2, rows, LATENT + rope_cols), bf16),
        cost_estimate=small_cost,
        name="latent_grads",
    )(kv_past, rope_past, kv_own, rope_own, expand, *after)


def first_block_kernel(blocks, *refs):
    refs[-1][...] = blocks[0]


def first_block(blocks, after):
    shape = blocks.shape[1:]
    return pl.pallas_call(
        first_block_kernel,
        grid=(1,),
        in_specs=[lead(blocks, 0)] + unread(after),
        out_specs=whole(shape),
        out_shape=jax.ShapeDtypeStruct(shape, bf16),
        cost_estimate=small_cost,
        name="first_block",
    )(blocks, *after)


def latent_back_kernel(own, back, unit, factor, gain, cosine, sine, *refs):
    grad_out, gain_grad_out = refs[-2:]
    grad = own[...].astype(f32) + back[...].astype(f32)
    plain = grad[:, :LATENT]
    gain_grad_out[...] = jnp.sum(plain * unit[...], axis=0, keepdims=True)
    grad_out[:, :LATENT] = norm_back(plain, unit[...], factor[...], gain[...]).astype(bf16)
    grad_out[:, LATENT:] = turn_back(grad[:, LATENT:], cosine[...], sine[...]).astype(bf16)


def latent_back_rows(own, back, unit, factor, gain, cosine, sine, after):
    rows, cols = own.shape
    inputs = [own, back, unit, factor, gain[None], cosine, sine]
    return pl.pallas_call(
        latent_back_kernel,
        grid=(1,),
        in_specs=[whole(array.shape) for array in inputs] + unread(after),
        out_specs=[whole((rows, cols)), whole((1, LATENT))],
        out_shape=[
            jax.ShapeDtypeStruct((rows, cols), bf16),
            jax.ShapeDtypeStruct((1, LATENT), f32),
        ],
        cost_estimate=small_cost,
        name="latent_back",
    )(*inputs, *after)


def tokens_back_kernel(grad, projected, compress, unit, factor, gain, hidden_grad, *refs):
    out, gain_grad_out = refs[-2:]
    total = grad[...].astype(f32) + dot_plain(projected[...], compress[...])
    gain_grad_out[...] = jnp.sum(total * unit[...], axis=0, keepdims=True)
    out[...] = hidden_grad[...] + norm_back(total, unit[...], factor[...], gain[...])


def tokens_back(grad, projected, compress, unit, factor, gain, hidden_grad, after):
    rows, width = grad.shape
    inputs = [grad, projected, compress, unit, factor, gain[None], hidden_grad]
    return pl.pallas_call(
        tokens_back_kernel,
        grid=(1,),
        in_specs=[whole(array.shape) for array in inputs] + unread(after),
        out_specs=[whole((rows, width)), whole((1, width))],
        out_shape=[
            jax.ShapeDtypeStruct((rows, width), f32),
            jax.ShapeDtypeStruct((1, width), f32),
        ],
        compiler_params=pltpu.CompilerParams(vmem_limit_bytes=40 * 1024 * 1024),
        cost_estimate=small_cost,
        name="tokens_back",
    )(*inputs, *after)


def slice_grad_kernel(index, left, right, *refs):
    refs[-1][...] = dot_left_t(left[...], right[...])


def slice_grad(left, right, index, cols, after):
    rows = left.shape[0]
    return pl.pallas_call(
        slice_grad_kernel,
        grid_spec=pltpu.PrefetchScalarGridSpec(
            num_scalar_prefetch=1,
            grid=(1,),
            in_specs=[
                pl.BlockSpec(left.shape, lambda i, index: (0, 0)),
                pl.BlockSpec((rows, cols), lambda i, index: (0, index[0])),
            ]
            + unread(after),
            out_specs=pl.BlockSpec((left.shape[1], cols), lambda i, index: (0, 0)),
        ),
        out_shape=jax.ShapeDtypeStruct((left.shape[1], cols), f32),
        cost_estimate=small_cost,
        name="slice_grad",
    )(index.reshape(1), left, right, *after)


def place_kernel(turned, bits, own, arrived, other, *refs):
    out = refs[-1]

    @pl.when(pl.program_id(0) == 0)
    def first():
        total = flat(own) + flat(arrived)
        out[0] = total.T if turned else total

    @pl.when(pl.program_id(0) == 1)
    def second():
        total = flat(other)
        out[0] = total.T if turned else total


def place_experts(bit, parts, item, turned, after):
    own, arrived, other = parts
    arrived_item, other_item = arrived[item], other[item]
    shape = own.shape[:-3:-1] if turned else own.shape[-2:]
    return pl.pallas_call(
        functools.partial(place_kernel, turned),
        grid_spec=pltpu.PrefetchScalarGridSpec(
            num_scalar_prefetch=1,
            grid=(2,),
            in_specs=[lead(own, 0, item), lead(arrived_item), lead(other_item)]
            + unread(after),
            out_specs=pl.BlockSpec(
                (1,) + shape, lambda i, bits: (jnp.where(i == 0, bits[0], 1 - bits[0]), 0, 0)
            ),
        ),
        out_shape=jax.ShapeDtypeStruct((2,) + shape, f32),
        compiler_params=pltpu.CompilerParams(vmem_limit_bytes=40 * 1024 * 1024),
        cost_estimate=small_cost,
        name="place_experts",
    )(bit.reshape(1), own, arrived_item, other_item, *after)


def split_query_columns(weight):
    head = NOPE + ROPE
    half = ROPE // 2
    pieces = [weight[:, :NOPE], weight[:, head : head + NOPE]]
    for part in range(2):
        for index in range(2):
            first = index * head + NOPE + part * half
            pieces.append(weight[:, first : first + half])
    return jnp.concatenate(pieces, axis=1)


def join_query_columns(grad):
    half = ROPE // 2
    base = 2 * NOPE
    pieces = []
    for index in range(2):
        pieces.append(grad[:, index * NOPE : (index + 1) * NOPE])
        for part in range(2):
            first = base + part * ROPE + index * half
            pieces.append(grad[:, first : first + half])
    return jnp.concatenate(pieces, axis=1)


class Pairing:
    def __init__(self, groups, members):
        self.groups = groups
        self.members = members
        self.bits = groups.bit_length() - 1
        top = self.bits - 1
        self.partner = (1 << top, 1)
        self.others = (
            [1 << bit for bit in range(top)],
            [1 << (bit + 1) for bit in range(top)],
        )
        self.group = lax.axis_index("dp")
        self.odd = lax.axis_index("expert") % 2

    def chosen(self, masks):
        return jnp.where(self.odd == 1, masks[1], masks[0])

    def place(self, masks):
        return self.group ^ self.chosen(masks)

    def bit(self):
        return jnp.where(self.group & self.chosen(self.partner), 1, 0)

    def swap(self, value, masks):
        pairs = []
        for group in range(self.groups):
            for member in range(self.members):
                other = group ^ masks[member % 2]
                pairs.append((group * self.members + member, other * self.members + member))
        return lax.ppermute(value, ("dp", "expert"), pairs)

    def swap_partner(self, value):
        return self.swap(value, self.partner)

    def masks(self):
        masks = [(0, 0), self.partner]
        for step in zip(*self.others):
            masks = masks + [(even ^ step[0], odd ^ step[1]) for even, odd in masks]
        return masks

    def places(self):
        return jnp.stack([self.place(mask) for mask in self.masks()])

    def spread(self, held):
        for step in zip(*self.others):
            held = held + [self.swap(piece, step) for piece in held]
        return held

    def collect(self, kept, given):
        steps = list(reversed(list(zip(*self.others))))
        for number, step in enumerate(steps):
            arrived = [self.swap(piece, step) for piece in given]
            if number < len(steps) - 1:
                total = kept.astype(f32) + jnp.stack(arrived).reshape(kept.shape).astype(f32)
                total = total.astype(bf16)
                half = total.shape[0] // 2
                kept, given = total[:half], list(total[half:].reshape((-1,) + total.shape[2:]))
        return (kept, arrived)

    def exchange(self, kept, arrived):
        items = kept.shape[1]
        total = [
            (kept[1, item].astype(f32) + arrived[items + item].astype(f32)).astype(bf16)
            for item in range(items)
        ]
        return (kept, arrived, [self.swap_partner(piece) for piece in total])

    def gather_members(self, value):
        member = lax.axis_index("expert")
        rows = value.shape[0]
        chips = [value]
        for other in range(1, self.members // 2):
            pairs = [(i, i ^ (2 * other)) for i in range(self.members)]
            chips.append(lax.ppermute(value, "expert", pairs))
        both = lax.ppermute(
            jnp.concatenate(chips), "expert", [(i, i ^ 1) for i in range(self.members)]
        )
        held = []
        for number, block in enumerate(chips):
            held += [block, both[number * rows : (number + 1) * rows]]
        bit = 1
        while bit < self.members:
            flip = (member & bit) != 0
            held = [jnp.where(flip, held[i ^ bit], held[i]) for i in range(self.members)]
            bit *= 2
        return jnp.concatenate(held)

    def total(self, value):
        for bit in range(self.bits):
            arrived = self.swap(value.astype(bf16), (1 << bit, 1 << (self.bits - 1 - bit)))
            value = value + arrived.astype(f32)
        return value

    def total_all(self, value):
        size = self.groups * self.members
        for bit in range(size.bit_length() - 1):
            pairs = [(i, i ^ (1 << bit)) for i in range(size)]
            value = value + lax.ppermute(value, ("dp", "expert"), pairs)
        return value


def body(
    tokens,
    target,
    valid,
    routes,
    lengths,
    first_gain_vector,
    second_gain_vector,
    latent_gain_vector,
    latent_compress_weight,
    query_weight,
    latent_expand_weight,
    output_weight,
    router_weight,
    shared_gate_weight,
    shared_up_weight,
    shared_down_weight,
    expert_gate_weight,
    expert_up_weight,
    expert_down_weight,
):
    rows, width = tokens.shape
    members = lax.axis_size("expert")
    groups = lax.axis_size("dp")
    member = lax.axis_index("expert")
    group = lax.axis_index("dp")
    group_size = rows * members
    local_experts = expert_gate_weight.shape[0]
    route_count = routes.shape[1]
    expert_count = router_weight.shape[1]
    hidden_width = expert_gate_weight.shape[2]
    capacity = rows * route_count * 4 // (3 * local_experts * members)
    pairing = Pairing(groups, members)
    bit = pairing.bit()

    def pick(array, index):
        return lax.dynamic_index_in_dim(array, index, 0, False)

    tokens_float = tokens.astype(f32)
    own_unit, own_factor = normalize(tokens_float)
    own_normed = (own_unit * first_gain_vector).astype(bf16)
    normed = lax.all_gather(own_normed, "expert", axis=0, tiled=True)
    half = ROPE // 2
    compress_t = latent_compress_weight.T
    compress_t = jnp.concatenate(
        [compress_t[: LATENT + half]]
        + [compress_t[LATENT : LATENT + half]]
        + [compress_t[LATENT + half :]] * 2
    )
    index = group * group_size + jnp.arange(group_size, dtype=jnp.int32)
    seq_id = jnp.floor_divide(index, SEQ)
    place = index - seq_id * SEQ
    cosine, sine = angles(place, half)
    cosine = jnp.concatenate([cosine] * 4, axis=1)
    sine = jnp.concatenate([-sine, -sine, sine, sine], axis=1)
    own_cos = lax.dynamic_slice_in_dim(cosine, member * rows, rows, 0)
    own_sin = lax.dynamic_slice_in_dim(sine, member * rows, rows, 0)
    projected = dot_right_t(own_normed, compress_t)
    latent_unit, latent_factor = normalize(projected[:, :LATENT])
    turned = projected[:, LATENT:]
    turned = turned * own_cos + jnp.roll(turned, ROPE, axis=1) * own_sin
    latent = jnp.concatenate([latent_unit * latent_gain_vector, turned], axis=1).astype(bf16)
    before = lax.ppermute(latent, "dp", [(i, i + 1) for i in range(groups - 1)])
    before = first_block(before[None], [normed])
    previous = lax.all_gather(before, "expert", axis=0, tiled=True)

    places = pairing.places()
    given, kept = prepare(bit, expert_gate_weight, expert_up_weight, expert_down_weight)
    expert_w = pairing.spread([kept, pairing.swap_partner(given)])

    shared_hidden_width = shared_gate_weight.shape[1]
    padded = -(-shared_hidden_width // 128) * 128
    shared_w = jnp.concatenate(
        [
            jnp.pad(weight, ((0, padded - shared_hidden_width), (0, 0)))
            for weight in (shared_gate_weight.T, shared_up_weight.T, shared_down_weight)
        ]
    )

    counted = valid.astype(f32)
    count = pairing.total_all(jnp.full((8, 128), jnp.sum(counted)))[0, 0]

    bounds = lax.dynamic_slice_in_dim(
        jnp.cumsum(lengths, axis=1), group * group_size // SEQ, 1, 0
    )
    doc_start = jnp.max(jnp.where(bounds <= place[:, None], bounds, 0), axis=1)
    in_block = jnp.arange(group_size, dtype=jnp.int32) % QUERY_BLOCK
    low = jnp.maximum(doc_start - place + WINDOW + in_block, in_block + 1)[:, None]

    hot = jnp.any(routes[:, :, None] == jnp.arange(expert_count, dtype=jnp.int32), axis=1)
    routes_t = routes.T.reshape(route_count, members, rows)
    order = jnp.arange(rows, dtype=jnp.int32)
    earlier = (order[:, None] < order[None, :]).astype(bf16)
    mine = member * local_experts + bit
    other = member * local_experts + 1 - bit

    def slots_of(expert):
        hit = jnp.any(routes_t == expert, axis=0)
        rank = dot_plain(hit.astype(bf16), earlier).astype(jnp.int32)
        slot = jnp.arange(capacity, dtype=jnp.int32)[None, :, None]
        return (hit[:, None, :] & (rank[:, None, :] == slot)).astype(bf16)

    slots = jnp.concatenate([slots_of(mine), slots_of(other)], axis=1)

    query_w = split_query_columns(query_weight)
    kv, key_rope, group_latent = own_keys(
        normed,
        cosine,
        sine,
        latent_gain_vector,
        compress_t,
        latent_expand_weight,
        [shared_w, query_w],
    )
    kv, key_rope = past_keys(previous, latent_expand_weight, kv, key_rope)
    query, mixed, logs, attention_part = attend(
        normed,
        cosine,
        sine,
        low,
        query_w,
        kv,
        key_rope,
        output_weight,
        expert_w[1:2],
    )
    attention = lax.psum_scatter(attention_part, "expert", scatter_dimension=0, tiled=True)
    hidden, hidden_unit, hidden_factor, own_branch = norm(
        tokens, attention, second_gain_vector, expert_w[2:3]
    )
    branch = lax.all_gather(own_branch, "expert", axis=0, tiled=True)

    logits = jnp.where(hot, dot_plain(branch, router_weight), masked_value)
    top = jnp.max(logits, axis=1, keepdims=True)
    raised = jnp.where(hot, jnp.exp(logits - top), 0.0)
    gates = raised / jnp.sum(raised, axis=1, keepdims=True)
    experts = jnp.arange(expert_count, dtype=jnp.int32)[None, :]
    gate_mine = jnp.sum(jnp.where(experts == mine, gates, 0.0), axis=1, keepdims=True)
    gate_other = jnp.sum(jnp.where(experts == other, gates, 0.0), axis=1, keepdims=True)

    in_mine, in_other = dispatch(branch, slots, expert_w[3:])
    in_arrived = pairing.swap_partner(in_other)
    shared_act, shared_slope, shared_hidden = shared_forward(branch, shared_w)
    act_a, slope_a, inner_a, out_arrived = expert_call(
        expert_kernel, "expert", places, in_arrived, [], expert_w, 3, 2, [shared_hidden]
    )
    out_other = pairing.swap_partner(out_arrived)
    act_m, slope_m, inner_m, out_mine = expert_call(
        expert_kernel, "expert", places, in_mine, [], expert_w, 3, 2, [out_arrived]
    )
    branch_part = combine(
        shared_hidden, shared_w, slots, out_mine, out_other, gate_mine, gate_other
    )
    branch_sum = lax.psum_scatter(branch_part, "expert", scatter_dimension=0, tiled=True)
    result = hidden + branch_sum.astype(f32)
    difference = result - target.astype(f32)
    squares = jnp.sum(counted[:, None] * difference * difference)
    total_tokens = rows * members * groups
    grad_out = total_tokens / count * counted[:, None] * difference

    grad_low = lax.all_gather(grad_out.astype(bf16), "expert", axis=0, tiled=True)

    out_grad_mine, out_grad_other, gate_grad_mine, gate_grad_other = out_grads(
        grad_low, slots, out_mine, out_other, gate_mine, gate_other
    )
    out_grad_arrived = pairing.swap_partner(out_grad_other)
    shared_grad = shared_back(grad_low, shared_w, shared_act, shared_slope, [out_grad_mine])
    gate_gm, up_gm, in_grad_mine = expert_call(
        expert_back_kernel,
        "expert_back",
        places,
        out_grad_mine,
        [act_m, slope_m],
        expert_w,
        2,
        1,
        [shared_grad],
    )
    gate_ga, up_ga, in_grad_arrived = expert_call(
        expert_back_kernel,
        "expert_back",
        places,
        out_grad_arrived,
        [act_a, slope_a],
        expert_w,
        2,
        1,
        [in_grad_mine],
    )
    in_grad_other = pairing.swap_partner(in_grad_arrived)

    down_kept, down_given = weight_grads(
        "down_grad",
        places,
        [[[(out_grad_mine, inner_m), (out_grad_arrived, inner_a)]]],
        [in_grad_arrived],
    )

    gate_grads = jnp.where(experts == mine, gate_grad_mine.reshape(-1, 1), 0.0) + jnp.where(
        experts == other, gate_grad_other.reshape(-1, 1), 0.0
    )
    logit_grad = gates * (gate_grads - jnp.sum(gates * gate_grads, axis=1, keepdims=True))
    logit_grad = logit_grad.astype(bf16)
    grad_router = dot_left_t(branch, logit_grad)
    branch_grad_part = combine_back(
        shared_grad,
        logit_grad,
        shared_w,
        router_weight,
        slots,
        in_grad_mine,
        in_grad_other,
        [down_kept],
    )
    branch_grad = lax.psum_scatter(
        branch_grad_part, "expert", scatter_dimension=0, tiled=True
    )

    gate_up_kept, gate_up_given = weight_grads(
        "gate_up_grad",
        places,
        [
            [[(in_mine, gate_gm), (in_arrived, gate_ga)]],
            [[(in_mine, up_gm), (in_arrived, up_ga)]],
        ],
        [branch_grad_part],
    )
    down_terms = pairing.collect(down_kept, down_given)
    gate_up_terms = pairing.collect(gate_up_kept, gate_up_given)
    shared_kept, shared_given = weight_grads(
        "shared_grads",
        places,
        [[[(branch, shared_grad)], [(grad_low, shared_hidden)]]],
        [gate_up_kept],
    )
    shared_terms = pairing.collect(shared_kept, shared_given)
    down_parts = pairing.exchange(*down_terms)
    gate_up_parts = pairing.exchange(*gate_up_terms)

    grad_hidden_own, grad_hidden_low, grad_norm2 = norm_back_rows(
        branch_grad,
        grad_out,
        hidden_unit,
        hidden_factor,
        second_gain_vector,
        down_terms[1] + gate_up_terms[1][:1] + [shared_kept],
    )
    grad_attention = lax.all_gather(grad_hidden_low, "expert", axis=0, tiled=True)
    query_grad, normed_grad_part, kv_past, rope_past, kv_own, rope_own = attend_back(
        grad_attention,
        query,
        logs,
        cosine,
        sine,
        low,
        query_w,
        kv,
        key_rope,
        output_weight,
        gate_up_terms[1],
    )

    latent_grad = lax.psum_scatter(
        latent_grads(
            kv_past, rope_past, kv_own, rope_own, latent_expand_weight, shared_terms[1]
        ),
        "expert",
        scatter_dimension=1,
        tiled=True,
    )
    normed_grad = lax.psum_scatter(
        normed_grad_part, "expert", scatter_dimension=0, tiled=True
    )

    attention_kept, attention_given = weight_grads(
        "attention_grads",
        places,
        [[[(normed, query_grad)], [(grad_attention, mixed)]]],
        [kv_own],
    )
    attention_terms = pairing.collect(attention_kept, attention_given)
    expand_grad = (
        dot_left_t(previous[:, :LATENT], kv_past) + dot_left_t(group_latent, kv_own)
    ).astype(bf16)
    expand_grad = expand_grad.reshape(groups, -1, expand_grad.shape[1])
    expand_pieces = jnp.stack([pick(expand_grad, places[i]) for i in range(groups)])[:, None]
    expand_parts = pairing.exchange(
        *pairing.collect(
            expand_pieces[: groups // 2], list(expand_pieces[groups // 2 :].squeeze(1))
        )
    )
    back = lax.ppermute(
        first_block(latent_grad, [attention_kept] + down_parts[2] + gate_up_parts[2][:1]),
        "dp",
        [(i + 1, i) for i in range(groups - 1)],
    )

    grad_projected, grad_latent_gain = latent_back_rows(
        latent_grad[1],
        back,
        latent_unit,
        latent_factor,
        latent_gain_vector,
        own_cos,
        own_sin,
        [],
    )
    group_grad = pairing.gather_members(grad_projected)
    expert_down_gradient = place_experts(bit, down_parts, 0, True, [grad_projected])
    expert_gate_gradient = place_experts(bit, gate_up_parts, 0, False, [grad_projected])
    expert_up_gradient = place_experts(bit, gate_up_parts, 1, False, [grad_projected])
    shared_parts = pairing.exchange(*shared_terms)
    attention_parts = pairing.exchange(*attention_terms)
    slice_cols = width // members
    compress_slice = slice_grad(
        group_grad,
        normed,
        member,
        slice_cols,
        [expert_down_gradient, expert_gate_gradient, expert_up_gradient]
        + attention_terms[1],
    )
    compress_slice = pairing.total(
        jnp.concatenate(
            [
                compress_slice[:LATENT],
                compress_slice[LATENT : LATENT + half] + compress_slice[LATENT + half : LATENT + ROPE],
                compress_slice[LATENT + ROPE : LATENT + ROPE + half]
                + compress_slice[LATENT + ROPE + half :],
            ]
        )
    ).astype(bf16)
    grad_kva = (
        lax.all_gather(compress_slice, "expert", axis=0, tiled=True)
        .reshape(members, -1, slice_cols)
        .transpose(0, 2, 1)
        .reshape(width, -1)
        .astype(f32)
    )
    grad_tokens, grad_norm1 = tokens_back(
        normed_grad,
        grad_projected,
        compress_t,
        own_unit,
        own_factor,
        first_gain_vector,
        grad_hidden_own,
        [compress_slice],
    )
    sums = [grad_router.reshape(-1), grad_norm2[0], grad_norm1[0], grad_latent_gain[0]]
    cuts = [sum(part.size for part in sums[:number]) for number in range(1, len(sums) + 1)]
    sums = pairing.total_all(
        jnp.concatenate(sums + [jnp.full((8 * 128,), squares)]).reshape(-1, 128)
    ).reshape(-1)
    grad_router = sums[: cuts[0]].reshape(grad_router.shape)
    grad_norm2, grad_norm1 = sums[cuts[0] : cuts[1]], sums[cuts[1] : cuts[2]]
    grad_latent_gain, squares = sums[cuts[2] : cuts[3]], sums[-1]

    query_cols, mixed_cols = query_w.shape[1], mixed.shape[1]
    shared_gate_gradient, shared_up_gradient, shared_down_gradient = finish(
        "shared_finish",
        shared_parts,
        [(i * padded, (i + 1) * padded, True) for i in range(3)],
        [shared_hidden_width] * 3,
        [compress_slice],
    )
    query_weight_gradient, output_weight_gradient = finish(
        "attention_finish",
        attention_parts,
        [(0, query_cols, False), (query_cols, query_cols + mixed_cols, True)],
        [0, mixed_cols],
        [compress_slice],
    )
    shared_gate_gradient, shared_up_gradient = shared_gate_gradient.T, shared_up_gradient.T
    query_weight_gradient = join_query_columns(query_weight_gradient)
    (latent_expand_gradient,) = finish(
        "expand_finish",
        expand_parts,
        [(0, expand_grad.shape[2], False)],
        [0],
        [compress_slice],
    )
    return (
        result.astype(bf16),
        squares / (count * width),
        grad_tokens,
        grad_norm1,
        grad_norm2,
        grad_latent_gain,
        grad_kva,
        query_weight_gradient,
        latent_expand_gradient,
        output_weight_gradient,
        grad_router,
        shared_gate_gradient,
        shared_up_gradient,
        shared_down_gradient,
        expert_gate_gradient,
        expert_up_gradient,
        expert_down_gradient,
    )


def solution(mesh):
    placed = (
        P(("dp", "expert"), None),
        P(("dp", "expert"), None),
        P(("dp", "expert")),
        P("dp", None),
        P(),
        P(),
        P(),
        P(),
        P(),
        P(None, "expert"),
        P(None, "expert"),
        P("expert", None),
        P(),
        P(None, "expert"),
        P(None, "expert"),
        P("expert", None),
        P("expert", "dp", None),
        P("expert", "dp", None),
        P("expert", None, "dp"),
    )
    return jax.shard_map(
        body,
        mesh=mesh,
        in_specs=placed,
        out_specs=(
            P(("dp", "expert"), None),
            P(),
            P(("dp", "expert"), None),
            P(),
            P(),
            P(),
            P(),
            P("dp", "expert"),
            P("dp", "expert"),
            P("expert", "dp"),
            P(),
            P("dp", "expert"),
            P("dp", "expert"),
            P("expert", "dp"),
            P("expert", "dp", None),
            P("expert", "dp", None),
            P("expert", None, "dp"),
        ),
        check_vma=False,
    )
```

```python
import functools

import jax
import jax.numpy as jnp
from jax import lax
from jax.experimental import pallas as pl
from jax.experimental.pallas import tpu as pltpu
from jax.sharding import PartitionSpec as P

NOPE = 128
ROPE = 64
VDIM = 128
LATENT = 512
SEQ = 4096
WINDOW = 1024
QUERY_BLOCK = 256

epsilon = 1e-06
masked_value = -1e30
score_scale = (NOPE + ROPE) ** (-0.5)
bf16 = jnp.bfloat16
f32 = jnp.float32
whole_vmem = pltpu.CompilerParams(vmem_limit_bytes=60 * 1024 * 1024)
small_cost = pl.CostEstimate(flops=1, bytes_accessed=1, transcendentals=0)


def dot_plain(left, right):
    return lax.dot_general(left, right, (((1,), (0,)), ((), ())), preferred_element_type=f32)


def dot_right_t(left, right):
    return lax.dot_general(left, right, (((1,), (1,)), ((), ())), preferred_element_type=f32)


def dot_left_t(left, right):
    return lax.dot_general(left, right, (((0,), (0,)), ((), ())), preferred_element_type=f32)


def normalize(values):
    factor = lax.rsqrt(jnp.mean(values * values, axis=-1, keepdims=True) + epsilon)
    return (values * factor, factor)


def norm_back(grad_out, unit, factor, gain):
    grad_unit = grad_out * gain
    return factor * (grad_unit - unit * jnp.mean(grad_unit * unit, axis=-1, keepdims=True))


def angles(place, half):
    freq = jnp.exp(-jnp.log(10000.0) * jnp.arange(half, dtype=f32) / half)
    angle = place.astype(f32)[:, None] * freq[None, :]
    return (jnp.cos(angle), jnp.sin(angle))


def silu_parts(values):
    sigma = jax.nn.sigmoid(values)
    return (values * sigma, sigma * (1.0 + values * (1.0 - sigma)))


def head_lanes(block, head):
    lane = lax.broadcasted_iota(jnp.int32, (block, 2 * ROPE), 1)
    return (lane // (ROPE // 2)) % 2 == head


def allowed_keys(low, block, span):
    row = lax.broadcasted_iota(jnp.int32, (block, span), 0)
    col = lax.broadcasted_iota(jnp.int32, (block, span), 1)
    return (col <= row + WINDOW) & (col >= low[:, :1])


def head_parts(query, lanes, keys, head):
    turned = jnp.where(lanes, query[:, 2 * NOPE :], 0)
    query_head = jnp.concatenate([query[:, head * NOPE : (head + 1) * NOPE], turned], axis=1)
    base = head * (NOPE + VDIM)
    rope = keys[:, 2 * (NOPE + VDIM) :]
    key_head = jnp.concatenate([keys[:, base : base + NOPE], rope], axis=1)
    return (query_head, key_head, keys[:, base + NOPE : base + NOPE + VDIM])


def attend_kernel(chunks, query_in, low, out_w, *refs):
    mixed_out, log_out, part_out = refs[-3:]
    keys = window_keys(refs, chunks)
    block = query_in.shape[0]
    query = query_in[...]
    mask = allowed_keys(low[...], block, WINDOW + block)
    mixed, logs = [], []
    for head in range(2):
        query_head, key_head, value_head = head_parts(query, head_lanes(block, head), keys, head)
        scores = jnp.where(mask, dot_right_t(query_head, key_head) * score_scale, masked_value)
        top = jnp.max(scores, axis=1, keepdims=True)
        raised = jnp.exp(scores - top)
        total = jnp.sum(raised, axis=1, keepdims=True)
        probs = (raised * (1.0 / total)).astype(bf16)
        mixed.append(dot_plain(probs, value_head))
        logs.append(top + jnp.log(total))
    lane = lax.broadcasted_iota(jnp.int32, (block, 128), 1)
    log_out[...] = jnp.where(lane == 0, logs[0], logs[1])
    mixed = jnp.concatenate(mixed, axis=1).astype(bf16)
    mixed_out[...] = mixed
    part_out[...] = dot_plain(mixed, out_w[...]).astype(bf16)


def by_rows(block, cols, offset=0):
    return pl.BlockSpec((block, cols), lambda i: (i + offset, 0))


def whole(shape):
    return pl.BlockSpec(shape, lambda i: (0, 0))


def unread(arrays):
    return [pl.BlockSpec(memory_space=pl.ANY) for _ in arrays]


def turn(values, cosine, sine):
    return values * cosine + pltpu.roll(values, ROPE, 1) * sine


def turn_back(values, cosine, sine):
    return values * cosine - pltpu.roll(values, ROPE, 1) * sine


def own_keys_kernel(normed, cosine, sine, gain, compress, expand, *refs):
    keys, latent = refs[-2:]
    projected = dot_right_t(normed[...], compress[...])
    unit, _ = normalize(projected[:, :LATENT])
    low = (unit * gain[...]).astype(bf16)
    latent[...] = low
    kv_cols = expand.shape[1]
    keys[:, :kv_cols] = dot_plain(low, expand[...]).astype(bf16)
    keys[:, kv_cols:] = turn(projected[:, LATENT:], cosine[...], sine[...]).astype(bf16)


def own_keys(normed, cosine, sine, gain, compress, expand, after):
    rows, width = normed.shape
    block = QUERY_BLOCK
    rope_cols = 2 * ROPE
    key_cols = expand.shape[1] + rope_cols
    return pl.pallas_call(
        own_keys_kernel,
        grid=(rows // block,),
        in_specs=[
            by_rows(block, width),
            by_rows(block, rope_cols),
            by_rows(block, rope_cols),
            whole((1, LATENT)),
            whole(compress.shape),
            whole(expand.shape),
        ]
        + unread(after),
        out_specs=[by_rows(block, key_cols), by_rows(block, LATENT)],
        out_shape=[
            jax.ShapeDtypeStruct((rows, key_cols), bf16),
            jax.ShapeDtypeStruct((rows, LATENT), bf16),
        ],
        compiler_params=whole_vmem,
        cost_estimate=small_cost,
        name="own_keys",
    )(normed, cosine, sine, gain[None], compress, expand, *after)


def key_blocks(keys, past, block, chunks):
    cols = keys.shape[1]
    blocks = past.shape[0] // block
    specs, operands = [], []
    for chunk in range(chunks):
        if chunk < chunks - 1:
            specs.append(
                pl.BlockSpec((block, cols), lambda i, c=chunk: (jnp.minimum(i + c, blocks - 1), 0))
            )
            operands.append(past)
        if chunk > 0:
            specs.append(
                pl.BlockSpec((block, cols), lambda i, c=chunk: (jnp.maximum(i + c - blocks, 0), 0))
            )
            operands.append(keys)
    return specs, operands


def window_keys(refs, chunks):
    step = pl.program_id(0)
    parts = [refs[0][...]]
    for chunk in range(1, chunks - 1):
        past, own = refs[2 * chunk - 1], refs[2 * chunk]
        parts.append(jnp.where(step + chunk < chunks - 1, past[...], own[...]))
    parts.append(refs[2 * chunks - 3][...])
    return jnp.concatenate(parts, axis=0)


def attend(query, low, keys, past, out_w, after):
    rows, query_cols = query.shape
    width = out_w.shape[1]
    block = QUERY_BLOCK
    chunks = 1 + WINDOW // block
    rows_of = functools.partial(by_rows, block)
    key_specs, key_operands = key_blocks(keys, past, block, chunks)
    return pl.pallas_call(
        functools.partial(attend_kernel, chunks),
        grid=(rows // block,),
        in_specs=[
            rows_of(query_cols),
            rows_of(low.shape[1]),
            whole(out_w.shape),
        ]
        + key_specs
        + unread(after),
        out_specs=[rows_of(2 * VDIM), rows_of(128), rows_of(width)],
        out_shape=[
            jax.ShapeDtypeStruct((rows, 2 * VDIM), bf16),
            jax.ShapeDtypeStruct((rows, 128), f32),
            jax.ShapeDtypeStruct((rows, width), bf16),
        ],
        compiler_params=whole_vmem,
        cost_estimate=small_cost,
        name="attend",
    )(query, low, out_w, *key_operands, *after)


def query_kernel(normed, cosine, sine, query_w, out):
    proj = dot_plain(normed[...], query_w[...])
    out[:, : 2 * NOPE] = proj[:, : 2 * NOPE].astype(bf16)
    out[:, 2 * NOPE :] = turn(proj[:, 2 * NOPE :], cosine[...], sine[...]).astype(bf16)


def project_query(normed, cosine, sine, query_w):
    rows, width = normed.shape
    block = QUERY_BLOCK
    cols = query_w.shape[1]
    return pl.pallas_call(
        query_kernel,
        grid=(rows // block,),
        in_specs=[
            by_rows(block, width),
            by_rows(block, 2 * ROPE),
            by_rows(block, 2 * ROPE),
            whole(query_w.shape),
        ],
        out_specs=by_rows(block, cols),
        out_shape=jax.ShapeDtypeStruct((rows, cols), bf16),
        compiler_params=whole_vmem,
        cost_estimate=small_cost,
        name="project_query",
    )(normed, cosine, sine, query_w)


def attend_back_kernel(
    chunks, grad, query_in, logs, cosine, sine, low, query_w, out_w, *refs
):
    keys = window_keys(refs, chunks)
    query_grad_out, part_out, kv_past, rope_past, kv_own, rope_own, kv_sum, rope_sum = refs[-8:]
    block = grad.shape[0]

    @pl.when(pl.program_id(0) == 0)
    def clear():
        kv_sum[...] = jnp.zeros_like(kv_sum)
        rope_sum[...] = jnp.zeros_like(rope_sum)

    def add(total, past, cols, piece):
        for chunk in range(chunks):
            part = piece[chunk * block : (chunk + 1) * block]
            if chunk < chunks - 1:
                part = part + total[chunk * block : (chunk + 1) * block, cols]
            if chunk == 0:
                past[:, cols] = part.astype(past.dtype)
            else:
                total[(chunk - 1) * block : chunk * block, cols] = part

    mixed_grad = dot_right_t(grad[...], out_w[...]).astype(bf16)
    mask = allowed_keys(low[...], block, WINDOW + block)
    query = query_in[...]
    plain, turned, rope_piece = [], 0.0, 0.0
    for head in range(2):
        lanes = head_lanes(block, head)
        query_head, key_head, value_head = head_parts(query, lanes, keys, head)
        base = head * (NOPE + VDIM)
        grad_head = mixed_grad[:, head * VDIM : (head + 1) * VDIM]
        scores = jnp.where(mask, dot_right_t(query_head, key_head) * score_scale, masked_value)
        probs = jnp.exp(scores - logs[:, head : head + 1])
        prob_grad = dot_right_t(grad_head, value_head)
        shift = jnp.sum(probs * prob_grad, axis=1, keepdims=True)
        score_grad = (probs * (prob_grad - shift)).astype(bf16)
        key_piece = dot_left_t(score_grad, query_head) * score_scale
        add(kv_sum, kv_past, slice(base, base + NOPE), key_piece[:, :NOPE])
        value_piece = dot_left_t(probs.astype(bf16), grad_head)
        add(kv_sum, kv_past, slice(base + NOPE, base + NOPE + VDIM), value_piece)
        rope_piece = rope_piece + key_piece[:, NOPE:]
        query_piece = dot_plain(score_grad, key_head) * score_scale
        plain.append(query_piece[:, :NOPE])
        turned = turned + jnp.where(lanes, query_piece[:, NOPE:], 0.0)
    add(rope_sum, rope_past, slice(0, 2 * ROPE), rope_piece)
    turned = turn_back(turned, cosine[...], sine[...])
    query_grad = jnp.concatenate(plain + [turned], axis=1).astype(bf16)
    query_grad_out[...] = query_grad
    part_out[...] = dot_right_t(query_grad, query_w[...]).astype(bf16)

    @pl.when(pl.program_id(0) == pl.num_programs(0) - 1)
    def finish():
        kv_own[...] = kv_sum[...].astype(bf16)
        rope_own[...] = rope_sum[...].astype(bf16)


def attend_back(grad, query, logs, cosine, sine, low, query_w, keys, past, out_w, after):
    rows, width = grad.shape
    block = QUERY_BLOCK
    chunks = 1 + WINDOW // block
    query_cols = query_w.shape[1]
    rows_of = functools.partial(by_rows, block)
    rope_cols = 2 * ROPE
    kv_cols = keys.shape[1] - rope_cols
    key_specs, key_operands = key_blocks(keys, past, block, chunks)
    return pl.pallas_call(
        functools.partial(attend_back_kernel, chunks),
        grid=(rows // block,),
        in_specs=[
            rows_of(width),
            rows_of(query_cols),
            rows_of(128),
            rows_of(2 * ROPE),
            rows_of(2 * ROPE),
            rows_of(low.shape[1]),
            whole(query_w.shape),
            whole(out_w.shape),
        ]
        + key_specs
        + unread(after),
        out_specs=[
            rows_of(query_cols),
            rows_of(width),
            rows_of(kv_cols),
            rows_of(rope_cols),
            whole((WINDOW, kv_cols)),
            whole((WINDOW, rope_cols)),
        ],
        out_shape=[
            jax.ShapeDtypeStruct((rows, query_cols), bf16),
            jax.ShapeDtypeStruct((rows, width), bf16),
            jax.ShapeDtypeStruct((rows, kv_cols), bf16),
            jax.ShapeDtypeStruct((rows, rope_cols), bf16),
            jax.ShapeDtypeStruct((WINDOW, kv_cols), bf16),
            jax.ShapeDtypeStruct((WINDOW, rope_cols), bf16),
        ],
        scratch_shapes=[pltpu.VMEM((WINDOW, kv_cols), f32), pltpu.VMEM((WINDOW, rope_cols), f32)],
        compiler_params=whole_vmem,
        cost_estimate=small_cost,
        name="attend_back",
    )(
        grad,
        query,
        logs,
        cosine,
        sine,
        low,
        query_w,
        out_w,
        *key_operands,
        *after,
    )


def norm_kernel(tokens, attention, gain, *refs):
    hidden_out, unit_out, factor_out, branch_out = refs[-4:]
    hidden = tokens[...].astype(f32) + attention[...].astype(f32)
    unit, factor = normalize(hidden)
    hidden_out[...] = hidden
    unit_out[...] = unit
    factor_out[...] = factor
    branch_out[...] = (unit * gain[...]).astype(bf16)


def norm(tokens, attention, gain, after):
    rows, width = tokens.shape
    full = whole((rows, width))
    return pl.pallas_call(
        norm_kernel,
        grid=(1,),
        in_specs=[full, full, whole((1, width))] + unread(after),
        out_specs=[full, full, whole((rows, 1)), full],
        out_shape=[
            jax.ShapeDtypeStruct((rows, width), f32),
            jax.ShapeDtypeStruct((rows, width), f32),
            jax.ShapeDtypeStruct((rows, 1), f32),
            jax.ShapeDtypeStruct((rows, width), bf16),
        ],
        cost_estimate=small_cost,
        compiler_params=whole_vmem,
        name="norm",
    )(tokens, attention, gain[None], *after)


def norm_back_kernel(branch_grad, grad_out, unit, factor, gain, *refs):
    hidden_grad_out, low_out, gain_grad_out = refs[-3:]
    grad = branch_grad[...].astype(f32)
    hidden_grad = grad_out[...] + norm_back(grad, unit[...], factor[...], gain[...])
    hidden_grad_out[...] = hidden_grad
    low_out[...] = hidden_grad.astype(bf16)
    gain_grad_out[...] = jnp.sum(grad * unit[...], axis=0, keepdims=True)


def norm_back_rows(branch_grad, grad_out, unit, factor, gain, after):
    rows, width = unit.shape
    full, line = whole((rows, width)), whole((1, width))
    return pl.pallas_call(
        norm_back_kernel,
        grid=(1,),
        in_specs=[full, full, full, whole((rows, 1)), line] + unread(after),
        out_specs=[full, full, line],
        out_shape=[
            jax.ShapeDtypeStruct((rows, width), f32),
            jax.ShapeDtypeStruct((rows, width), bf16),
            jax.ShapeDtypeStruct((1, width), f32),
        ],
        cost_estimate=small_cost,
        compiler_params=whole_vmem,
        name="norm_back",
    )(branch_grad, grad_out, unit, factor, gain[None], *after)


def column_tiles(hidden):
    return [(first, min(first + 512, hidden)) for first in range(0, hidden, 512)]


class Copies:
    def __init__(self, semaphores):
        self.semaphores = semaphores
        self.groups = {}
        self.used = 0

    def start(self, group, source, target):
        copy = pltpu.make_async_copy(source, target, self.semaphores.at[self.used])
        self.used += 1
        copy.start()
        self.groups.setdefault(group, []).append(copy)

    def wait(self, group):
        for copy in self.groups.pop(group):
            copy.wait()


def merged(ref, cols):
    value = ref[:, :, cols]
    return value.reshape(-1, value.shape[-1])


def expert_kernel(count, extra, row, places, slot_in, *refs):
    weights = refs[:count]
    outs = refs[count + extra : count + extra + 4]
    act_s, slope_s, inner_s, result, gate_w, up_w, down_w, semaphores = refs[count + extra + 4 :]
    depth, hidden = gate_w.shape[1:]
    rows = pl.ds(row, slot_in.shape[0])
    copies = Copies(semaphores)
    for first, last in column_tiles(hidden):
        cols = slice(first, last)
        for index, weight in enumerate(weights):
            place = places[index]
            copies.start(first, weight.at[0, :, cols], gate_w.at[place, :, cols])
            copies.start(first, weight.at[1, :, cols], up_w.at[place, :, cols])
    for index, weight in enumerate(weights):
        copies.start("down", weight.at[2], down_w.at[places[index]])
    for first, last in column_tiles(hidden):
        cols = slice(first, last)
        copies.wait(first)
        gate = dot_plain(slot_in[...], merged(gate_w, cols))
        up = dot_plain(slot_in[...], merged(up_w, cols))
        act, slope = silu_parts(gate)
        act_s[:, cols] = act.astype(bf16)
        slope_s[:, cols] = (up * slope).astype(bf16)
        inner_s[:, cols] = (act * up).astype(bf16)
        for source, target in zip((act_s, slope_s, inner_s), outs):
            copies.start("out", source.at[:, cols], target.at[rows, cols])
    copies.wait("down")
    for index in range(count):
        cols = slice(index * depth, (index + 1) * depth)
        result[:, cols] = dot_right_t(inner_s[...], down_w[index]).astype(bf16)
        copies.start("out", result.at[:, cols], outs[3].at[:, cols])
    copies.wait("out")


def expert_back_kernel(count, extra, row, places, out_grad, act, slope, *refs):
    weights = refs[:count]
    outs = refs[count + extra : count + extra + 3]
    gate_s, up_s, result, gate_w, up_w, down_w, semaphores = refs[count + extra + 3 :]
    depth, hidden = gate_w.shape[1:]
    copies = Copies(semaphores)
    for first, last in column_tiles(hidden):
        cols = slice(first, last)
        for index, weight in enumerate(weights):
            copies.start(first, weight.at[2, :, cols], down_w.at[places[index], :, cols])
    for index, weight in enumerate(weights):
        copies.start("back", weight.at[0], gate_w.at[places[index]])
        copies.start("back", weight.at[1], up_w.at[places[index]])
    for first, last in column_tiles(hidden):
        cols = slice(first, last)
        copies.wait(first)
        inner = dot_plain(out_grad[...], merged(down_w, cols))
        gate_s[:, cols] = (inner * slope[:, cols].astype(f32)).astype(bf16)
        up_s[:, cols] = (inner * act[:, cols].astype(f32)).astype(bf16)
        for source, target in zip((gate_s, up_s), outs):
            copies.start("out", source.at[:, cols], target.at[:, cols])
    copies.wait("back")
    for index in range(count):
        cols = slice(index * depth, (index + 1) * depth)
        result[:, cols] = (
            dot_right_t(gate_s[...], gate_w[index]) + dot_right_t(up_s[...], up_w[index])
        ).astype(bf16)
        copies.start("out", result.at[:, cols], outs[2].at[:, cols])
    copies.wait("out")


def expert_call(kernel, name, places, slots, fixed, weights, outputs, after, row=0, total=0, held=()):
    count = len(weights)
    rows, width = slots.shape
    _, depth, hidden = weights[0].shape
    inputs = [slots] + fixed
    tiles = len(column_tiles(hidden))
    weight_s = pltpu.VMEM((count, depth, hidden), bf16)
    scratch = [(rows, hidden)] * outputs + [(rows, width)]
    shapes = [(total or rows, hidden)] * outputs + [(rows, width)]
    first_held = 1 + len(inputs) + count + len(after)
    return pl.pallas_call(
        functools.partial(kernel, count, len(after) + len(held), row),
        grid_spec=pltpu.PrefetchScalarGridSpec(
            num_scalar_prefetch=1,
            grid=(1,),
            in_specs=[pl.BlockSpec(array.shape, lambda i, places: (0, 0)) for array in inputs]
            + unread(weights)
            + unread(after)
            + unread(held),
            out_specs=unread(shapes),
            scratch_shapes=[pltpu.VMEM(shape, bf16) for shape in scratch]
            + [weight_s] * 3
            + [pltpu.SemaphoreType.DMA((count * (2 * tiles + 3) + 3 * tiles,))],
        ),
        out_shape=[jax.ShapeDtypeStruct(shape, bf16) for shape in shapes],
        input_output_aliases={first_held + index: index for index in range(len(held))},
        compiler_params=whole_vmem,
        cost_estimate=small_cost,
        name=name,
    )(places, *inputs, *weights, *after, *held)


def weight_grad_kernel(count, plan, places, *refs):
    half = count // 2
    outs = refs[-1 - half * len(plan) :]
    step = pl.program_id(0)
    for number, segments in enumerate(plan):
        first = 0
        for terms in segments:
            grad = 0.0
            for left, right, row in terms:
                rows = slice(row, row + refs[left].shape[0])
                grad = grad + dot_left_t(refs[left][...], refs[right][rows])
            last = first + grad.shape[1]
            for index in range(count):

                @pl.when(step == index)
                def store(index=index, number=number, cols=slice(first, last), grad=grad):
                    if index < half:
                        outs[0][index, number, :, cols] = grad.astype(bf16)
                    else:
                        out = outs[1 + (index - half) * len(plan) + number]
                        out[:, cols] = grad.astype(bf16)

            first = last


def weight_grads(name, places, outputs, after=()):
    count = places.shape[0]
    lefts, rights = [], []

    def number_of(array, held):
        for number, other in enumerate(held):
            if array is other:
                return number
        held.append(array)
        return len(held) - 1

    plan, flops = [], 0
    for segments in outputs:
        planned, columns = [], 0
        for terms in segments:
            numbers = []
            for blocks, right in terms:
                row = 0
                for left in blocks if isinstance(blocks, list) else [blocks]:
                    numbers.append((number_of(left, lefts), number_of(right, rights), row))
                    row += left.shape[0]
                flops += 2 * row * left.shape[1] * right.shape[1]
            planned.append(numbers)
            columns += terms[0][1].shape[1]
        plan.append(planned)
    plan = [
        [[(left, len(lefts) + right, row) for left, right, row in numbers] for numbers in planned]
        for planned in plan
    ]
    piece = (lefts[0].shape[1] // count, columns)
    shapes = [(count // 2, len(outputs)) + piece] + [piece] * (count // 2 * len(outputs))
    kept, *given = pl.pallas_call(
        functools.partial(weight_grad_kernel, count, plan),
        grid_spec=pltpu.PrefetchScalarGridSpec(
            num_scalar_prefetch=1,
            grid=(count,),
            in_specs=[
                pl.BlockSpec((left.shape[0], left.shape[1] // count), lambda i, places: (0, places[i]))
                for left in lefts
            ]
            + [pl.BlockSpec(right.shape, lambda i, places: (0, 0)) for right in rights]
            + unread(after),
            out_specs=[pl.BlockSpec(shapes[0], lambda i, places: (0, 0, 0, 0))]
            + [pl.BlockSpec(shape, lambda i, places: (0, 0)) for shape in shapes[1:]],
        ),
        out_shape=[jax.ShapeDtypeStruct(shape, bf16) for shape in shapes],
        compiler_params=whole_vmem,
        cost_estimate=small_cost,
        name=name,
    )(places, *lefts, *rights, *after)
    return kept, given


def lead(array, *indices):
    shape = (1,) * len(indices) + array.shape[-2:]
    return pl.BlockSpec(shape, lambda i, *prefetched: indices + (0, 0))


def flat(ref):
    for _ in ref.shape[2:]:
        ref = ref.at[0]
    return ref[...].astype(f32)


def add_pair_kernel(kept, arrived, *refs):
    refs[-1][...] = (flat(kept) + flat(arrived)).astype(bf16)


def add_pair(kept, arrived, item, after):
    return pl.pallas_call(
        add_pair_kernel,
        grid=(1,),
        in_specs=[lead(kept, 1, item), lead(arrived)] + unread(after),
        out_specs=whole(arrived.shape),
        out_shape=jax.ShapeDtypeStruct(arrived.shape, bf16),
        cost_estimate=small_cost,
        compiler_params=whole_vmem,
        name="add_pair",
    )(kept, arrived, *after)


def finish_kernel(cuts, own, arrived, other, *refs):
    total = flat(own) + flat(arrived) + flat(other)
    outs = refs[-len(cuts) :]
    for (first, last, turned), out in zip(cuts, outs):
        part = total[:, first:last]
        out[...] = part.T[: out.shape[0]] if turned else part


def finish(name, parts, cuts, sizes, after):
    own, arrived, other = parts
    arrived, other = arrived[0], other[0]
    rows = own.shape[-2]
    shapes = [
        (size, rows) if turned else (rows, last - first)
        for (first, last, turned), size in zip(cuts, sizes)
    ]
    return pl.pallas_call(
        functools.partial(finish_kernel, cuts),
        grid=(1,),
        in_specs=[lead(own, 0, 0), lead(arrived), lead(other)] + unread(after),
        out_specs=[whole(shape) for shape in shapes],
        out_shape=[jax.ShapeDtypeStruct(shape, f32) for shape in shapes],
        compiler_params=whole_vmem,
        cost_estimate=small_cost,
        name=name,
    )(own, arrived, other, *after)


def prepare_kernel(bits, gate, up, down, *outs):
    for step in range(2):

        @pl.when(pl.program_id(0) == step)
        def copy(step=step):
            outs[step][0] = gate[0]
            outs[step][1] = up[0]
            outs[step][2] = down[0].T


def prepare(bit, gate, up, down):
    _, depth, hidden = gate.shape
    shape = (3, depth, hidden)

    def chosen(array):
        return pl.BlockSpec(
            (1,) + array.shape[1:], lambda i, bits: (jnp.where(i == 0, 1 - bits[0], bits[0]), 0, 0)
        )

    return pl.pallas_call(
        prepare_kernel,
        grid_spec=pltpu.PrefetchScalarGridSpec(
            num_scalar_prefetch=1,
            grid=(2,),
            in_specs=[chosen(gate), chosen(up), chosen(down)],
            out_specs=[pl.BlockSpec(shape, lambda i, bits: (0, 0, 0))] * 2,
        ),
        out_shape=[jax.ShapeDtypeStruct(shape, bf16)] * 2,
        compiler_params=whole_vmem,
        cost_estimate=small_cost,
        name="prepare",
    )(bit.reshape(1), gate, up, down)


def dispatch_kernel(branch, slots, *refs):
    mine_out, others_out = refs[-3], refs[-2:]
    capacity = slots.shape[1] // 2
    step = pl.program_id(0)
    for owner in range(slots.shape[0]):
        rows = slots.shape[2]
        places = slice(owner * capacity, (owner + 1) * capacity)
        rows_in = dot_plain(slots[owner], branch[owner * rows : (owner + 1) * rows]).astype(bf16)
        mine_out[places] = rows_in[:capacity]
        for half, other_out in enumerate(others_out):

            @pl.when(step == half)
            def store(other_out=other_out, places=places, rows_in=rows_in):
                other_out[places] = rows_in[capacity:]


def slot_specs(slots, step):
    members, both, rows = slots.shape
    return (
        pl.BlockSpec((step, both, rows), lambda i: (i, 0, 0)),
        functools.partial(by_rows, step * both // 2),
        functools.partial(by_rows, step * rows),
        (members // step,),
    )


def dispatch(branch, slots, after):
    members, both, _ = slots.shape
    width = branch.shape[1]
    slot_spec, slot_rows, token_rows, grid = slot_specs(slots, members // 2)
    half = (members * both // 4, width)
    return pl.pallas_call(
        dispatch_kernel,
        grid=grid,
        in_specs=[token_rows(width), slot_spec] + unread(after),
        out_specs=[slot_rows(width), whole(half), whole(half)],
        out_shape=[
            jax.ShapeDtypeStruct((members * both // 2, width), bf16),
            jax.ShapeDtypeStruct(half, bf16),
            jax.ShapeDtypeStruct(half, bf16),
        ],
        cost_estimate=small_cost,
        compiler_params=whole_vmem,
        name="dispatch",
    )(branch, slots, *after)


def shared_kernel(branch, weights, router, hot, *refs):
    act_out, slope_out, inner_out, gates_out = refs[-4:]
    named = hot[...] != 0
    logits = jnp.where(named, dot_right_t(branch[...], router[...]), masked_value)
    raised = jnp.exp(logits - jnp.max(logits, axis=1, keepdims=True))
    raised = jnp.where(named, raised, 0.0)
    gates_out[...] = raised / jnp.sum(raised, axis=1, keepdims=True)
    hidden = act_out.shape[1]
    both = dot_right_t(branch[...], weights[...])
    gate, up = both[:, :hidden], both[:, hidden:]
    act, slope = silu_parts(gate)
    act_out[...] = act.astype(bf16)
    slope_out[...] = (up * slope).astype(bf16)
    inner_out[...] = (act * up).astype(bf16)


def router_rows(weights):
    last = weights.shape[0] // 128 - 1
    return pl.BlockSpec((128, weights.shape[1]), lambda i, *prefetched: (last, 0))


def shared_forward(branch, weights, hot, after):
    rows, width = branch.shape
    hidden = (weights.shape[0] - 128) // 3
    block = 512
    shape = jax.ShapeDtypeStruct((rows, hidden), bf16)
    return pl.pallas_call(
        shared_kernel,
        grid=(rows // block,),
        in_specs=[
            by_rows(block, width),
            whole((2 * hidden, width)),
            router_rows(weights),
            by_rows(block, 128),
        ]
        + unread(after),
        out_specs=[by_rows(block, hidden)] * 3 + [by_rows(block, 128)],
        out_shape=[shape] * 3 + [jax.ShapeDtypeStruct((rows, 128), f32)],
        compiler_params=whole_vmem,
        cost_estimate=small_cost,
        name="shared_forward",
    )(branch, weights, weights, hot, *after)


def shared_back_kernel(grad, down, act, slope, *refs):
    out = refs[-1]
    hidden = act.shape[1]
    inner = dot_right_t(grad[...], down[...])
    out[:, :hidden] = (inner * slope[...].astype(f32)).astype(bf16)
    out[:, hidden:] = (inner * act[...].astype(f32)).astype(bf16)


def shared_back(grad, weights, act, slope, after):
    rows, width = grad.shape
    hidden = act.shape[1]
    block = 512
    return pl.pallas_call(
        shared_back_kernel,
        grid=(rows // block,),
        in_specs=[
            by_rows(block, width),
            pl.BlockSpec((hidden, width), lambda i: (2, 0)),
            by_rows(block, hidden),
            by_rows(block, hidden),
        ]
        + unread(after),
        out_specs=by_rows(block, 2 * hidden),
        out_shape=jax.ShapeDtypeStruct((rows, 2 * hidden), bf16),
        compiler_params=whole_vmem,
        cost_estimate=small_cost,
        name="shared_back",
    )(grad, weights, act, slope, *after)


def combine_kernel(named, inner, down, slots, out_mine, other_a, other_b, gates, out):
    lane = lax.broadcasted_iota(jnp.int32, gates.shape, 1)
    gate_mine, gate_other = [
        jnp.sum(jnp.where(lane == named[index], gates[...], 0.0), axis=1, keepdims=True)
        for index in range(2)
    ]
    out_other = jnp.where(pl.program_id(0) == 0, other_a[...], other_b[...])
    rows = slots.shape[2]
    capacity = slots.shape[1] // 2
    total = dot_plain(inner[...], down[...])
    for owner in range(slots.shape[0]):
        tokens = slice(owner * rows, (owner + 1) * rows)
        places = slice(owner * capacity, (owner + 1) * capacity)
        mine = dot_left_t(slots[owner, :capacity], out_mine[places])
        other = dot_left_t(slots[owner, capacity:], out_other[places])
        part = total[tokens] + gate_mine[tokens] * mine + gate_other[tokens] * other
        out[tokens] = part.astype(bf16)


def combine(inner, weights, slots, out_mine, out_other, gates, named):
    hidden, width = inner.shape[1], weights.shape[1]
    members, both, rows = slots.shape
    half = members // 2

    def part(rows, cols):
        return pl.BlockSpec((rows, cols), lambda i, named: (i, 0))

    def all_of(shape):
        return pl.BlockSpec(shape, lambda i, named: (0, 0))

    return pl.pallas_call(
        combine_kernel,
        grid_spec=pltpu.PrefetchScalarGridSpec(
            num_scalar_prefetch=1,
            grid=(2,),
            in_specs=[
                part(half * rows, hidden),
                pl.BlockSpec((hidden, width), lambda i, named: (2, 0)),
                pl.BlockSpec((half, both, rows), lambda i, named: (i, 0, 0)),
                part(half * both // 2, width),
                all_of(out_other[0].shape),
                all_of(out_other[1].shape),
                part(half * rows, 128),
            ],
            out_specs=part(half * rows, width),
        ),
        out_shape=jax.ShapeDtypeStruct((inner.shape[0], width), bf16),
        compiler_params=whole_vmem,
        cost_estimate=small_cost,
        name="combine",
    )(named, inner, weights, slots, out_mine, *out_other, gates)


def out_grad_kernel(grad, slots, out_mine, other_a, other_b, gate_mine, gate_other, *refs):
    out_other = jnp.where(pl.program_id(0) < pl.num_programs(0) // 2, other_a[...], other_b[...])
    grad_mine, grad_other, gate_grad_mine, gate_grad_other = refs[-4:]
    rows = slots.shape[2]
    capacity = slots.shape[1] // 2
    for owner in range(slots.shape[0]):
        places = slice(owner * capacity, (owner + 1) * capacity)
        hot = slots[owner].astype(f32)
        both = dot_plain(slots[owner], grad[owner * rows : (owner + 1) * rows])
        halves = (
            (hot[:capacity], both[:capacity], out_mine, gate_mine, grad_mine, gate_grad_mine),
            (hot[capacity:], both[capacity:], out_other, gate_other, grad_other, gate_grad_other),
        )
        for hot_half, slot_grad, out, gate, grad_out, gate_out in halves:
            slot_gate = jnp.sum(hot_half * gate[owner], axis=1, keepdims=True)
            grad_out[places] = (slot_gate * slot_grad).astype(bf16)
            gate_grad = jnp.sum(slot_grad * out[places].astype(f32), axis=1, keepdims=True)
            gate_out[owner] = jnp.sum(hot_half * gate_grad, axis=0, keepdims=True)


def out_grads(grad, slots, out_mine, out_other, gate_mine, gate_other, after):
    members, both, rows = slots.shape
    width = grad.shape[1]
    slot_spec, slot_rows, token_rows, grid = slot_specs(slots, 2)
    line = pl.BlockSpec((2, 1, rows), lambda i: (i, 0, 0))
    steps = members // 4
    first_half = pl.BlockSpec((both, width), lambda i: (jnp.minimum(i, steps - 1), 0))
    second_half = pl.BlockSpec((both, width), lambda i: (jnp.maximum(i - steps, 0), 0))
    grads = jax.ShapeDtypeStruct((members * both // 2, width), bf16)
    gates = jax.ShapeDtypeStruct((members, 1, rows), f32)
    return pl.pallas_call(
        out_grad_kernel,
        grid=grid,
        in_specs=[
            token_rows(width),
            slot_spec,
            slot_rows(width),
            first_half,
            second_half,
            line,
            line,
        ]
        + unread(after),
        out_specs=[slot_rows(width), slot_rows(width), line, line],
        out_shape=[grads, grads, gates, gates],
        compiler_params=whole_vmem,
        cost_estimate=small_cost,
        name="out_grads",
    )(
        grad,
        slots,
        out_mine,
        *out_other,
        gate_mine.reshape(members, 1, rows),
        gate_other.reshape(members, 1, rows),
        *after,
    )


def combine_back_kernel(grads, logit_grad, weights, router, slots, in_mine, in_other, *refs):
    out = refs[-1]
    rows = slots.shape[2]
    capacity = slots.shape[1] // 2
    total = dot_plain(grads[...], weights[...]) + dot_plain(logit_grad[...], router[...])
    for owner in range(slots.shape[0]):
        tokens = slice(owner * rows, (owner + 1) * rows)
        places = slice(owner * capacity, (owner + 1) * capacity)
        arrived = jnp.concatenate([in_mine[places], in_other[places]], axis=0)
        out[tokens] = (total[tokens] + dot_left_t(slots[owner], arrived)).astype(bf16)


def combine_back(grads, logit_grad, weights, slots, in_mine, in_other, after):
    width = weights.shape[1]
    slot_spec, slot_rows, token_rows, grid = slot_specs(slots, 4)
    return pl.pallas_call(
        combine_back_kernel,
        grid=grid,
        in_specs=[
            token_rows(grads.shape[1]),
            token_rows(logit_grad.shape[1]),
            whole((grads.shape[1], width)),
            router_rows(weights),
            slot_spec,
            slot_rows(width),
            slot_rows(width),
        ]
        + unread(after),
        out_specs=token_rows(width),
        out_shape=jax.ShapeDtypeStruct((grads.shape[0], width), bf16),
        compiler_params=whole_vmem,
        cost_estimate=small_cost,
        name="combine_back",
    )(grads, logit_grad, weights, weights, slots, in_mine, in_other, *after)


def latent_grad_kernel(kv_past, rope_past, kv_own, rope_own, expand, *refs):
    out = refs[-1]
    for index, (kv, rope) in enumerate(((kv_past, rope_past), (kv_own, rope_own))):
        out[index, :, :LATENT] = dot_right_t(kv[...], expand[...]).astype(bf16)
        out[index, :, LATENT:] = rope[...]


def latent_grads(kv_past, rope_past, kv_own, rope_own, expand, after):
    rows, cols = kv_past.shape
    rope_cols = rope_past.shape[1]
    block = QUERY_BLOCK
    kv_spec, rope_spec = by_rows(block, cols), by_rows(block, rope_cols)
    return pl.pallas_call(
        latent_grad_kernel,
        grid=(rows // block,),
        in_specs=[kv_spec, rope_spec, kv_spec, rope_spec, whole(expand.shape)] + unread(after),
        out_specs=pl.BlockSpec((2, block, LATENT + rope_cols), lambda i: (0, i, 0)),
        out_shape=jax.ShapeDtypeStruct((2, rows, LATENT + rope_cols), bf16),
        cost_estimate=small_cost,
        compiler_params=whole_vmem,
        name="latent_grads",
    )(kv_past, rope_past, kv_own, rope_own, expand, *after)


def first_block_kernel(blocks, *refs):
    refs[-1][...] = blocks[0]


def first_block(blocks, after):
    shape = blocks.shape[1:]
    return pl.pallas_call(
        first_block_kernel,
        grid=(1,),
        in_specs=[lead(blocks, 0)] + unread(after),
        out_specs=whole(shape),
        out_shape=jax.ShapeDtypeStruct(shape, blocks.dtype),
        cost_estimate=small_cost,
        compiler_params=whole_vmem,
        name="first_block",
    )(blocks, *after)


def join_kernel(count, *refs):
    rows = refs[0].shape[0]
    for index in range(count):
        refs[-1][index * rows : (index + 1) * rows] = refs[index][...]


def join_rows(blocks, after):
    rows, cols = blocks[0].shape
    shape = (len(blocks) * rows, cols)
    return pl.pallas_call(
        functools.partial(join_kernel, len(blocks)),
        grid=(1,),
        in_specs=[whole((rows, cols))] * len(blocks) + unread(after),
        out_specs=whole(shape),
        out_shape=jax.ShapeDtypeStruct(shape, blocks[0].dtype),
        cost_estimate=small_cost,
        compiler_params=whole_vmem,
        name="join_rows",
    )(*blocks, *after)


def latent_back_kernel(own, back, unit, factor, gain, cosine, sine, *refs):
    grad_out, gain_grad_out = refs[-2:]
    grad = own[...].astype(f32) + back[...].astype(f32)
    plain = grad[:, :LATENT]
    gain_grad_out[...] = jnp.sum(plain * unit[...], axis=0, keepdims=True)
    grad_out[:, :LATENT] = norm_back(plain, unit[...], factor[...], gain[...]).astype(bf16)
    grad_out[:, LATENT:] = turn_back(grad[:, LATENT:], cosine[...], sine[...]).astype(bf16)


def latent_back_rows(own, back, unit, factor, gain, cosine, sine, after):
    rows, cols = own.shape
    inputs = [own, back, unit, factor, gain[None], cosine, sine]
    return pl.pallas_call(
        latent_back_kernel,
        grid=(1,),
        in_specs=[whole(array.shape) for array in inputs] + unread(after),
        out_specs=[whole((rows, cols)), whole((1, LATENT))],
        out_shape=[
            jax.ShapeDtypeStruct((rows, cols), bf16),
            jax.ShapeDtypeStruct((1, LATENT), f32),
        ],
        cost_estimate=small_cost,
        compiler_params=whole_vmem,
        name="latent_back",
    )(*inputs, *after)


def tokens_back_kernel(grad, projected, compress, unit, factor, gain, hidden_grad, *refs):
    out, gain_grad_out = refs[-2:]
    total = grad[...].astype(f32) + dot_plain(projected[...], compress[...])
    gain_grad_out[...] = jnp.sum(total * unit[...], axis=0, keepdims=True)
    out[...] = hidden_grad[...] + norm_back(total, unit[...], factor[...], gain[...])


def tokens_back(grad, projected, compress, unit, factor, gain, hidden_grad, after):
    rows, width = grad.shape
    inputs = [grad, projected, compress, unit, factor, gain[None], hidden_grad]
    return pl.pallas_call(
        tokens_back_kernel,
        grid=(1,),
        in_specs=[whole(array.shape) for array in inputs] + unread(after),
        out_specs=[whole((rows, width)), whole((1, width))],
        out_shape=[
            jax.ShapeDtypeStruct((rows, width), f32),
            jax.ShapeDtypeStruct((1, width), f32),
        ],
        compiler_params=whole_vmem,
        cost_estimate=small_cost,
        name="tokens_back",
    )(*inputs, *after)


def slice_grad_kernel(index, left, right, *refs):
    out = refs[-1]
    half = ROPE // 2
    grad = dot_left_t(left[...], right[...])
    out[:LATENT] = grad[:LATENT]
    turned = grad[LATENT:]
    out[LATENT : LATENT + half] = turned[:half] + turned[half:ROPE]
    out[LATENT + half :] = turned[ROPE : ROPE + half] + turned[ROPE + half :]


def beside_kernel(blocks, out):
    cols = blocks.shape[2]
    for index in range(blocks.shape[0]):
        out[:, index * cols : (index + 1) * cols] = blocks[index].astype(f32)


def beside(blocks, rows):
    count, _, cols = blocks.shape
    step = rows // 4
    return pl.pallas_call(
        beside_kernel,
        grid=(4,),
        in_specs=[pl.BlockSpec((count, step, cols), lambda i: (0, i, 0))],
        out_specs=by_rows(step, count * cols),
        out_shape=jax.ShapeDtypeStruct((rows, count * cols), f32),
        cost_estimate=small_cost,
        compiler_params=whole_vmem,
        name="beside",
    )(blocks)


def slice_grad(left, right, index, cols, after):
    rows = left.shape[0]
    out_rows = LATENT + ROPE
    return pl.pallas_call(
        slice_grad_kernel,
        grid_spec=pltpu.PrefetchScalarGridSpec(
            num_scalar_prefetch=1,
            grid=(1,),
            in_specs=[
                pl.BlockSpec(left.shape, lambda i, index: (0, 0)),
                pl.BlockSpec((rows, cols), lambda i, index: (0, index[0])),
            ]
            + unread(after),
            out_specs=pl.BlockSpec((out_rows, cols), lambda i, index: (0, 0)),
        ),
        out_shape=jax.ShapeDtypeStruct((out_rows, cols), f32),
        cost_estimate=small_cost,
        compiler_params=whole_vmem,
        name="slice_grad",
    )(index.reshape(1), left, right, *after)


def place_kernel(turned, bits, own, arrived, other, *refs):
    out = refs[-1]

    @pl.when(pl.program_id(0) == 0)
    def first():
        total = flat(own) + flat(arrived)
        out[0] = total.T if turned else total

    @pl.when(pl.program_id(0) == 1)
    def second():
        total = flat(other)
        out[0] = total.T if turned else total


def place_experts(bit, parts, item, turned, after):
    own, arrived, other = parts
    arrived_item, other_item = arrived[item], other[item]
    shape = own.shape[:-3:-1] if turned else own.shape[-2:]
    return pl.pallas_call(
        functools.partial(place_kernel, turned),
        grid_spec=pltpu.PrefetchScalarGridSpec(
            num_scalar_prefetch=1,
            grid=(2,),
            in_specs=[lead(own, 0, item), lead(arrived_item), lead(other_item)]
            + unread(after),
            out_specs=pl.BlockSpec(
                (1,) + shape, lambda i, bits: (jnp.where(i == 0, bits[0], 1 - bits[0]), 0, 0)
            ),
        ),
        out_shape=jax.ShapeDtypeStruct((2,) + shape, f32),
        compiler_params=whole_vmem,
        cost_estimate=small_cost,
        name="place_experts",
    )(bit.reshape(1), own, arrived_item, other_item, *after)


def split_query_columns(weight):
    head = NOPE + ROPE
    half = ROPE // 2
    pieces = [weight[:, :NOPE], weight[:, head : head + NOPE]]
    for part in range(2):
        for index in range(2):
            first = index * head + NOPE + part * half
            pieces.append(weight[:, first : first + half])
    return jnp.concatenate(pieces, axis=1)


def join_query_columns(grad):
    half = ROPE // 2
    base = 2 * NOPE
    pieces = []
    for index in range(2):
        pieces.append(grad[:, index * NOPE : (index + 1) * NOPE])
        for part in range(2):
            first = base + part * ROPE + index * half
            pieces.append(grad[:, first : first + half])
    return jnp.concatenate(pieces, axis=1)


class Pairing:
    def __init__(self, groups, members):
        self.groups = groups
        self.members = members
        self.bits = groups.bit_length() - 1
        top = self.bits - 1
        self.partner = (1 << top, 1)
        self.others = (
            [1 << bit for bit in range(top)],
            [1 << (bit + 1) for bit in range(top)],
        )
        self.group = lax.axis_index("dp")
        self.odd = lax.axis_index("expert") % 2

    def chosen(self, masks):
        return jnp.where(self.odd == 1, masks[1], masks[0])

    def place(self, masks):
        return self.group ^ self.chosen(masks)

    def bit(self):
        return jnp.where(self.group & self.chosen(self.partner), 1, 0)

    def swap(self, value, masks):
        pairs = []
        for group in range(self.groups):
            for member in range(self.members):
                other = group ^ masks[member % 2]
                pairs.append((group * self.members + member, other * self.members + member))
        return lax.ppermute(value, ("dp", "expert"), pairs)

    def swap_partner(self, value):
        return self.swap(value, self.partner)

    def masks(self):
        masks = [(0, 0), self.partner]
        for step in zip(*self.others):
            masks = masks + [(even ^ step[0], odd ^ step[1]) for even, odd in masks]
        return masks

    def places(self):
        return jnp.stack([self.place(mask) for mask in self.masks()])

    def spread(self, held):
        for step in zip(*self.others):
            held = held + [self.swap(piece, step) for piece in held]
        return held

    def collect(self, kept, given):
        steps = list(reversed(list(zip(*self.others))))
        for number, step in enumerate(steps):
            arrived = [self.swap(piece, step) for piece in given]
            if number < len(steps) - 1:
                total = kept.astype(f32) + jnp.stack(arrived).reshape(kept.shape).astype(f32)
                total = total.astype(bf16)
                half = total.shape[0] // 2
                kept, given = total[:half], list(total[half:].reshape((-1,) + total.shape[2:]))
        return (kept, arrived)

    def partner_sum(self, kept, arrived, item, after=()):
        return add_pair(kept, arrived[kept.shape[1] + item], item, after)

    def gather_members(self, value, after):
        member = lax.axis_index("expert")
        rows = value.shape[0]
        chips = [value]
        for other in range(1, self.members // 2):
            pairs = [(i, i ^ (2 * other)) for i in range(self.members)]
            chips.append(lax.ppermute(value, "expert", pairs))
        both = lax.ppermute(
            join_rows(chips, after), "expert", [(i, i ^ 1) for i in range(self.members)]
        )
        held = []
        for number, block in enumerate(chips):
            held += [block, both[number * rows : (number + 1) * rows]]
        bit = 1
        while bit < self.members:
            flip = (member & bit) != 0
            held = [jnp.where(flip, held[i ^ bit], held[i]) for i in range(self.members)]
            bit *= 2
        return jnp.concatenate(held)

    def total(self, value):
        for bit in range(self.bits):
            arrived = self.swap(value.astype(bf16), (1 << bit, 1 << (self.bits - 1 - bit)))
            value = value + arrived.astype(f32)
        return value

    def total_members(self, value):
        for bit in range(self.members.bit_length() - 1):
            pairs = [(i, i ^ (1 << bit)) for i in range(self.members)]
            value = value + lax.ppermute(value, "expert", pairs)
        return value

    def total_all(self, value):
        size = self.groups * self.members
        for bit in range(size.bit_length() - 1):
            pairs = [(i, i ^ (1 << bit)) for i in range(size)]
            value = value + lax.ppermute(value, ("dp", "expert"), pairs)
        return value


def body(
    tokens,
    target,
    valid,
    routes,
    lengths,
    first_gain_vector,
    second_gain_vector,
    latent_gain_vector,
    latent_compress_weight,
    query_weight,
    latent_expand_weight,
    output_weight,
    router_weight,
    shared_gate_weight,
    shared_up_weight,
    shared_down_weight,
    expert_gate_weight,
    expert_up_weight,
    expert_down_weight,
):
    rows, width = tokens.shape
    members = lax.axis_size("expert")
    groups = lax.axis_size("dp")
    member = lax.axis_index("expert")
    group = lax.axis_index("dp")
    group_size = rows * members
    local_experts = expert_gate_weight.shape[0]
    route_count = routes.shape[1]
    expert_count = router_weight.shape[1]
    hidden_width = expert_gate_weight.shape[2]
    capacity = rows * route_count * 4 // (3 * local_experts * members)
    pairing = Pairing(groups, members)
    bit = pairing.bit()

    def pick(array, index):
        return lax.dynamic_index_in_dim(array, index, 0, False)

    tokens_float = tokens.astype(f32)
    own_unit, own_factor = normalize(tokens_float)
    own_normed = (own_unit * first_gain_vector).astype(bf16)
    normed = lax.all_gather(own_normed, "expert", axis=0, tiled=True)
    half = ROPE // 2
    compress_t = latent_compress_weight.T
    compress_t = jnp.concatenate(
        [compress_t[: LATENT + half]]
        + [compress_t[LATENT : LATENT + half]]
        + [compress_t[LATENT + half :]] * 2
    )
    index = group * group_size + jnp.arange(group_size, dtype=jnp.int32)
    seq_id = jnp.floor_divide(index, SEQ)
    place = index - seq_id * SEQ
    cosine, sine = angles(place, half)
    cosine = jnp.concatenate([cosine] * 4, axis=1)
    sine = jnp.concatenate([-sine, -sine, sine, sine], axis=1)
    own_cos = lax.dynamic_slice_in_dim(cosine, member * rows, rows, 0)
    own_sin = lax.dynamic_slice_in_dim(sine, member * rows, rows, 0)
    projected = dot_right_t(own_normed, compress_t)
    latent_unit, latent_factor = normalize(projected[:, :LATENT])
    places = pairing.places()
    given, kept = prepare(bit, expert_gate_weight, expert_up_weight, expert_down_weight)
    expert_w = pairing.spread([kept, pairing.swap_partner(given)])

    shared_hidden_width = shared_gate_weight.shape[1]
    padded = -(-shared_hidden_width // 128) * 128
    shared_w = jnp.concatenate(
        [
            jnp.pad(weight, ((0, extent - weight.shape[0]), (0, 0)))
            for weight, extent in (
                (shared_gate_weight.T, padded),
                (shared_up_weight.T, padded),
                (shared_down_weight, padded),
                (router_weight.T, 128),
            )
        ]
    )

    counted = valid.astype(f32)
    count = pairing.total_all(jnp.full((8, 128), jnp.sum(counted)))[0, 0]

    bounds = lax.dynamic_slice_in_dim(
        jnp.cumsum(lengths, axis=1), group * group_size // SEQ, 1, 0
    )
    doc_start = jnp.max(jnp.where(bounds <= place[:, None], bounds, 0), axis=1)
    in_block = jnp.arange(group_size, dtype=jnp.int32) % QUERY_BLOCK
    low = jnp.maximum(doc_start - place + WINDOW + in_block, in_block + 1)
    low = jnp.broadcast_to(low[:, None], (group_size, 128))

    hot = jnp.any(routes[:, :, None] == jnp.arange(128, dtype=jnp.int32), axis=1).astype(bf16)
    routes_t = routes.T.reshape(route_count, members, rows)
    order = jnp.arange(rows, dtype=jnp.int32)
    earlier = (order[:, None] < order[None, :]).astype(bf16)
    mine = member * local_experts + bit
    other = member * local_experts + 1 - bit

    def slots_of(expert):
        hit = jnp.any(routes_t == expert, axis=0)
        rank = dot_plain(hit.astype(bf16), earlier).astype(jnp.int32)
        slot = jnp.arange(capacity, dtype=jnp.int32)[None, :, None]
        return (hit[:, None, :] & (rank[:, None, :] == slot)).astype(bf16)

    slots = jnp.concatenate([slots_of(mine), slots_of(other)], axis=1)

    query_w = split_query_columns(query_weight)
    keys, group_latent = own_keys(
        normed,
        cosine,
        sine,
        latent_gain_vector,
        compress_t,
        latent_expand_weight,
        [shared_w, query_w],
    )
    forward = [(i, i + 1) for i in range(groups - 1)]
    past = lax.ppermute(keys, "dp", forward)
    previous = lax.ppermute(group_latent, "dp", forward)
    query = project_query(normed, cosine, sine, query_w)
    mixed, logs, attention_part = attend(query, low, keys, past, output_weight, expert_w[1:2])
    attention = lax.psum_scatter(attention_part, "expert", scatter_dimension=0, tiled=True)
    hidden, hidden_unit, hidden_factor, own_branch = norm(
        tokens, attention, second_gain_vector, expert_w[2:3]
    )
    branch = lax.all_gather(own_branch, "expert", axis=0, tiled=True)

    in_mine, *in_others = dispatch(branch, slots, expert_w[3:])
    in_arrived = [pairing.swap_partner(half) for half in in_others]
    act_m, slope_m, inner_m, out_mine = expert_call(
        expert_kernel, "expert", places, in_mine, [], expert_w, 3, []
    )
    half_rows, slot_rows = in_arrived[0].shape[0], in_mine.shape[0]
    *held, out_first = expert_call(
        expert_kernel,
        "expert",
        places,
        in_arrived[0],
        [],
        expert_w,
        3,
        [out_mine],
        0,
        slot_rows,
    )
    *held, out_second = expert_call(
        expert_kernel, "expert", places, in_arrived[1], [], expert_w, 3, [], half_rows, slot_rows, held
    )
    act_a, slope_a, inner_a = held
    out_other = [pairing.swap_partner(half) for half in (out_first, out_second)]
    shared_act, shared_slope, shared_hidden, gates = shared_forward(
        branch, shared_w, hot, [out_second, out_other[0]]
    )
    experts = jnp.arange(128, dtype=jnp.int32)[None, :]
    gate_mine = jnp.sum(jnp.where(experts == mine, gates, 0.0), axis=1)
    gate_other = jnp.sum(jnp.where(experts == other, gates, 0.0), axis=1)
    branch_part = combine(
        shared_hidden, shared_w, slots, out_mine, out_other, gates, jnp.stack([mine, other])
    )
    branch_sum = lax.psum_scatter(branch_part, "expert", scatter_dimension=0, tiled=True)
    result = hidden + branch_sum.astype(f32)
    difference = result - target.astype(f32)
    squares = jnp.sum(counted[:, None] * difference * difference)
    squares = pairing.total_all(jnp.full((8, 128), squares))
    total_tokens = rows * members * groups
    grad_out = total_tokens / count * counted[:, None] * difference

    grad_low = lax.all_gather(grad_out.astype(bf16), "expert", axis=0, tiled=True)

    out_grad_mine, out_grad_other, gate_grad_mine, gate_grad_other = out_grads(
        grad_low, slots, out_mine, out_other, gate_mine, gate_other, [previous, squares]
    )
    out_grad_arrived = pairing.swap_partner(out_grad_other)
    shared_grad = shared_back(grad_low, shared_w, shared_act, shared_slope, [out_grad_mine])
    gate_gm, up_gm, in_grad_mine = expert_call(
        expert_back_kernel,
        "expert_back",
        places,
        out_grad_mine,
        [act_m, slope_m],
        expert_w,
        2,
        [shared_grad],
    )
    gate_ga, up_ga, in_grad_arrived = expert_call(
        expert_back_kernel,
        "expert_back",
        places,
        out_grad_arrived,
        [act_a, slope_a],
        expert_w,
        2,
        [in_grad_mine],
    )
    in_grad_other = pairing.swap_partner(in_grad_arrived)

    down_kept, down_given = weight_grads(
        "down_grad",
        places,
        [[[(out_grad_mine, inner_m), (out_grad_arrived, inner_a)]]],
        [in_grad_arrived],
    )

    gate_grads = jnp.where(experts == mine, gate_grad_mine.reshape(-1, 1), 0.0) + jnp.where(
        experts == other, gate_grad_other.reshape(-1, 1), 0.0
    )
    logit_grad = gates * (gate_grads - jnp.sum(gates * gate_grads, axis=1, keepdims=True))
    logit_total = pairing.total_members(
        first_block(logit_grad[:, :expert_count].T[None], [down_kept])
    )
    logit_grad = logit_grad.astype(bf16)
    branch_slice = lax.dynamic_slice_in_dim(branch, member * (width // members), width // members, 1)
    router_slice = dot_plain(logit_total.astype(bf16), branch_slice)
    branch_grad_part = combine_back(
        shared_grad,
        logit_grad,
        shared_w,
        slots,
        in_grad_mine,
        in_grad_other,
        [logit_total],
    )
    branch_grad = lax.psum_scatter(
        branch_grad_part, "expert", scatter_dimension=0, tiled=True
    )

    down_terms = pairing.collect(down_kept, down_given)
    gate_up_kept, gate_up_given = weight_grads(
        "gate_up_grad",
        places,
        [
            [[(in_mine, gate_gm), (in_arrived, gate_ga)]],
            [[(in_mine, up_gm), (in_arrived, up_ga)]],
        ],
        [branch_grad_part],
    )
    gate_up_terms = pairing.collect(gate_up_kept, gate_up_given)
    shared_kept, shared_given = weight_grads(
        "shared_grads",
        places,
        [[[(branch, shared_grad)], [(grad_low, shared_hidden)]]],
        [gate_up_kept],
    )
    shared_terms = pairing.collect(shared_kept, shared_given)
    down_sum = pairing.partner_sum(*down_terms, 0)
    gate_sum, up_sum = [pairing.partner_sum(*gate_up_terms, item) for item in range(2)]
    down_other, gate_other_half, up_other_half = [
        pairing.swap_partner(total) for total in (down_sum, gate_sum, up_sum)
    ]
    down_parts = (*down_terms, [down_other])
    gate_up_parts = (*gate_up_terms, [gate_other_half, up_other_half])

    grad_hidden_own, grad_hidden_low, grad_norm2 = norm_back_rows(
        branch_grad,
        grad_out,
        hidden_unit,
        hidden_factor,
        second_gain_vector,
        down_terms[1] + gate_up_terms[1][2:3] + [shared_kept],
    )
    grad_attention = lax.all_gather(grad_hidden_low, "expert", axis=0, tiled=True)
    query_grad, normed_grad_part, kv_past, rope_past, kv_own, rope_own = attend_back(
        grad_attention,
        query,
        logs,
        cosine,
        sine,
        low,
        query_w,
        keys,
        past,
        output_weight,
        [down_sum, gate_sum],
    )

    latent_grad = lax.psum_scatter(
        latent_grads(
            kv_past, rope_past, kv_own, rope_own, latent_expand_weight, shared_terms[1] + [down_other, gate_other_half, up_sum]
        ),
        "expert",
        scatter_dimension=1,
        tiled=True,
    )
    normed_grad = lax.psum_scatter(
        normed_grad_part, "expert", scatter_dimension=0, tiled=True
    )

    attention_kept, attention_given = weight_grads(
        "attention_grads",
        places,
        [[[(normed, query_grad)], [(grad_attention, mixed)]]],
        [kv_own],
    )
    expand_grad = (
        dot_left_t(previous, kv_past) + dot_left_t(group_latent, kv_own)
    ).astype(bf16)
    expand_grad = expand_grad.reshape(groups, -1, expand_grad.shape[1])
    expand_pieces = jnp.stack([pick(expand_grad, places[i]) for i in range(groups)])[:, None]
    expand_terms = pairing.collect(
        expand_pieces[: groups // 2], list(expand_pieces[groups // 2 :].squeeze(1))
    )
    expert_down_gradient = place_experts(bit, down_parts, 0, True, [attention_kept])
    expand_sum = pairing.partner_sum(*expand_terms, 0)
    expand_parts = (*expand_terms, [pairing.swap_partner(expand_sum)])
    shared_sum = pairing.partner_sum(*shared_terms, 0)
    shared_parts = (*shared_terms, [pairing.swap_partner(shared_sum)])
    back = lax.ppermute(
        first_block(
            latent_grad,
            [attention_kept, expert_down_gradient, up_other_half, gate_up_terms[1][0], shared_sum]
            + [expand_pieces],
        ),
        "dp",
        [(i + 1, i) for i in range(groups - 1)],
    )

    grad_projected, grad_latent_gain = latent_back_rows(
        latent_grad[1],
        back,
        latent_unit,
        latent_factor,
        latent_gain_vector,
        own_cos,
        own_sin,
        gate_up_terms[1][1:2],
    )
    expert_gate_gradient = place_experts(bit, gate_up_parts, 0, False, [grad_projected])
    expert_up_gradient = place_experts(bit, gate_up_parts, 1, False, [grad_projected])
    slice_cols = width // members
    group_grad = pairing.gather_members(
        grad_projected, [expert_gate_gradient, expert_up_gradient, expand_sum]
    )
    attention_terms = pairing.collect(
        attention_kept, attention_given
    )
    compress_slice = slice_grad(group_grad, normed, member, slice_cols, [])
    grad_tokens, grad_norm1 = tokens_back(
        normed_grad,
        grad_projected,
        compress_t,
        own_unit,
        own_factor,
        first_gain_vector,
        grad_hidden_own,
        [],
    )
    gains = jnp.concatenate(
        [grad_latent_gain[0], grad_norm2[0], grad_norm1[0]]
    ).reshape(-1, slice_cols)
    gain_rows = -(-gains.shape[0] // 16) * 16
    gains = jnp.pad(gains, ((0, gain_rows - gains.shape[0]), (0, 0)))
    compress_rows = compress_slice.shape[0]
    compress_slice = pairing.total(
        jnp.concatenate([compress_slice, router_slice, gains])
    ).astype(bf16)
    compress_all = lax.all_gather(compress_slice, "expert", axis=0)
    kva_t = beside(compress_all, compress_rows)
    grad_kva = kva_t.T
    router_rows = compress_rows + expert_count
    grad_router = (
        compress_all[:, compress_rows:router_rows].transpose(0, 2, 1).reshape(width, -1).astype(f32)
    )
    gains = jnp.sum(compress_all[:, router_rows:].astype(f32), axis=0).reshape(-1)
    grad_latent_gain, gains = gains[:LATENT], gains[LATENT:]
    grad_norm2, grad_norm1 = gains[:width], gains[width : 2 * width]

    attention_sum = pairing.partner_sum(*attention_terms, 0, [group_grad])
    attention_parts = (*attention_terms, [pairing.swap_partner(attention_sum)])
    query_cols, mixed_cols = query_w.shape[1], mixed.shape[1]
    shared_gate_gradient, shared_up_gradient, shared_down_gradient = finish(
        "shared_finish",
        shared_parts,
        [(i * padded, (i + 1) * padded, True) for i in range(3)],
        [shared_hidden_width] * 3,
        [compress_slice],
    )
    query_weight_gradient, output_weight_gradient = finish(
        "attention_finish",
        attention_parts,
        [(0, query_cols, False), (query_cols, query_cols + mixed_cols, True)],
        [0, mixed_cols],
        [kva_t],
    )
    shared_gate_gradient, shared_up_gradient = shared_gate_gradient.T, shared_up_gradient.T
    query_weight_gradient = join_query_columns(query_weight_gradient)
    (latent_expand_gradient,) = finish(
        "expand_finish",
        expand_parts,
        [(0, expand_grad.shape[2], False)],
        [0],
        [compress_slice],
    )
    return (
        result.astype(bf16),
        squares[0, 0] / (count * width),
        grad_tokens,
        grad_norm1,
        grad_norm2,
        grad_latent_gain,
        grad_kva,
        query_weight_gradient,
        latent_expand_gradient,
        output_weight_gradient,
        grad_router,
        shared_gate_gradient,
        shared_up_gradient,
        shared_down_gradient,
        expert_gate_gradient,
        expert_up_gradient,
        expert_down_gradient,
    )


def solution(mesh):
    placed = (
        P(("dp", "expert"), None),
        P(("dp", "expert"), None),
        P(("dp", "expert")),
        P("dp", None),
        P(),
        P(),
        P(),
        P(),
        P(),
        P(None, "expert"),
        P(None, "expert"),
        P("expert", None),
        P(),
        P(None, "expert"),
        P(None, "expert"),
        P("expert", None),
        P("expert", "dp", None),
        P("expert", "dp", None),
        P("expert", None, "dp"),
    )
    return jax.shard_map(
        body,
        mesh=mesh,
        in_specs=placed,
        out_specs=(
            P(("dp", "expert"), None),
            P(),
            P(("dp", "expert"), None),
            P(),
            P(),
            P(),
            P(),
            P("dp", "expert"),
            P("dp", "expert"),
            P("expert", "dp"),
            P(),
            P("dp", "expert"),
            P("dp", "expert"),
            P("expert", "dp"),
            P("expert", "dp", None),
            P("expert", "dp", None),
            P("expert", None, "dp"),
        ),
        check_vma=False,
    )
```

```python
import functools

import jax
import jax.numpy as jnp
from jax import lax
from jax.experimental import pallas as pl
from jax.experimental.pallas import tpu as pltpu
from jax.sharding import PartitionSpec as P

NOPE = 128
ROPE = 64
VDIM = 128
LATENT = 512
SEQ = 4096
WINDOW = 1024
QUERY_BLOCK = 256

epsilon = 1e-06
masked_value = -1e30
score_scale = (NOPE + ROPE) ** (-0.5)
bf16 = jnp.bfloat16
f32 = jnp.float32
whole_vmem = pltpu.CompilerParams(vmem_limit_bytes=60 * 1024 * 1024)
small_cost = pl.CostEstimate(flops=1, bytes_accessed=1, transcendentals=0)


def dot_plain(left, right):
    return lax.dot_general(left, right, (((1,), (0,)), ((), ())), preferred_element_type=f32)


def dot_right_t(left, right):
    return lax.dot_general(left, right, (((1,), (1,)), ((), ())), preferred_element_type=f32)


def dot_left_t(left, right):
    return lax.dot_general(left, right, (((0,), (0,)), ((), ())), preferred_element_type=f32)


def normalize(values):
    factor = lax.rsqrt(jnp.mean(values * values, axis=-1, keepdims=True) + epsilon)
    return (values * factor, factor)


def norm_back(grad_out, unit, factor, gain):
    grad_unit = grad_out * gain
    return factor * (grad_unit - unit * jnp.mean(grad_unit * unit, axis=-1, keepdims=True))


def angles(place, half):
    freq = jnp.exp(-jnp.log(10000.0) * jnp.arange(half, dtype=f32) / half)
    angle = place.astype(f32)[:, None] * freq[None, :]
    return (jnp.cos(angle), jnp.sin(angle))


def silu_parts(values):
    sigma = jax.nn.sigmoid(values)
    return (values * sigma, sigma * (1.0 + values * (1.0 - sigma)))


def head_lanes(block, head):
    lane = lax.broadcasted_iota(jnp.int32, (block, 2 * ROPE), 1)
    return (lane // (ROPE // 2)) % 2 == head


def allowed_keys(low, block, span):
    row = lax.broadcasted_iota(jnp.int32, (block, span), 0)
    col = lax.broadcasted_iota(jnp.int32, (block, span), 1)
    return (col <= row + WINDOW) & (col >= low[:, :1])


def head_parts(query, lanes, keys, head):
    turned = jnp.where(lanes, query[:, 2 * NOPE :], 0)
    query_head = jnp.concatenate([query[:, head * NOPE : (head + 1) * NOPE], turned], axis=1)
    base = head * (NOPE + VDIM)
    rope = keys[:, 2 * (NOPE + VDIM) :]
    key_head = jnp.concatenate([keys[:, base : base + NOPE], rope], axis=1)
    return (query_head, key_head, keys[:, base + NOPE : base + NOPE + VDIM])


def attend_kernel(chunks, query_in, low, out_w, *refs):
    mixed_out, log_out, part_out = refs[-3:]
    keys = window_keys(refs, chunks)
    block = query_in.shape[0]
    query = query_in[...]
    mask = allowed_keys(low[...], block, WINDOW + block)
    mixed, logs = [], []
    for head in range(2):
        query_head, key_head, value_head = head_parts(query, head_lanes(block, head), keys, head)
        scores = jnp.where(mask, dot_right_t(query_head, key_head) * score_scale, masked_value)
        top = jnp.max(scores, axis=1, keepdims=True)
        raised = jnp.exp(scores - top)
        total = jnp.sum(raised, axis=1, keepdims=True)
        probs = (raised * (1.0 / total)).astype(bf16)
        mixed.append(dot_plain(probs, value_head))
        logs.append(top + jnp.log(total))
    lane = lax.broadcasted_iota(jnp.int32, (block, 128), 1)
    log_out[...] = jnp.where(lane == 0, logs[0], logs[1])
    mixed = jnp.concatenate(mixed, axis=1).astype(bf16)
    mixed_out[...] = mixed
    part_out[...] = dot_plain(mixed, out_w[...]).astype(bf16)


def by_rows(block, cols, offset=0):
    return pl.BlockSpec((block, cols), lambda i: (i + offset, 0))


def whole(shape):
    return pl.BlockSpec(shape, lambda i: (0, 0))


def unread(arrays):
    return [pl.BlockSpec(memory_space=pl.ANY) for _ in arrays]


def turn(values, cosine, sine):
    return values * cosine + pltpu.roll(values, ROPE, 1) * sine


def turn_back(values, cosine, sine):
    return values * cosine - pltpu.roll(values, ROPE, 1) * sine


def own_keys_kernel(normed, cosine, sine, gain, compress, expand, *refs):
    keys, latent = refs[-2:]
    projected = dot_right_t(normed[...], compress[...])
    unit, _ = normalize(projected[:, :LATENT])
    low = (unit * gain[...]).astype(bf16)
    latent[...] = low
    kv_cols = expand.shape[1]
    keys[:, :kv_cols] = dot_plain(low, expand[...]).astype(bf16)
    keys[:, kv_cols:] = turn(projected[:, LATENT:], cosine[...], sine[...]).astype(bf16)


def own_keys(normed, cosine, sine, gain, compress, expand, after):
    rows, width = normed.shape
    block = QUERY_BLOCK
    rope_cols = 2 * ROPE
    key_cols = expand.shape[1] + rope_cols
    return pl.pallas_call(
        own_keys_kernel,
        grid=(rows // block,),
        in_specs=[
            by_rows(block, width),
            by_rows(block, rope_cols),
            by_rows(block, rope_cols),
            whole((1, LATENT)),
            whole(compress.shape),
            whole(expand.shape),
        ]
        + unread(after),
        out_specs=[by_rows(block, key_cols), by_rows(block, LATENT)],
        out_shape=[
            jax.ShapeDtypeStruct((rows, key_cols), bf16),
            jax.ShapeDtypeStruct((rows, LATENT), bf16),
        ],
        compiler_params=whole_vmem,
        cost_estimate=small_cost,
        name="own_keys",
    )(normed, cosine, sine, gain[None], compress, expand, *after)


def key_blocks(keys, past, block, chunks):
    cols = keys.shape[1]
    blocks = past.shape[0] // block
    specs, operands = [], []
    for chunk in range(chunks):
        if chunk < chunks - 1:
            specs.append(
                pl.BlockSpec((block, cols), lambda i, c=chunk: (jnp.minimum(i + c, blocks - 1), 0))
            )
            operands.append(past)
        if chunk > 0:
            specs.append(
                pl.BlockSpec((block, cols), lambda i, c=chunk: (jnp.maximum(i + c - blocks, 0), 0))
            )
            operands.append(keys)
    return specs, operands


def window_keys(refs, chunks):
    step = pl.program_id(0)
    parts = [refs[0][...]]
    for chunk in range(1, chunks - 1):
        past, own = refs[2 * chunk - 1], refs[2 * chunk]
        parts.append(jnp.where(step + chunk < chunks - 1, past[...], own[...]))
    parts.append(refs[2 * chunks - 3][...])
    return jnp.concatenate(parts, axis=0)


def attend(query, low, keys, past, out_w, after):
    rows, query_cols = query.shape
    width = out_w.shape[1]
    block = QUERY_BLOCK
    chunks = 1 + WINDOW // block
    rows_of = functools.partial(by_rows, block)
    key_specs, key_operands = key_blocks(keys, past, block, chunks)
    return pl.pallas_call(
        functools.partial(attend_kernel, chunks),
        grid=(rows // block,),
        in_specs=[
            rows_of(query_cols),
            rows_of(low.shape[1]),
            whole(out_w.shape),
        ]
        + key_specs
        + unread(after),
        out_specs=[rows_of(2 * VDIM), rows_of(128), rows_of(width)],
        out_shape=[
            jax.ShapeDtypeStruct((rows, 2 * VDIM), bf16),
            jax.ShapeDtypeStruct((rows, 128), f32),
            jax.ShapeDtypeStruct((rows, width), bf16),
        ],
        compiler_params=whole_vmem,
        cost_estimate=small_cost,
        name="attend",
    )(query, low, out_w, *key_operands, *after)


def query_kernel(normed, cosine, sine, query_w, out):
    proj = dot_plain(normed[...], query_w[...])
    out[:, : 2 * NOPE] = proj[:, : 2 * NOPE].astype(bf16)
    out[:, 2 * NOPE :] = turn(proj[:, 2 * NOPE :], cosine[...], sine[...]).astype(bf16)


def project_query(normed, cosine, sine, query_w):
    rows, width = normed.shape
    block = QUERY_BLOCK
    cols = query_w.shape[1]
    return pl.pallas_call(
        query_kernel,
        grid=(rows // block,),
        in_specs=[
            by_rows(block, width),
            by_rows(block, 2 * ROPE),
            by_rows(block, 2 * ROPE),
            whole(query_w.shape),
        ],
        out_specs=by_rows(block, cols),
        out_shape=jax.ShapeDtypeStruct((rows, cols), bf16),
        compiler_params=whole_vmem,
        cost_estimate=small_cost,
        name="project_query",
    )(normed, cosine, sine, query_w)


def attend_back_kernel(
    chunks, grad, query_in, logs, cosine, sine, low, query_w, out_w, *refs
):
    keys = window_keys(refs, chunks)
    query_grad_out, part_out, kv_past, rope_past, kv_own, rope_own, kv_sum, rope_sum = refs[-8:]
    block = grad.shape[0]

    @pl.when(pl.program_id(0) == 0)
    def clear():
        kv_sum[...] = jnp.zeros_like(kv_sum)
        rope_sum[...] = jnp.zeros_like(rope_sum)

    def add(total, past, cols, piece):
        for chunk in range(chunks):
            part = piece[chunk * block : (chunk + 1) * block]
            if chunk < chunks - 1:
                part = part + total[chunk * block : (chunk + 1) * block, cols]
            if chunk == 0:
                past[:, cols] = part.astype(past.dtype)
            else:
                total[(chunk - 1) * block : chunk * block, cols] = part

    mixed_grad = dot_right_t(grad[...], out_w[...]).astype(bf16)
    mask = allowed_keys(low[...], block, WINDOW + block)
    query = query_in[...]
    plain, turned, rope_piece = [], 0.0, 0.0
    for head in range(2):
        lanes = head_lanes(block, head)
        query_head, key_head, value_head = head_parts(query, lanes, keys, head)
        base = head * (NOPE + VDIM)
        grad_head = mixed_grad[:, head * VDIM : (head + 1) * VDIM]
        scores = jnp.where(mask, dot_right_t(query_head, key_head) * score_scale, masked_value)
        probs = jnp.exp(scores - logs[:, head : head + 1])
        prob_grad = dot_right_t(grad_head, value_head)
        shift = jnp.sum(probs * prob_grad, axis=1, keepdims=True)
        score_grad = (probs * (prob_grad - shift)).astype(bf16)
        key_piece = dot_left_t(score_grad, query_head) * score_scale
        add(kv_sum, kv_past, slice(base, base + NOPE), key_piece[:, :NOPE])
        value_piece = dot_left_t(probs.astype(bf16), grad_head)
        add(kv_sum, kv_past, slice(base + NOPE, base + NOPE + VDIM), value_piece)
        rope_piece = rope_piece + key_piece[:, NOPE:]
        query_piece = dot_plain(score_grad, key_head) * score_scale
        plain.append(query_piece[:, :NOPE])
        turned = turned + jnp.where(lanes, query_piece[:, NOPE:], 0.0)
    add(rope_sum, rope_past, slice(0, 2 * ROPE), rope_piece)
    turned = turn_back(turned, cosine[...], sine[...])
    query_grad = jnp.concatenate(plain + [turned], axis=1).astype(bf16)
    query_grad_out[...] = query_grad
    part_out[...] = dot_right_t(query_grad, query_w[...]).astype(bf16)

    @pl.when(pl.program_id(0) == pl.num_programs(0) - 1)
    def finish():
        kv_own[...] = kv_sum[...].astype(bf16)
        rope_own[...] = rope_sum[...].astype(bf16)


def attend_back(grad, query, logs, cosine, sine, low, query_w, keys, past, out_w, after):
    rows, width = grad.shape
    block = QUERY_BLOCK
    chunks = 1 + WINDOW // block
    query_cols = query_w.shape[1]
    rows_of = functools.partial(by_rows, block)
    rope_cols = 2 * ROPE
    kv_cols = keys.shape[1] - rope_cols
    key_specs, key_operands = key_blocks(keys, past, block, chunks)
    return pl.pallas_call(
        functools.partial(attend_back_kernel, chunks),
        grid=(rows // block,),
        in_specs=[
            rows_of(width),
            rows_of(query_cols),
            rows_of(128),
            rows_of(2 * ROPE),
            rows_of(2 * ROPE),
            rows_of(low.shape[1]),
            whole(query_w.shape),
            whole(out_w.shape),
        ]
        + key_specs
        + unread(after),
        out_specs=[
            rows_of(query_cols),
            rows_of(width),
            rows_of(kv_cols),
            rows_of(rope_cols),
            whole((WINDOW, kv_cols)),
            whole((WINDOW, rope_cols)),
        ],
        out_shape=[
            jax.ShapeDtypeStruct((rows, query_cols), bf16),
            jax.ShapeDtypeStruct((rows, width), bf16),
            jax.ShapeDtypeStruct((rows, kv_cols), bf16),
            jax.ShapeDtypeStruct((rows, rope_cols), bf16),
            jax.ShapeDtypeStruct((WINDOW, kv_cols), bf16),
            jax.ShapeDtypeStruct((WINDOW, rope_cols), bf16),
        ],
        scratch_shapes=[pltpu.VMEM((WINDOW, kv_cols), f32), pltpu.VMEM((WINDOW, rope_cols), f32)],
        compiler_params=whole_vmem,
        cost_estimate=small_cost,
        name="attend_back",
    )(
        grad,
        query,
        logs,
        cosine,
        sine,
        low,
        query_w,
        out_w,
        *key_operands,
        *after,
    )


def norm_kernel(tokens, attention, gain, *refs):
    hidden_out, unit_out, factor_out, branch_out = refs[-4:]
    hidden = tokens[...].astype(f32) + attention[...].astype(f32)
    unit, factor = normalize(hidden)
    hidden_out[...] = hidden
    unit_out[...] = unit
    factor_out[...] = factor
    branch_out[...] = (unit * gain[...]).astype(bf16)


def norm(tokens, attention, gain, after):
    rows, width = tokens.shape
    full = whole((rows, width))
    return pl.pallas_call(
        norm_kernel,
        grid=(1,),
        in_specs=[full, full, whole((1, width))] + unread(after),
        out_specs=[full, full, whole((rows, 1)), full],
        out_shape=[
            jax.ShapeDtypeStruct((rows, width), f32),
            jax.ShapeDtypeStruct((rows, width), f32),
            jax.ShapeDtypeStruct((rows, 1), f32),
            jax.ShapeDtypeStruct((rows, width), bf16),
        ],
        cost_estimate=small_cost,
        compiler_params=whole_vmem,
        name="norm",
    )(tokens, attention, gain[None], *after)


def norm_back_kernel(branch_grad, grad_out, unit, factor, gain, *refs):
    hidden_grad_out, low_out, gain_grad_out = refs[-3:]
    grad = branch_grad[...].astype(f32)
    hidden_grad = grad_out[...] + norm_back(grad, unit[...], factor[...], gain[...])
    hidden_grad_out[...] = hidden_grad
    low_out[...] = hidden_grad.astype(bf16)
    gain_grad_out[...] = jnp.sum(grad * unit[...], axis=0, keepdims=True)


def norm_back_rows(branch_grad, grad_out, unit, factor, gain, after):
    rows, width = unit.shape
    full, line = whole((rows, width)), whole((1, width))
    return pl.pallas_call(
        norm_back_kernel,
        grid=(1,),
        in_specs=[full, full, full, whole((rows, 1)), line] + unread(after),
        out_specs=[full, full, line],
        out_shape=[
            jax.ShapeDtypeStruct((rows, width), f32),
            jax.ShapeDtypeStruct((rows, width), bf16),
            jax.ShapeDtypeStruct((1, width), f32),
        ],
        cost_estimate=small_cost,
        compiler_params=whole_vmem,
        name="norm_back",
    )(branch_grad, grad_out, unit, factor, gain[None], *after)


def column_tiles(hidden):
    return [(first, min(first + 512, hidden)) for first in range(0, hidden, 512)]


class Copies:
    def __init__(self, semaphores):
        self.semaphores = semaphores
        self.groups = {}
        self.used = 0

    def start(self, group, source, target):
        copy = pltpu.make_async_copy(source, target, self.semaphores.at[self.used])
        self.used += 1
        copy.start()
        self.groups.setdefault(group, []).append(copy)

    def wait(self, group):
        for copy in self.groups.pop(group):
            copy.wait()


def merged(ref, cols):
    value = ref[:, :, cols]
    return value.reshape(-1, value.shape[-1])


def expert_kernel(count, extra, row, places, slot_in, *refs):
    weights = refs[:count]
    outs = refs[count + extra : count + extra + 4]
    act_s, slope_s, inner_s, result, gate_w, up_w, down_w, semaphores = refs[count + extra + 4 :]
    depth, hidden = gate_w.shape[1:]
    rows = pl.ds(row, slot_in.shape[0])
    copies = Copies(semaphores)
    for first, last in column_tiles(hidden):
        cols = slice(first, last)
        for index, weight in enumerate(weights):
            place = places[index]
            copies.start(first, weight.at[0, :, cols], gate_w.at[place, :, cols])
            copies.start(first, weight.at[1, :, cols], up_w.at[place, :, cols])
    for index, weight in enumerate(weights):
        copies.start("down", weight.at[2], down_w.at[places[index]])
    for first, last in column_tiles(hidden):
        cols = slice(first, last)
        copies.wait(first)
        gate = dot_plain(slot_in[...], merged(gate_w, cols))
        up = dot_plain(slot_in[...], merged(up_w, cols))
        act, slope = silu_parts(gate)
        act_s[:, cols] = act.astype(bf16)
        slope_s[:, cols] = (up * slope).astype(bf16)
        inner_s[:, cols] = (act * up).astype(bf16)
        for source, target in zip((act_s, slope_s, inner_s), outs):
            copies.start("out", source.at[:, cols], target.at[rows, cols])
    copies.wait("down")
    for index in range(count):
        cols = slice(index * depth, (index + 1) * depth)
        result[:, cols] = dot_right_t(inner_s[...], down_w[index]).astype(bf16)
        copies.start("out", result.at[:, cols], outs[3].at[:, cols])
    copies.wait("out")


def expert_back_kernel(count, extra, row, places, out_grad, act, slope, *refs):
    weights = refs[:count]
    outs = refs[count + extra : count + extra + 3]
    gate_s, up_s, result, gate_w, up_w, down_w, semaphores = refs[count + extra + 3 :]
    depth, hidden = gate_w.shape[1:]
    copies = Copies(semaphores)
    for first, last in column_tiles(hidden):
        cols = slice(first, last)
        for index, weight in enumerate(weights):
            copies.start(first, weight.at[2, :, cols], down_w.at[places[index], :, cols])
    for index, weight in enumerate(weights):
        copies.start("back", weight.at[0], gate_w.at[places[index]])
        copies.start("back", weight.at[1], up_w.at[places[index]])
    for first, last in column_tiles(hidden):
        cols = slice(first, last)
        copies.wait(first)
        inner = dot_plain(out_grad[...], merged(down_w, cols))
        gate_s[:, cols] = (inner * slope[:, cols].astype(f32)).astype(bf16)
        up_s[:, cols] = (inner * act[:, cols].astype(f32)).astype(bf16)
        for source, target in zip((gate_s, up_s), outs):
            copies.start("out", source.at[:, cols], target.at[:, cols])
    copies.wait("back")
    for index in range(count):
        cols = slice(index * depth, (index + 1) * depth)
        result[:, cols] = (
            dot_right_t(gate_s[...], gate_w[index]) + dot_right_t(up_s[...], up_w[index])
        ).astype(bf16)
        copies.start("out", result.at[:, cols], outs[2].at[:, cols])
    copies.wait("out")


def expert_call(kernel, name, places, slots, fixed, weights, outputs, after, row=0, total=0, held=()):
    count = len(weights)
    rows, width = slots.shape
    _, depth, hidden = weights[0].shape
    inputs = [slots] + fixed
    tiles = len(column_tiles(hidden))
    weight_s = pltpu.VMEM((count, depth, hidden), bf16)
    scratch = [(rows, hidden)] * outputs + [(rows, width)]
    shapes = [(total or rows, hidden)] * outputs + [(rows, width)]
    first_held = 1 + len(inputs) + count + len(after)
    return pl.pallas_call(
        functools.partial(kernel, count, len(after) + len(held), row),
        grid_spec=pltpu.PrefetchScalarGridSpec(
            num_scalar_prefetch=1,
            grid=(1,),
            in_specs=[pl.BlockSpec(array.shape, lambda i, places: (0, 0)) for array in inputs]
            + unread(weights)
            + unread(after)
            + unread(held),
            out_specs=unread(shapes),
            scratch_shapes=[pltpu.VMEM(shape, bf16) for shape in scratch]
            + [weight_s] * 3
            + [pltpu.SemaphoreType.DMA((count * (2 * tiles + 3) + 3 * tiles,))],
        ),
        out_shape=[jax.ShapeDtypeStruct(shape, bf16) for shape in shapes],
        input_output_aliases={first_held + index: index for index in range(len(held))},
        compiler_params=whole_vmem,
        cost_estimate=small_cost,
        name=name,
    )(places, *inputs, *weights, *after, *held)


def weight_grad_kernel(count, plan, places, *refs):
    half = count // 2
    outs = refs[-1 - half * len(plan) :]
    step = pl.program_id(0)
    for number, segments in enumerate(plan):
        first = 0
        for terms in segments:
            grad = 0.0
            for left, right, row in terms:
                rows = slice(row, row + refs[left].shape[0])
                grad = grad + dot_left_t(refs[left][...], refs[right][rows])
            last = first + grad.shape[1]
            for index in range(count):

                @pl.when(step == index)
                def store(index=index, number=number, cols=slice(first, last), grad=grad):
                    if index < half:
                        outs[0][index, number, :, cols] = grad.astype(bf16)
                    else:
                        out = outs[1 + (index - half) * len(plan) + number]
                        out[:, cols] = grad.astype(bf16)

            first = last


def weight_grads(name, places, outputs, after=()):
    count = places.shape[0]
    lefts, rights = [], []

    def number_of(array, held):
        for number, other in enumerate(held):
            if array is other:
                return number
        held.append(array)
        return len(held) - 1

    plan, flops = [], 0
    for segments in outputs:
        planned, columns = [], 0
        for terms in segments:
            numbers = []
            for blocks, right in terms:
                row = 0
                for left in blocks if isinstance(blocks, list) else [blocks]:
                    numbers.append((number_of(left, lefts), number_of(right, rights), row))
                    row += left.shape[0]
                flops += 2 * row * left.shape[1] * right.shape[1]
            planned.append(numbers)
            columns += terms[0][1].shape[1]
        plan.append(planned)
    plan = [
        [[(left, len(lefts) + right, row) for left, right, row in numbers] for numbers in planned]
        for planned in plan
    ]
    piece = (lefts[0].shape[1] // count, columns)
    shapes = [(count // 2, len(outputs)) + piece] + [piece] * (count // 2 * len(outputs))
    kept, *given = pl.pallas_call(
        functools.partial(weight_grad_kernel, count, plan),
        grid_spec=pltpu.PrefetchScalarGridSpec(
            num_scalar_prefetch=1,
            grid=(count,),
            in_specs=[
                pl.BlockSpec((left.shape[0], left.shape[1] // count), lambda i, places: (0, places[i]))
                for left in lefts
            ]
            + [pl.BlockSpec(right.shape, lambda i, places: (0, 0)) for right in rights]
            + unread(after),
            out_specs=[pl.BlockSpec(shapes[0], lambda i, places: (0, 0, 0, 0))]
            + [pl.BlockSpec(shape, lambda i, places: (0, 0)) for shape in shapes[1:]],
        ),
        out_shape=[jax.ShapeDtypeStruct(shape, bf16) for shape in shapes],
        compiler_params=whole_vmem,
        cost_estimate=small_cost,
        name=name,
    )(places, *lefts, *rights, *after)
    return kept, given


def lead(array, *indices):
    shape = (1,) * len(indices) + array.shape[-2:]
    return pl.BlockSpec(shape, lambda i, *prefetched: indices + (0, 0))


def flat(ref):
    for _ in ref.shape[2:]:
        ref = ref.at[0]
    return ref[...].astype(f32)


def add_pair_kernel(kept, arrived, *refs):
    refs[-1][...] = (flat(kept) + flat(arrived)).astype(bf16)


def add_pair(kept, arrived, item, after):
    return pl.pallas_call(
        add_pair_kernel,
        grid=(1,),
        in_specs=[lead(kept, 1, item), lead(arrived)] + unread(after),
        out_specs=whole(arrived.shape),
        out_shape=jax.ShapeDtypeStruct(arrived.shape, bf16),
        cost_estimate=small_cost,
        compiler_params=whole_vmem,
        name="add_pair",
    )(kept, arrived, *after)


def finish_kernel(cuts, own, arrived, other, *refs):
    total = flat(own) + flat(arrived) + flat(other)
    outs = refs[-len(cuts) :]
    for (first, last, turned), out in zip(cuts, outs):
        part = total[:, first:last]
        out[...] = part.T[: out.shape[0]] if turned else part


def finish(name, parts, cuts, sizes, after):
    own, arrived, other = parts
    arrived, other = arrived[0], other[0]
    rows = own.shape[-2]
    shapes = [
        (size, rows) if turned else (rows, last - first)
        for (first, last, turned), size in zip(cuts, sizes)
    ]
    return pl.pallas_call(
        functools.partial(finish_kernel, cuts),
        grid=(1,),
        in_specs=[lead(own, 0, 0), lead(arrived), lead(other)] + unread(after),
        out_specs=[whole(shape) for shape in shapes],
        out_shape=[jax.ShapeDtypeStruct(shape, f32) for shape in shapes],
        compiler_params=whole_vmem,
        cost_estimate=small_cost,
        name=name,
    )(own, arrived, other, *after)


def prepare_kernel(bits, gate, up, down, *outs):
    for step in range(2):

        @pl.when(pl.program_id(0) == step)
        def copy(step=step):
            outs[step][0] = gate[0]
            outs[step][1] = up[0]
            outs[step][2] = down[0].T


def prepare(bit, gate, up, down):
    _, depth, hidden = gate.shape
    shape = (3, depth, hidden)

    def chosen(array):
        return pl.BlockSpec(
            (1,) + array.shape[1:], lambda i, bits: (jnp.where(i == 0, 1 - bits[0], bits[0]), 0, 0)
        )

    return pl.pallas_call(
        prepare_kernel,
        grid_spec=pltpu.PrefetchScalarGridSpec(
            num_scalar_prefetch=1,
            grid=(2,),
            in_specs=[chosen(gate), chosen(up), chosen(down)],
            out_specs=[pl.BlockSpec(shape, lambda i, bits: (0, 0, 0))] * 2,
        ),
        out_shape=[jax.ShapeDtypeStruct(shape, bf16)] * 2,
        compiler_params=whole_vmem,
        cost_estimate=small_cost,
        name="prepare",
    )(bit.reshape(1), gate, up, down)


def dispatch_kernel(branch, slots, *refs):
    mine_out, others_out = refs[-3], refs[-2:]
    capacity = slots.shape[1] // 2
    step = pl.program_id(0)
    for owner in range(slots.shape[0]):
        rows = slots.shape[2]
        places = slice(owner * capacity, (owner + 1) * capacity)
        rows_in = dot_plain(slots[owner], branch[owner * rows : (owner + 1) * rows]).astype(bf16)
        mine_out[places] = rows_in[:capacity]
        for half, other_out in enumerate(others_out):

            @pl.when(step == half)
            def store(other_out=other_out, places=places, rows_in=rows_in):
                other_out[places] = rows_in[capacity:]


def slot_specs(slots, step):
    members, both, rows = slots.shape
    return (
        pl.BlockSpec((step, both, rows), lambda i: (i, 0, 0)),
        functools.partial(by_rows, step * both // 2),
        functools.partial(by_rows, step * rows),
        (members // step,),
    )


def dispatch(branch, slots, after):
    members, both, _ = slots.shape
    width = branch.shape[1]
    slot_spec, slot_rows, token_rows, grid = slot_specs(slots, members // 2)
    half = (members * both // 4, width)
    return pl.pallas_call(
        dispatch_kernel,
        grid=grid,
        in_specs=[token_rows(width), slot_spec] + unread(after),
        out_specs=[slot_rows(width), whole(half), whole(half)],
        out_shape=[
            jax.ShapeDtypeStruct((members * both // 2, width), bf16),
            jax.ShapeDtypeStruct(half, bf16),
            jax.ShapeDtypeStruct(half, bf16),
        ],
        cost_estimate=small_cost,
        compiler_params=whole_vmem,
        name="dispatch",
    )(branch, slots, *after)


def shared_kernel(branch, weights, router, hot, *refs):
    act_out, slope_out, inner_out, gates_out = refs[-4:]
    named = hot[...] != 0
    logits = jnp.where(named, dot_right_t(branch[...], router[...]), masked_value)
    raised = jnp.exp(logits - jnp.max(logits, axis=1, keepdims=True))
    raised = jnp.where(named, raised, 0.0)
    gates_out[...] = raised / jnp.sum(raised, axis=1, keepdims=True)
    hidden = act_out.shape[1]
    both = dot_right_t(branch[...], weights[...])
    gate, up = both[:, :hidden], both[:, hidden:]
    act, slope = silu_parts(gate)
    act_out[...] = act.astype(bf16)
    slope_out[...] = (up * slope).astype(bf16)
    inner_out[...] = (act * up).astype(bf16)


def router_rows(weights):
    last = weights.shape[0] // 128 - 1
    return pl.BlockSpec((128, weights.shape[1]), lambda i, *prefetched: (last, 0))


def shared_forward(branch, weights, hot, after):
    rows, width = branch.shape
    hidden = (weights.shape[0] - 128) // 3
    block = 512
    shape = jax.ShapeDtypeStruct((rows, hidden), bf16)
    return pl.pallas_call(
        shared_kernel,
        grid=(rows // block,),
        in_specs=[
            by_rows(block, width),
            whole((2 * hidden, width)),
            router_rows(weights),
            by_rows(block, 128),
        ]
        + unread(after),
        out_specs=[by_rows(block, hidden)] * 3 + [by_rows(block, 128)],
        out_shape=[shape] * 3 + [jax.ShapeDtypeStruct((rows, 128), f32)],
        compiler_params=whole_vmem,
        cost_estimate=small_cost,
        name="shared_forward",
    )(branch, weights, weights, hot, *after)


def shared_back_kernel(grad, down, act, slope, *refs):
    out = refs[-1]
    hidden = act.shape[1]
    inner = dot_right_t(grad[...], down[...])
    out[:, :hidden] = (inner * slope[...].astype(f32)).astype(bf16)
    out[:, hidden:] = (inner * act[...].astype(f32)).astype(bf16)


def shared_back(grad, weights, act, slope, after):
    rows, width = grad.shape
    hidden = act.shape[1]
    block = 512
    return pl.pallas_call(
        shared_back_kernel,
        grid=(rows // block,),
        in_specs=[
            by_rows(block, width),
            pl.BlockSpec((hidden, width), lambda i: (2, 0)),
            by_rows(block, hidden),
            by_rows(block, hidden),
        ]
        + unread(after),
        out_specs=by_rows(block, 2 * hidden),
        out_shape=jax.ShapeDtypeStruct((rows, 2 * hidden), bf16),
        compiler_params=whole_vmem,
        cost_estimate=small_cost,
        name="shared_back",
    )(grad, weights, act, slope, *after)


def combine_kernel(named, inner, down, slots, out_mine, other_a, other_b, gates, out):
    lane = lax.broadcasted_iota(jnp.int32, gates.shape, 1)
    gate_mine, gate_other = [
        jnp.sum(jnp.where(lane == named[index], gates[...], 0.0), axis=1, keepdims=True)
        for index in range(2)
    ]
    out_other = jnp.where(pl.program_id(0) == 0, other_a[...], other_b[...])
    rows = slots.shape[2]
    capacity = slots.shape[1] // 2
    total = dot_plain(inner[...], down[...])
    for owner in range(slots.shape[0]):
        tokens = slice(owner * rows, (owner + 1) * rows)
        places = slice(owner * capacity, (owner + 1) * capacity)
        mine = dot_left_t(slots[owner, :capacity], out_mine[places])
        other = dot_left_t(slots[owner, capacity:], out_other[places])
        part = total[tokens] + gate_mine[tokens] * mine + gate_other[tokens] * other
        out[tokens] = part.astype(bf16)


def combine(inner, weights, slots, out_mine, out_other, gates, named):
    hidden, width = inner.shape[1], weights.shape[1]
    members, both, rows = slots.shape
    half = members // 2

    def part(rows, cols):
        return pl.BlockSpec((rows, cols), lambda i, named: (i, 0))

    def all_of(shape):
        return pl.BlockSpec(shape, lambda i, named: (0, 0))

    return pl.pallas_call(
        combine_kernel,
        grid_spec=pltpu.PrefetchScalarGridSpec(
            num_scalar_prefetch=1,
            grid=(2,),
            in_specs=[
                part(half * rows, hidden),
                pl.BlockSpec((hidden, width), lambda i, named: (2, 0)),
                pl.BlockSpec((half, both, rows), lambda i, named: (i, 0, 0)),
                part(half * both // 2, width),
                all_of(out_other[0].shape),
                all_of(out_other[1].shape),
                part(half * rows, 128),
            ],
            out_specs=part(half * rows, width),
        ),
        out_shape=jax.ShapeDtypeStruct((inner.shape[0], width), bf16),
        compiler_params=whole_vmem,
        cost_estimate=small_cost,
        name="combine",
    )(named, inner, weights, slots, out_mine, *out_other, gates)


def out_grad_kernel(grad, slots, out_mine, other_a, other_b, gate_mine, gate_other, *refs):
    out_other = jnp.where(pl.program_id(0) < pl.num_programs(0) // 2, other_a[...], other_b[...])
    grad_mine, grad_other, gate_grad_mine, gate_grad_other = refs[-4:]
    rows = slots.shape[2]
    capacity = slots.shape[1] // 2
    for owner in range(slots.shape[0]):
        places = slice(owner * capacity, (owner + 1) * capacity)
        hot = slots[owner].astype(f32)
        both = dot_plain(slots[owner], grad[owner * rows : (owner + 1) * rows])
        halves = (
            (hot[:capacity], both[:capacity], out_mine, gate_mine, grad_mine, gate_grad_mine),
            (hot[capacity:], both[capacity:], out_other, gate_other, grad_other, gate_grad_other),
        )
        for hot_half, slot_grad, out, gate, grad_out, gate_out in halves:
            slot_gate = jnp.sum(hot_half * gate[owner], axis=1, keepdims=True)
            grad_out[places] = (slot_gate * slot_grad).astype(bf16)
            gate_grad = jnp.sum(slot_grad * out[places].astype(f32), axis=1, keepdims=True)
            gate_out[owner] = jnp.sum(hot_half * gate_grad, axis=0, keepdims=True)


def out_grads(grad, slots, out_mine, out_other, gate_mine, gate_other, after):
    members, both, rows = slots.shape
    width = grad.shape[1]
    slot_spec, slot_rows, token_rows, grid = slot_specs(slots, 2)
    line = pl.BlockSpec((2, 1, rows), lambda i: (i, 0, 0))
    steps = members // 4
    first_half = pl.BlockSpec((both, width), lambda i: (jnp.minimum(i, steps - 1), 0))
    second_half = pl.BlockSpec((both, width), lambda i: (jnp.maximum(i - steps, 0), 0))
    grads = jax.ShapeDtypeStruct((members * both // 2, width), bf16)
    gates = jax.ShapeDtypeStruct((members, 1, rows), f32)
    return pl.pallas_call(
        out_grad_kernel,
        grid=grid,
        in_specs=[
            token_rows(width),
            slot_spec,
            slot_rows(width),
            first_half,
            second_half,
            line,
            line,
        ]
        + unread(after),
        out_specs=[slot_rows(width), slot_rows(width), line, line],
        out_shape=[grads, grads, gates, gates],
        compiler_params=whole_vmem,
        cost_estimate=small_cost,
        name="out_grads",
    )(
        grad,
        slots,
        out_mine,
        *out_other,
        gate_mine.reshape(members, 1, rows),
        gate_other.reshape(members, 1, rows),
        *after,
    )


def combine_back_kernel(grads, logit_grad, weights, router, slots, in_mine, in_other, *refs):
    out = refs[-1]
    rows = slots.shape[2]
    capacity = slots.shape[1] // 2
    total = dot_plain(grads[...], weights[...]) + dot_plain(logit_grad[...], router[...])
    for owner in range(slots.shape[0]):
        tokens = slice(owner * rows, (owner + 1) * rows)
        places = slice(owner * capacity, (owner + 1) * capacity)
        arrived = jnp.concatenate([in_mine[places], in_other[places]], axis=0)
        out[tokens] = (total[tokens] + dot_left_t(slots[owner], arrived)).astype(bf16)


def combine_back(grads, logit_grad, weights, slots, in_mine, in_other, after):
    width = weights.shape[1]
    slot_spec, slot_rows, token_rows, grid = slot_specs(slots, 4)
    return pl.pallas_call(
        combine_back_kernel,
        grid=grid,
        in_specs=[
            token_rows(grads.shape[1]),
            token_rows(logit_grad.shape[1]),
            whole((grads.shape[1], width)),
            router_rows(weights),
            slot_spec,
            slot_rows(width),
            slot_rows(width),
        ]
        + unread(after),
        out_specs=token_rows(width),
        out_shape=jax.ShapeDtypeStruct((grads.shape[0], width), bf16),
        compiler_params=whole_vmem,
        cost_estimate=small_cost,
        name="combine_back",
    )(grads, logit_grad, weights, weights, slots, in_mine, in_other, *after)


def latent_grad_kernel(kv_past, rope_past, kv_own, rope_own, expand, *refs):
    out = refs[-1]
    for index, (kv, rope) in enumerate(((kv_past, rope_past), (kv_own, rope_own))):
        out[index, :, :LATENT] = dot_right_t(kv[...], expand[...]).astype(bf16)
        out[index, :, LATENT:] = rope[...]


def latent_grads(kv_past, rope_past, kv_own, rope_own, expand, after):
    rows, cols = kv_past.shape
    rope_cols = rope_past.shape[1]
    block = QUERY_BLOCK
    kv_spec, rope_spec = by_rows(block, cols), by_rows(block, rope_cols)
    return pl.pallas_call(
        latent_grad_kernel,
        grid=(rows // block,),
        in_specs=[kv_spec, rope_spec, kv_spec, rope_spec, whole(expand.shape)] + unread(after),
        out_specs=pl.BlockSpec((2, block, LATENT + rope_cols), lambda i: (0, i, 0)),
        out_shape=jax.ShapeDtypeStruct((2, rows, LATENT + rope_cols), bf16),
        cost_estimate=small_cost,
        compiler_params=whole_vmem,
        name="latent_grads",
    )(kv_past, rope_past, kv_own, rope_own, expand, *after)


def first_block_kernel(blocks, *refs):
    refs[-1][...] = blocks[0]


def first_block(blocks, after):
    shape = blocks.shape[1:]
    return pl.pallas_call(
        first_block_kernel,
        grid=(1,),
        in_specs=[lead(blocks, 0)] + unread(after),
        out_specs=whole(shape),
        out_shape=jax.ShapeDtypeStruct(shape, blocks.dtype),
        cost_estimate=small_cost,
        compiler_params=whole_vmem,
        name="first_block",
    )(blocks, *after)


def join_kernel(count, *refs):
    rows = refs[0].shape[0]
    for index in range(count):
        refs[-1][index * rows : (index + 1) * rows] = refs[index][...]


def join_rows(blocks, after):
    rows, cols = blocks[0].shape
    shape = (len(blocks) * rows, cols)
    return pl.pallas_call(
        functools.partial(join_kernel, len(blocks)),
        grid=(1,),
        in_specs=[whole((rows, cols))] * len(blocks) + unread(after),
        out_specs=whole(shape),
        out_shape=jax.ShapeDtypeStruct(shape, blocks[0].dtype),
        cost_estimate=small_cost,
        compiler_params=whole_vmem,
        name="join_rows",
    )(*blocks, *after)


def latent_back_kernel(own, back, unit, factor, gain, cosine, sine, *refs):
    grad_out, gain_grad_out = refs[-2:]
    grad = own[...].astype(f32) + back[...].astype(f32)
    plain = grad[:, :LATENT]
    gain_grad_out[...] = jnp.sum(plain * unit[...], axis=0, keepdims=True)
    grad_out[:, :LATENT] = norm_back(plain, unit[...], factor[...], gain[...]).astype(bf16)
    grad_out[:, LATENT:] = turn_back(grad[:, LATENT:], cosine[...], sine[...]).astype(bf16)


def latent_back_rows(own, back, unit, factor, gain, cosine, sine, after):
    rows, cols = own.shape
    inputs = [own, back, unit, factor, gain[None], cosine, sine]
    return pl.pallas_call(
        latent_back_kernel,
        grid=(1,),
        in_specs=[whole(array.shape) for array in inputs] + unread(after),
        out_specs=[whole((rows, cols)), whole((1, LATENT))],
        out_shape=[
            jax.ShapeDtypeStruct((rows, cols), bf16),
            jax.ShapeDtypeStruct((1, LATENT), f32),
        ],
        cost_estimate=small_cost,
        compiler_params=whole_vmem,
        name="latent_back",
    )(*inputs, *after)


def gain_part_kernel(grad, normed, gain, *refs):
    out = refs[-1]
    step = pl.program_id(0)

    @pl.when(step == 0)
    def clear():
        out[...] = jnp.zeros_like(out)

    out[...] += jnp.sum(grad[...].astype(f32) * normed[...].astype(f32), axis=0, keepdims=True)

    @pl.when(step == pl.num_programs(0) - 1)
    def divide():
        out[...] = out[...] / gain[...]


def gain_part(grad, normed, gain):
    rows, width = grad.shape
    block = QUERY_BLOCK
    return pl.pallas_call(
        gain_part_kernel,
        grid=(rows // block,),
        in_specs=[by_rows(block, width), by_rows(block, width), whole((1, width))],
        out_specs=whole((1, width)),
        out_shape=jax.ShapeDtypeStruct((1, width), f32),
        compiler_params=whole_vmem,
        cost_estimate=small_cost,
        name="gain_part",
    )(grad, normed, gain[None])


def gain_rest_kernel(projected, compress, unit, part, out):
    total = dot_plain(projected[...], compress[...])
    out[...] = part[...] + jnp.sum(total * unit[...], axis=0, keepdims=True)


def gain_rest(projected, compress, unit, part):
    inputs = [projected, compress, unit, part]
    return pl.pallas_call(
        gain_rest_kernel,
        grid=(1,),
        in_specs=[whole(array.shape) for array in inputs],
        out_specs=whole(part.shape),
        out_shape=jax.ShapeDtypeStruct(part.shape, f32),
        compiler_params=whole_vmem,
        cost_estimate=small_cost,
        name="gain_rest",
    )(*inputs)


def tokens_back_kernel(grad, projected, compress, unit, factor, gain, hidden_grad, *refs):
    out = refs[-1]
    total = grad[...].astype(f32) + dot_plain(projected[...], compress[...])
    out[...] = hidden_grad[...] + norm_back(total, unit[...], factor[...], gain[...])


def tokens_back(grad, projected, compress, unit, factor, gain, hidden_grad, after):
    rows, width = grad.shape
    inputs = [grad, projected, compress, unit, factor, gain[None], hidden_grad]
    return pl.pallas_call(
        tokens_back_kernel,
        grid=(1,),
        in_specs=[whole(array.shape) for array in inputs] + unread(after),
        out_specs=whole((rows, width)),
        out_shape=jax.ShapeDtypeStruct((rows, width), f32),
        compiler_params=whole_vmem,
        cost_estimate=small_cost,
        name="tokens_back",
    )(*inputs, *after)


def slice_grad_kernel(index, left, right, *refs):
    out = refs[-1]
    half = ROPE // 2
    grad = dot_left_t(left[...], right[...])
    out[:LATENT] = grad[:LATENT]
    turned = grad[LATENT:]
    out[LATENT : LATENT + half] = turned[:half] + turned[half:ROPE]
    out[LATENT + half :] = turned[ROPE : ROPE + half] + turned[ROPE + half :]


def beside_kernel(blocks, out):
    cols = blocks.shape[2]
    for index in range(blocks.shape[0]):
        out[:, index * cols : (index + 1) * cols] = blocks[index].astype(f32)


def beside(blocks, rows):
    count, _, cols = blocks.shape
    step = rows // 4
    return pl.pallas_call(
        beside_kernel,
        grid=(4,),
        in_specs=[pl.BlockSpec((count, step, cols), lambda i: (0, i, 0))],
        out_specs=by_rows(step, count * cols),
        out_shape=jax.ShapeDtypeStruct((rows, count * cols), f32),
        cost_estimate=small_cost,
        compiler_params=whole_vmem,
        name="beside",
    )(blocks)


def slice_grad(left, right, index, cols, after):
    rows = left.shape[0]
    out_rows = LATENT + ROPE
    return pl.pallas_call(
        slice_grad_kernel,
        grid_spec=pltpu.PrefetchScalarGridSpec(
            num_scalar_prefetch=1,
            grid=(1,),
            in_specs=[
                pl.BlockSpec(left.shape, lambda i, index: (0, 0)),
                pl.BlockSpec((rows, cols), lambda i, index: (0, index[0])),
            ]
            + unread(after),
            out_specs=pl.BlockSpec((out_rows, cols), lambda i, index: (0, 0)),
        ),
        out_shape=jax.ShapeDtypeStruct((out_rows, cols), f32),
        cost_estimate=small_cost,
        compiler_params=whole_vmem,
        name="slice_grad",
    )(index.reshape(1), left, right, *after)


def place_kernel(turned, bits, own, arrived, other, *refs):
    out = refs[-1]

    @pl.when(pl.program_id(0) == 0)
    def first():
        total = flat(own) + flat(arrived)
        out[0] = total.T if turned else total

    @pl.when(pl.program_id(0) == 1)
    def second():
        total = flat(other)
        out[0] = total.T if turned else total


def place_experts(bit, parts, item, turned, after):
    own, arrived, other = parts
    arrived_item, other_item = arrived[item], other[item]
    shape = own.shape[:-3:-1] if turned else own.shape[-2:]
    return pl.pallas_call(
        functools.partial(place_kernel, turned),
        grid_spec=pltpu.PrefetchScalarGridSpec(
            num_scalar_prefetch=1,
            grid=(2,),
            in_specs=[lead(own, 0, item), lead(arrived_item), lead(other_item)]
            + unread(after),
            out_specs=pl.BlockSpec(
                (1,) + shape, lambda i, bits: (jnp.where(i == 0, bits[0], 1 - bits[0]), 0, 0)
            ),
        ),
        out_shape=jax.ShapeDtypeStruct((2,) + shape, f32),
        compiler_params=whole_vmem,
        cost_estimate=small_cost,
        name="place_experts",
    )(bit.reshape(1), own, arrived_item, other_item, *after)


def split_query_columns(weight):
    head = NOPE + ROPE
    half = ROPE // 2
    pieces = [weight[:, :NOPE], weight[:, head : head + NOPE]]
    for part in range(2):
        for index in range(2):
            first = index * head + NOPE + part * half
            pieces.append(weight[:, first : first + half])
    return jnp.concatenate(pieces, axis=1)


def join_query_columns(grad):
    half = ROPE // 2
    base = 2 * NOPE
    pieces = []
    for index in range(2):
        pieces.append(grad[:, index * NOPE : (index + 1) * NOPE])
        for part in range(2):
            first = base + part * ROPE + index * half
            pieces.append(grad[:, first : first + half])
    return jnp.concatenate(pieces, axis=1)


class Pairing:
    def __init__(self, groups, members):
        self.groups = groups
        self.members = members
        self.bits = groups.bit_length() - 1
        top = self.bits - 1
        self.partner = (1 << top, 1)
        self.others = (
            [1 << bit for bit in range(top)],
            [1 << (bit + 1) for bit in range(top)],
        )
        self.group = lax.axis_index("dp")
        self.odd = lax.axis_index("expert") % 2

    def chosen(self, masks):
        return jnp.where(self.odd == 1, masks[1], masks[0])

    def place(self, masks):
        return self.group ^ self.chosen(masks)

    def bit(self):
        return jnp.where(self.group & self.chosen(self.partner), 1, 0)

    def swap(self, value, masks):
        pairs = []
        for group in range(self.groups):
            for member in range(self.members):
                other = group ^ masks[member % 2]
                pairs.append((group * self.members + member, other * self.members + member))
        return lax.ppermute(value, ("dp", "expert"), pairs)

    def swap_partner(self, value):
        return self.swap(value, self.partner)

    def masks(self):
        masks = [(0, 0), self.partner]
        for step in zip(*self.others):
            masks = masks + [(even ^ step[0], odd ^ step[1]) for even, odd in masks]
        return masks

    def places(self):
        return jnp.stack([self.place(mask) for mask in self.masks()])

    def spread(self, held):
        for step in zip(*self.others):
            held = held + [self.swap(piece, step) for piece in held]
        return held

    def collect(self, kept, given):
        steps = list(reversed(list(zip(*self.others))))
        for number, step in enumerate(steps):
            arrived = [self.swap(piece, step) for piece in given]
            if number < len(steps) - 1:
                total = kept.astype(f32) + jnp.stack(arrived).reshape(kept.shape).astype(f32)
                total = total.astype(bf16)
                half = total.shape[0] // 2
                kept, given = total[:half], list(total[half:].reshape((-1,) + total.shape[2:]))
        return (kept, arrived)

    def partner_sum(self, kept, arrived, item, after=()):
        return add_pair(kept, arrived[kept.shape[1] + item], item, after)

    def gather_members(self, value, after):
        member = lax.axis_index("expert")
        rows = value.shape[0]
        chips = [value]
        for other in range(1, self.members // 2):
            pairs = [(i, i ^ (2 * other)) for i in range(self.members)]
            chips.append(lax.ppermute(value, "expert", pairs))
        both = lax.ppermute(
            join_rows(chips, after), "expert", [(i, i ^ 1) for i in range(self.members)]
        )
        held = []
        for number, block in enumerate(chips):
            held += [block, both[number * rows : (number + 1) * rows]]
        bit = 1
        while bit < self.members:
            flip = (member & bit) != 0
            held = [jnp.where(flip, held[i ^ bit], held[i]) for i in range(self.members)]
            bit *= 2
        return jnp.concatenate(held)

    def total(self, value):
        for bit in range(self.bits):
            arrived = self.swap(value.astype(bf16), (1 << bit, 1 << (self.bits - 1 - bit)))
            value = value + arrived.astype(f32)
        return value

    def total_members(self, value):
        def turned(mask):
            return [(i, i ^ mask) for i in range(self.members)]

        value = value + lax.ppermute(value, "expert", turned(1))
        masks = range(2, self.members, 2)
        return sum([lax.ppermute(value, "expert", turned(mask)) for mask in masks], value)

    def total_all(self, value):
        size = self.groups * self.members
        for bit in range(size.bit_length() - 1):
            pairs = [(i, i ^ (1 << bit)) for i in range(size)]
            value = value + lax.ppermute(value, ("dp", "expert"), pairs)
        return value


def body(
    tokens,
    target,
    valid,
    routes,
    lengths,
    first_gain_vector,
    second_gain_vector,
    latent_gain_vector,
    latent_compress_weight,
    query_weight,
    latent_expand_weight,
    output_weight,
    router_weight,
    shared_gate_weight,
    shared_up_weight,
    shared_down_weight,
    expert_gate_weight,
    expert_up_weight,
    expert_down_weight,
):
    rows, width = tokens.shape
    members = lax.axis_size("expert")
    groups = lax.axis_size("dp")
    member = lax.axis_index("expert")
    group = lax.axis_index("dp")
    group_size = rows * members
    local_experts = expert_gate_weight.shape[0]
    route_count = routes.shape[1]
    expert_count = router_weight.shape[1]
    hidden_width = expert_gate_weight.shape[2]
    capacity = rows * route_count * 4 // (3 * local_experts * members)
    pairing = Pairing(groups, members)
    bit = pairing.bit()

    def pick(array, index):
        return lax.dynamic_index_in_dim(array, index, 0, False)

    tokens_float = tokens.astype(f32)
    own_unit, own_factor = normalize(tokens_float)
    own_normed = (own_unit * first_gain_vector).astype(bf16)
    normed = lax.all_gather(own_normed, "expert", axis=0, tiled=True)
    half = ROPE // 2
    compress_t = latent_compress_weight.T
    compress_t = jnp.concatenate(
        [compress_t[: LATENT + half]]
        + [compress_t[LATENT : LATENT + half]]
        + [compress_t[LATENT + half :]] * 2
    )
    index = group * group_size + jnp.arange(group_size, dtype=jnp.int32)
    seq_id = jnp.floor_divide(index, SEQ)
    place = index - seq_id * SEQ
    cosine, sine = angles(place, half)
    cosine = jnp.concatenate([cosine] * 4, axis=1)
    sine = jnp.concatenate([-sine, -sine, sine, sine], axis=1)
    own_cos = lax.dynamic_slice_in_dim(cosine, member * rows, rows, 0)
    own_sin = lax.dynamic_slice_in_dim(sine, member * rows, rows, 0)
    projected = dot_right_t(own_normed, compress_t)
    latent_unit, latent_factor = normalize(projected[:, :LATENT])
    places = pairing.places()
    given, kept = prepare(bit, expert_gate_weight, expert_up_weight, expert_down_weight)
    expert_w = pairing.spread([kept, pairing.swap_partner(given)])

    shared_hidden_width = shared_gate_weight.shape[1]
    padded = -(-shared_hidden_width // 128) * 128
    shared_w = jnp.concatenate(
        [
            jnp.pad(weight, ((0, extent - weight.shape[0]), (0, 0)))
            for weight, extent in (
                (shared_gate_weight.T, padded),
                (shared_up_weight.T, padded),
                (shared_down_weight, padded),
                (router_weight.T, 128),
            )
        ]
    )

    counted = valid.astype(f32)
    count = pairing.total_all(jnp.full((8, 128), jnp.sum(counted)))[0, 0]

    bounds = lax.dynamic_slice_in_dim(
        jnp.cumsum(lengths, axis=1), group * group_size // SEQ, 1, 0
    )
    doc_start = jnp.max(jnp.where(bounds <= place[:, None], bounds, 0), axis=1)
    in_block = jnp.arange(group_size, dtype=jnp.int32) % QUERY_BLOCK
    low = jnp.maximum(doc_start - place + WINDOW + in_block, in_block + 1)
    low = jnp.broadcast_to(low[:, None], (group_size, 128))

    hot = jnp.any(routes[:, :, None] == jnp.arange(128, dtype=jnp.int32), axis=1).astype(bf16)
    routes_t = routes.T.reshape(route_count, members, rows)
    order = jnp.arange(rows, dtype=jnp.int32)
    earlier = (order[:, None] < order[None, :]).astype(bf16)
    mine = member * local_experts + bit
    other = member * local_experts + 1 - bit

    def slots_of(expert):
        hit = jnp.any(routes_t == expert, axis=0)
        rank = dot_plain(hit.astype(bf16), earlier).astype(jnp.int32)
        slot = jnp.arange(capacity, dtype=jnp.int32)[None, :, None]
        return (hit[:, None, :] & (rank[:, None, :] == slot)).astype(bf16)

    slots = jnp.concatenate([slots_of(mine), slots_of(other)], axis=1)

    query_w = split_query_columns(query_weight)
    keys, group_latent = own_keys(
        normed,
        cosine,
        sine,
        latent_gain_vector,
        compress_t,
        latent_expand_weight,
        [shared_w, query_w, hot, slots],
    )
    forward = [(i, i + 1) for i in range(groups - 1)]
    past = lax.ppermute(keys, "dp", forward)
    previous = lax.ppermute(group_latent, "dp", forward)
    query = project_query(normed, cosine, sine, query_w)
    mixed, logs, attention_part = attend(query, low, keys, past, output_weight, expert_w[1:2])
    attention = lax.psum_scatter(attention_part, "expert", scatter_dimension=0, tiled=True)
    hidden, hidden_unit, hidden_factor, own_branch = norm(
        tokens, attention, second_gain_vector, expert_w[2:3]
    )
    branch = lax.all_gather(own_branch, "expert", axis=0, tiled=True)

    in_mine, *in_others = dispatch(branch, slots, expert_w[3:])
    in_arrived = [pairing.swap_partner(half) for half in in_others]
    act_m, slope_m, inner_m, out_mine = expert_call(
        expert_kernel, "expert", places, in_mine, [], expert_w, 3, []
    )
    half_rows, slot_rows = in_arrived[0].shape[0], in_mine.shape[0]
    *held, out_first = expert_call(
        expert_kernel,
        "expert",
        places,
        in_arrived[0],
        [],
        expert_w,
        3,
        [out_mine],
        0,
        slot_rows,
    )
    *held, out_second = expert_call(
        expert_kernel, "expert", places, in_arrived[1], [], expert_w, 3, [], half_rows, slot_rows, held
    )
    act_a, slope_a, inner_a = held
    out_other = [pairing.swap_partner(half) for half in (out_first, out_second)]
    shared_act, shared_slope, shared_hidden, gates = shared_forward(
        branch, shared_w, hot, [out_second, out_other[0]]
    )
    experts = jnp.arange(128, dtype=jnp.int32)[None, :]
    gate_mine = jnp.sum(jnp.where(experts == mine, gates, 0.0), axis=1)
    gate_other = jnp.sum(jnp.where(experts == other, gates, 0.0), axis=1)
    branch_part = combine(
        shared_hidden, shared_w, slots, out_mine, out_other, gates, jnp.stack([mine, other])
    )
    branch_sum = lax.psum_scatter(branch_part, "expert", scatter_dimension=0, tiled=True)
    result = hidden + branch_sum.astype(f32)
    difference = result - target.astype(f32)
    squares = jnp.sum(counted[:, None] * difference * difference)
    squares = pairing.total_all(jnp.full((8, 128), squares))
    total_tokens = rows * members * groups
    grad_out = total_tokens / count * counted[:, None] * difference

    grad_low = lax.all_gather(grad_out.astype(bf16), "expert", axis=0, tiled=True)

    out_grad_mine, out_grad_other, gate_grad_mine, gate_grad_other = out_grads(
        grad_low, slots, out_mine, out_other, gate_mine, gate_other, [previous, squares]
    )
    out_grad_arrived = pairing.swap_partner(out_grad_other)
    gate_gm, up_gm, in_grad_mine = expert_call(
        expert_back_kernel,
        "expert_back",
        places,
        out_grad_mine,
        [act_m, slope_m],
        expert_w,
        2,
        [],
    )
    shared_grad = shared_back(grad_low, shared_w, shared_act, shared_slope, [in_grad_mine])
    gate_ga, up_ga, in_grad_arrived = expert_call(
        expert_back_kernel,
        "expert_back",
        places,
        out_grad_arrived,
        [act_a, slope_a],
        expert_w,
        2,
        [shared_grad],
    )
    in_grad_other = pairing.swap_partner(in_grad_arrived)

    down_kept, down_given = weight_grads(
        "down_grad",
        places,
        [[[(out_grad_mine, inner_m), (out_grad_arrived, inner_a)]]],
        [in_grad_arrived],
    )

    gate_grads = jnp.where(experts == mine, gate_grad_mine.reshape(-1, 1), 0.0) + jnp.where(
        experts == other, gate_grad_other.reshape(-1, 1), 0.0
    )
    logit_grad = gates * (gate_grads - jnp.sum(gates * gate_grads, axis=1, keepdims=True))
    logit_total = pairing.total_members(
        first_block(logit_grad[:, :expert_count].T[None], [down_kept])
    )
    logit_grad = logit_grad.astype(bf16)
    branch_slice = lax.dynamic_slice_in_dim(branch, member * (width // members), width // members, 1)
    router_slice = dot_plain(logit_total.astype(bf16), branch_slice)
    branch_grad_part = combine_back(
        shared_grad,
        logit_grad,
        shared_w,
        slots,
        in_grad_mine,
        in_grad_other,
        [logit_total],
    )
    branch_grad = lax.psum_scatter(
        branch_grad_part, "expert", scatter_dimension=0, tiled=True
    )

    down_terms = pairing.collect(down_kept, down_given)
    gate_up_kept, gate_up_given = weight_grads(
        "gate_up_grad",
        places,
        [
            [[(in_mine, gate_gm), (in_arrived, gate_ga)]],
            [[(in_mine, up_gm), (in_arrived, up_ga)]],
        ],
        [branch_grad_part],
    )
    gate_up_terms = pairing.collect(gate_up_kept, gate_up_given)
    shared_kept, shared_given = weight_grads(
        "shared_grads",
        places,
        [[[(branch, shared_grad)], [(grad_low, shared_hidden)]]],
        [gate_up_kept],
    )
    shared_terms = pairing.collect(shared_kept, shared_given)
    down_sum = pairing.partner_sum(*down_terms, 0)
    gate_sum, up_sum = [pairing.partner_sum(*gate_up_terms, item) for item in range(2)]
    down_other, gate_other_half, up_other_half = [
        pairing.swap_partner(total) for total in (down_sum, gate_sum, up_sum)
    ]
    down_parts = (*down_terms, [down_other])
    gate_up_parts = (*gate_up_terms, [gate_other_half, up_other_half])

    grad_hidden_own, grad_hidden_low, grad_norm2 = norm_back_rows(
        branch_grad,
        grad_out,
        hidden_unit,
        hidden_factor,
        second_gain_vector,
        down_terms[1] + gate_up_terms[1][2:3] + [shared_kept],
    )
    grad_attention = lax.all_gather(grad_hidden_low, "expert", axis=0, tiled=True)
    query_grad, normed_grad_part, kv_past, rope_past, kv_own, rope_own = attend_back(
        grad_attention,
        query,
        logs,
        cosine,
        sine,
        low,
        query_w,
        keys,
        past,
        output_weight,
        [down_sum, gate_sum],
    )

    latent_grad = lax.psum_scatter(
        latent_grads(
            kv_past, rope_past, kv_own, rope_own, latent_expand_weight, shared_terms[1] + [down_other, gate_other_half, up_sum]
        ),
        "expert",
        scatter_dimension=1,
        tiled=True,
    )
    normed_grad = lax.psum_scatter(
        normed_grad_part, "expert", scatter_dimension=0, tiled=True
    )

    attention_kept, attention_given = weight_grads(
        "attention_grads",
        places,
        [[[(normed, query_grad)], [(grad_attention, mixed)]]],
        [kv_own],
    )
    expand_grad = (
        dot_left_t(previous, kv_past) + dot_left_t(group_latent, kv_own)
    ).astype(bf16)
    expand_grad = expand_grad.reshape(groups, -1, expand_grad.shape[1])
    expand_pieces = jnp.stack([pick(expand_grad, places[i]) for i in range(groups)])[:, None]
    expand_terms = pairing.collect(
        expand_pieces[: groups // 2], list(expand_pieces[groups // 2 :].squeeze(1))
    )
    norm1_part = gain_part(normed_grad_part, normed, first_gain_vector)
    expert_down_gradient = place_experts(bit, down_parts, 0, True, [attention_kept])
    expand_sum = pairing.partner_sum(*expand_terms, 0)
    expand_parts = (*expand_terms, [pairing.swap_partner(expand_sum)])
    shared_sum = pairing.partner_sum(*shared_terms, 0)
    shared_parts = (*shared_terms, [pairing.swap_partner(shared_sum)])
    back = lax.ppermute(
        first_block(
            latent_grad,
            [attention_kept, expert_down_gradient, up_other_half, gate_up_terms[1][0], shared_sum]
            + [expand_pieces, norm1_part],
        ),
        "dp",
        [(i + 1, i) for i in range(groups - 1)],
    )

    grad_projected, grad_latent_gain = latent_back_rows(
        latent_grad[1],
        back,
        latent_unit,
        latent_factor,
        latent_gain_vector,
        own_cos,
        own_sin,
        [],
    )
    expert_gate_gradient = place_experts(bit, gate_up_parts, 0, False, [grad_projected])
    expert_up_gradient = place_experts(bit, gate_up_parts, 1, False, [grad_projected])
    slice_cols = width // members
    grad_norm1 = gain_rest(grad_projected, compress_t, own_unit, norm1_part)
    group_grad = pairing.gather_members(
        grad_projected, [expert_gate_gradient, expert_up_gradient, expand_sum, grad_norm1]
    )
    attention_terms = pairing.collect(
        attention_kept, attention_given
    )
    compress_slice = slice_grad(group_grad, normed, member, slice_cols, [])
    grad_tokens = tokens_back(
        normed_grad,
        grad_projected,
        compress_t,
        own_unit,
        own_factor,
        first_gain_vector,
        grad_hidden_own,
        [],
    )
    gains = jnp.concatenate(
        [grad_latent_gain[0], grad_norm2[0], grad_norm1[0]]
    ).reshape(-1, slice_cols)
    gain_rows = -(-gains.shape[0] // 16) * 16
    gains = jnp.pad(gains, ((0, gain_rows - gains.shape[0]), (0, 0)))
    compress_rows = compress_slice.shape[0]
    compress_slice = pairing.total(
        jnp.concatenate([compress_slice, router_slice, gains])
    ).astype(bf16)
    compress_all = lax.all_gather(compress_slice, "expert", axis=0)
    kva_t = beside(compress_all, compress_rows)
    grad_kva = kva_t.T
    router_rows = compress_rows + expert_count
    grad_router = (
        compress_all[:, compress_rows:router_rows].transpose(0, 2, 1).reshape(width, -1).astype(f32)
    )
    gains = jnp.sum(compress_all[:, router_rows:].astype(f32), axis=0).reshape(-1)
    grad_latent_gain, gains = gains[:LATENT], gains[LATENT:]
    grad_norm2, grad_norm1 = gains[:width], gains[width : 2 * width]

    attention_sum = pairing.partner_sum(*attention_terms, 0, [group_grad])
    attention_parts = (*attention_terms, [pairing.swap_partner(attention_sum)])
    query_cols, mixed_cols = query_w.shape[1], mixed.shape[1]
    shared_gate_gradient, shared_up_gradient, shared_down_gradient = finish(
        "shared_finish",
        shared_parts,
        [(i * padded, (i + 1) * padded, True) for i in range(3)],
        [shared_hidden_width] * 3,
        [compress_slice, grad_tokens],
    )
    query_weight_gradient, output_weight_gradient = finish(
        "attention_finish",
        attention_parts,
        [(0, query_cols, False), (query_cols, query_cols + mixed_cols, True)],
        [0, mixed_cols],
        [kva_t],
    )
    shared_gate_gradient, shared_up_gradient = shared_gate_gradient.T, shared_up_gradient.T
    query_weight_gradient = join_query_columns(query_weight_gradient)
    (latent_expand_gradient,) = finish(
        "expand_finish",
        expand_parts,
        [(0, expand_grad.shape[2], False)],
        [0],
        [compress_slice],
    )
    return (
        result.astype(bf16),
        squares[0, 0] / (count * width),
        grad_tokens,
        grad_norm1,
        grad_norm2,
        grad_latent_gain,
        grad_kva,
        query_weight_gradient,
        latent_expand_gradient,
        output_weight_gradient,
        grad_router,
        shared_gate_gradient,
        shared_up_gradient,
        shared_down_gradient,
        expert_gate_gradient,
        expert_up_gradient,
        expert_down_gradient,
    )


def solution(mesh):
    placed = (
        P(("dp", "expert"), None),
        P(("dp", "expert"), None),
        P(("dp", "expert")),
        P("dp", None),
        P(),
        P(),
        P(),
        P(),
        P(),
        P(None, "expert"),
        P(None, "expert"),
        P("expert", None),
        P(),
        P(None, "expert"),
        P(None, "expert"),
        P("expert", None),
        P("expert", "dp", None),
        P("expert", "dp", None),
        P("expert", None, "dp"),
    )
    return jax.shard_map(
        body,
        mesh=mesh,
        in_specs=placed,
        out_specs=(
            P(("dp", "expert"), None),
            P(),
            P(("dp", "expert"), None),
            P(),
            P(),
            P(),
            P(),
            P("dp", "expert"),
            P("dp", "expert"),
            P("expert", "dp"),
            P(),
            P("dp", "expert"),
            P("dp", "expert"),
            P("expert", "dp"),
            P("expert", "dp", None),
            P("expert", "dp", None),
            P("expert", None, "dp"),
        ),
        check_vma=False,
    )
```
